32 devices in a mesh: cfg: 2 (over core), req: 8 (over z, x), seq: 2 (over y).
Axes of the slice: x: 2, y: 2, z: 4, core: 2. Of those that a mesh axis runs over, the one named last changes fastest.
Arguments:
- hidden: bfloat16 [2, 8, 576, 1536], P('cfg', 'req', 'seq'), may hold values from -6 to 6
- latent: float32 [8, 576, 64], P('req', 'seq', 'cfg'), may hold values from -6 to 6
- modulation: float32 [8, 5, 1536], P('req'), may hold values from -3 to 3
- w_qkv: bfloat16 [1536, 4608], P('req'), may hold values from -1 to 1
- w_out: bfloat16 [1536, 1536], P('req'), may hold values from -0.15625 to 0.15625
- q_gain: float32 [1536], replicated, may hold values from 0 to 2
- k_gain: float32 [1536], replicated, may hold values from 0 to 2
- w_head: bfloat16 [1536, 64], replicated, may hold values from -0.15625 to 0.15625
- lengths: int32 [8], P('req'), may hold values from 288 to 576, as said below
- guidance: float32 [8], P('req'), may hold values from 3 to 7
- step_size: float32 [8], P('req'), may hold values from 0.03 to 0.3
Outputs:
- new_latent: float32 [8, 576, 64], P('req', 'seq', 'cfg')
The draws below stay inside these ranges and needn't reach their ends.
Inputs may be any that keep to these rules, and one draw needn't show every extreme that they name: `lengths`: some request has exactly 576 video tokens in every draw.
All inputs are finite; a program needn't handle non-finite values.
Results may differ from the reference program's by a relative error of at most 0.01.
Values may be sent and summed in bfloat16 or wider, within the bound.
No kernel may reach another device: no remote copies, remote signals or barrier semaphores. Data moves between devices by JAX's collectives and lax.ppermute only.
A program may use at most 128 MiB of HBM per device.

```python
import math
import jax
import jax.numpy as jnp
from jax import lax

D = 1536
H = 12
DH = 128
OUT = 64
TOK_DEV = 288
REQUESTS = 8
TOKENS = 576


def draw_lengths(key, part):
    first, second = jax.random.split(jax.random.fold_in(key, 11))
    base = jax.random.randint(first, (REQUESTS,), TOK_DEV, TOKENS + 1)
    picked = jax.random.randint(second, (), 0, REQUESTS)
    return jnp.where(jnp.arange(REQUESTS) == picked, TOKENS, base).astype(jnp.int32)


def draw_hidden(key, part):
    noise_key = jax.random.fold_in(jax.random.fold_in(key, 21), 0)
    noise = jnp.clip(jax.random.normal(noise_key, (2, REQUESTS, TOKENS, D), jnp.float32), -6.0, 6.0)
    return noise.astype(jnp.bfloat16)


def draw_w_qkv(key, part):
    own_key = jax.random.fold_in(key, 31)
    return (jnp.clip(jax.random.normal(own_key, (D, 3 * D), jnp.float32), -6.0, 6.0) * D ** (-0.5)).astype(jnp.bfloat16)


def draw_q_gain(key, part):
    own_key = jax.random.fold_in(key, 41)
    return 1.0 + 0.15 * jnp.clip(jax.random.normal(own_key, (D,), jnp.float32), -5.0, 5.0)


def draw_k_gain(key, part):
    own_key = jax.random.fold_in(key, 43)
    return 1.0 + 0.15 * jnp.clip(jax.random.normal(own_key, (D,), jnp.float32), -5.0, 5.0)


def block_scale(key, extent, cuts, smallest, high):
    def one(dim, parts):
        draws = jax.random.uniform(jax.random.fold_in(jax.random.fold_in(key, 6), dim), (parts,), jnp.float32, smallest / len(cuts), high / len(cuts))
        return jnp.repeat(jnp.exp(draws), extent[dim] // parts).reshape((-1,) + (1,) * (len(extent) - dim - 1))

    level = one(*cuts[0])
    for cut in cuts[1:]:
        level = level * one(*cut)
    return level


def scatter_about(key, shape, scale, most, shards=(), held_as=jnp.bfloat16):
    array = scale * jax.random.normal(key, shape, jnp.float32)
    if shards:
        array = array * block_scale(key, shape, shards, -0.22, 0.18)
    return jnp.clip(array, -most, most).astype(held_as)


def setup_inputs(seed: int = 0) -> dict:
    key_list = jax.random.split(jax.random.key(seed), 12)
    hidden = draw_hidden(jax.random.fold_in(key_list[11], 71), 0)
    latent = scatter_about(key_list[1], (REQUESTS, TOKENS, OUT), 1.0, 6.0, ((0, 8), (1, 2), (2, 2)), jnp.float32)
    modulation = scatter_about(key_list[2], (REQUESTS, 5, D), 0.5, 3.0, ((0, 8),), jnp.float32)
    w_qkv = draw_w_qkv(jax.random.fold_in(key_list[11], 71), 0)
    w_out = scatter_about(key_list[4], (D, D), D ** -0.5, 0.15625, ((0, 8),))
    q_gain = draw_q_gain(jax.random.fold_in(key_list[11], 71), 0)
    k_gain = draw_k_gain(jax.random.fold_in(key_list[11], 71), 0)
    w_head = scatter_about(key_list[7], (D, OUT), D ** -0.5, 0.15625)
    lengths = draw_lengths(jax.random.fold_in(key_list[11], 71), 0)
    guidance = jnp.clip(3.0 + 4.0 * jax.random.uniform(key_list[9], (REQUESTS,), jnp.float32) ** block_scale(key_list[9], (REQUESTS,), ((0, 8),), -0.2, 0.2), 3.0, 7.0)
    step_size = jnp.clip(jnp.exp(math.log(0.3) - 2.3025852 * jax.random.uniform(key_list[10], (REQUESTS,), jnp.float32) ** block_scale(key_list[10], (REQUESTS,), ((0, 8),), -0.2, 0.2)), 0.03, 0.3)
    return {"hidden": hidden, "latent": latent, "modulation": modulation, "w_qkv": w_qkv, "w_out": w_out, "q_gain": q_gain, "k_gain": k_gain, "w_head": w_head, "lengths": lengths, "guidance": guidance, "step_size": step_size}


def layer_norm(values):
    centered = values - lax.optimization_barrier(jnp.mean(values, axis=-1, keepdims=True))
    return centered / jnp.sqrt(lax.optimization_barrier(jnp.mean(centered * centered, axis=-1, keepdims=True)) + 1e-06)

def rms_gain(values, gain):
    return values / jnp.sqrt(lax.optimization_barrier(jnp.mean(values * values, axis=-1, keepdims=True)) + 1e-06) * gain

def one_pass(state, modes, w_qkv, w_out, q_gain, k_gain, w_head, valid):
    width = state.shape[1]
    wide = state.astype(jnp.float32)
    normed = (layer_norm(wide) * (1.0 + modes[1]) + modes[0]).astype(jnp.bfloat16)
    qkv = jnp.dot(normed, w_qkv, preferred_element_type=jnp.float32)
    query = rms_gain(qkv[:, :width], q_gain).astype(jnp.bfloat16)
    keys = rms_gain(qkv[:, width:2 * width], k_gain).astype(jnp.bfloat16)
    values = qkv[:, 2 * width:].astype(jnp.bfloat16)
    rows = state.shape[0]
    query = query.reshape(rows, H, DH).astype(jnp.float32)
    keys = keys.reshape(rows, H, DH).astype(jnp.float32)
    values = values.reshape(rows, H, DH).astype(jnp.float32)
    scores = jnp.einsum('qhd,khd->qhk', query, keys) / jnp.sqrt(jnp.float32(DH))
    scores = jnp.where(valid[None, None, :], scores, jnp.float32(-1e+30))
    top = lax.optimization_barrier(jnp.max(scores, axis=-1, keepdims=True))
    probs = jnp.where(valid[None, None, :], jnp.exp(scores - top), jnp.float32(0.0))
    total = lax.optimization_barrier(jnp.sum(probs, axis=-1))
    weighted = jnp.einsum('qhk,khd->qhd', probs.astype(jnp.bfloat16).astype(jnp.float32), values)
    attended = (weighted / total[:, :, None]).reshape(rows, width).astype(jnp.bfloat16)
    projected = jnp.dot(attended, w_out, preferred_element_type=jnp.float32)
    block_out = (wide + modes[2] * projected).astype(jnp.bfloat16)
    head_in = (layer_norm(block_out.astype(jnp.float32)) * (1.0 + modes[4]) + modes[3]).astype(jnp.bfloat16)
    return jnp.dot(head_in, w_head, preferred_element_type=jnp.float32)

def reference(hidden, latent, modulation, w_qkv, w_out, q_gain, k_gain, w_head, lengths, guidance, step_size):

    def per_request(items):
        states, lat, modes, length, scale, step = items
        valid = jnp.arange(states.shape[1], dtype=jnp.int32) < length
        cond = one_pass(states[0], modes, w_qkv, w_out, q_gain, k_gain, w_head, valid)
        uncond = one_pass(states[1], modes, w_qkv, w_out, q_gain, k_gain, w_head, valid)
        guided = uncond + scale * (cond - uncond)
        return jnp.where(valid[:, None], lat - step * guided, lat)
    return lax.map(per_request, (jnp.transpose(hidden, (1, 0, 2, 3)), latent, modulation, lengths, guidance, step_size))
```

```python
import functools

import jax
import jax.numpy as jnp
from jax import lax
from jax.experimental import pallas as pl
from jax.experimental.pallas import tpu as pltpu
from jax.sharding import PartitionSpec as P

DH = 128
SWAP = [(0, 1), (1, 0)]
VMEM = pl.BlockSpec(memory_space=pltpu.VMEM)
SMEM = pl.BlockSpec(memory_space=pltpu.SMEM)
BF16 = jnp.bfloat16
F32 = jnp.float32


def params(megabytes):
    return pltpu.CompilerParams(vmem_limit_bytes=megabytes * 2**20)


def cost(flops, moved, exps=0):
    return pl.CostEstimate(flops=int(flops), bytes_accessed=int(moved), transcendentals=int(exps))


def passed_along(value, axis, steps):
    count = lax.axis_size(axis)
    pairs = [(source, (source + steps) % count) for source in range(count)]
    return lax.ppermute(value, axis, pairs)


def from_partner(value, axis, apart):
    mask = 2**apart
    pairs = [(source, source ^ mask) for source in range(lax.axis_size(axis))]
    return lax.ppermute(value, axis, pairs)


def layer_norm(values):
    centered = values - jnp.mean(values, axis=-1, keepdims=True)
    return centered / jnp.sqrt(jnp.mean(centered * centered, axis=-1, keepdims=True) + 1e-06)


def rms_gain(values, gain):
    return values / jnp.sqrt(jnp.mean(values * values, axis=-1, keepdims=True) + 1e-06) * gain


def add_rows(left, piece):
    return jnp.dot(left, piece, preferred_element_type=jnp.float32)


def attend(state, query, stacked, start, length):
    top, total, weighted = state
    keys = stacked[0]
    values = stacked[1]
    count = keys.shape[0]
    scores = jnp.einsum("qhd,khd->qhk", query, keys, preferred_element_type=jnp.float32) / jnp.sqrt(
        jnp.float32(query.shape[2])
    )
    valid = start + jnp.arange(count, dtype=jnp.int32) < length
    scores = jnp.where(valid[None, None, :], scores, jnp.float32(-1e30))
    new_top = jnp.maximum(top, jnp.max(scores, axis=-1))
    factor = jnp.exp(top - new_top)
    probs = jnp.where(valid[None, None, :], jnp.exp(scores - new_top[:, :, None]), jnp.float32(0.0))
    total = total * factor + jnp.sum(probs, axis=-1)
    weighted = weighted * factor[:, :, None] + jnp.einsum(
        "qhk,khd->qhd", probs.astype(jnp.bfloat16), values, preferred_element_type=jnp.float32
    )
    return (new_top, total, weighted)


def ring_local(
    hidden, latent, modulation, w_qkv, w_out, q_gain, k_gain, w_head, lengths, guidance, step_size
):
    state = hidden[0, 0]
    modes = modulation[0]
    length = lengths[0]
    rows = state.shape[0]
    width = state.shape[1]
    heads = q_gain.shape[0] // DH
    wide = state.astype(jnp.float32)
    normed = (layer_norm(wide) * (1.0 + modes[1]) + modes[0]).astype(jnp.bfloat16)
    qkv = add_rows(normed, lax.all_gather(w_qkv, "req", axis=0, tiled=True))
    query = rms_gain(qkv[:, :width], q_gain).astype(jnp.bfloat16).reshape(rows, heads, DH)
    keys = rms_gain(qkv[:, width : 2 * width], k_gain).astype(jnp.bfloat16).reshape(rows, heads, DH)
    values = qkv[:, 2 * width :].astype(jnp.bfloat16).reshape(rows, heads, DH)
    stacked = jnp.stack([keys, values])
    position = lax.axis_index("seq")
    members = lax.axis_size("seq")
    start_state = (
        jnp.full((rows, heads), -1e30, jnp.float32),
        jnp.zeros((rows, heads), jnp.float32),
        jnp.zeros((rows, heads, DH), jnp.float32),
    )
    first = attend(start_state, query, stacked, position * rows, length)

    def cycle_step(turn, carry):
        moving, inner = carry
        moving = passed_along(moving, "seq", 1)
        source = (position - turn) % members
        return (moving, attend(inner, query, moving, source * rows, length))

    moved, result = lax.fori_loop(1, members, cycle_step, (stacked, first))
    top, total, weighted = result
    attended = (weighted / total[:, :, None]).reshape(rows, width).astype(jnp.bfloat16)
    projected = add_rows(attended, lax.all_gather(w_out, "req", axis=0, tiled=True))
    block_out = (wide + modes[2] * projected).astype(jnp.bfloat16)
    head_in = (layer_norm(block_out.astype(jnp.float32)) * (1.0 + modes[4]) + modes[3]).astype(
        jnp.bfloat16
    )
    velocity = jnp.dot(head_in, w_head, preferred_element_type=jnp.float32)
    branch = lax.axis_index("cfg")
    scale = guidance[0]
    channels = velocity.shape[1] // 2
    own = lax.dynamic_slice_in_dim(velocity, branch * channels, channels, 1)
    outgoing = lax.dynamic_slice_in_dim(velocity, (1 - branch) * channels, channels, 1)
    other = from_partner(outgoing.astype(jnp.bfloat16), "cfg", 0).astype(outgoing.dtype)
    cond = jnp.where(branch == 0, own, other)
    uncond = jnp.where(branch == 0, other, own)
    guided = uncond + scale * (cond - uncond)
    valid = position * rows + jnp.arange(rows, dtype=jnp.int32) < length
    current = latent[0]
    updated = jnp.where(valid[:, None], current - step_size[0] * guided, current)
    return updated[None]


def norm_kernel(state_ref, modes_ref, out_ref):
    wide = state_ref[...].astype(F32)
    scale = 1.0 + modes_ref[1:2, :]
    out_ref[...] = (layer_norm(wide) * scale + modes_ref[0:1, :]).astype(BF16)


def normalise(state, modes):
    return pl.pallas_call(
        norm_kernel,
        out_shape=jax.ShapeDtypeStruct(state.shape, BF16),
        in_specs=[VMEM, VMEM],
        out_specs=VMEM,
        compiler_params=params(24),
        cost_estimate=cost(10 * state.size, 4 * state.size),
    )(state, modes)


def place_pair(pair_ref, first_ref, second_ref, side):
    depth = first_ref.shape[0]
    pair_ref[pl.ds(pl.multiple_of(side * depth, depth), depth), :] = first_ref[...]
    pair_ref[pl.ds(pl.multiple_of((1 - side) * depth, depth), depth), :] = second_ref[...]


def qkv_kernel(pairs, has_acc, sums, *refs):
    where_ref = refs[0]
    norm_refs = refs[1:5]
    piece_refs = refs[5 : 5 + 2 * pairs]
    refs = refs[5 + 2 * pairs :]
    acc_ref = None
    if has_acc:
        acc_ref, refs = refs[0], refs[1:]
    out_ref = refs[0]
    pair_ref = refs[-1]
    depth = piece_refs[0].shape[0]
    side = where_ref[0]
    for k in range(pairs):
        place_pair(pair_ref.at[pl.ds(2 * depth * k, 2 * depth)], piece_refs[2 * k], piece_refs[2 * k + 1], side)
    third = out_ref.shape[2] // 3
    for block in range(4):
        total = acc_ref[block] if has_acc else None
        for k in range(pairs):
            columns = pl.ds(pl.multiple_of(where_ref[1 + k] * 2 * depth, 2 * depth), 2 * depth)
            part = jnp.dot(
                norm_refs[block][:, columns],
                pair_ref[2 * depth * k : 2 * depth * (k + 1), :],
                preferred_element_type=F32,
            )
            total = part if total is None else total + part
        out_ref[block] = total
        if sums:
            sums_ref = refs[1]
            ones = jnp.ones((8, third), F32)
            for j in range(2):
                part = total[:, j * third : (j + 1) * third]
                sums_ref[block, 8 * j : 8 * j + 8, :] = lax.dot_general(
                    ones,
                    part * part,
                    (((1,), (1,)), ((), ())),
                    precision=lax.Precision.HIGHEST,
                    preferred_element_type=F32,
                )


def qkv_part(where, norms, pieces, acc, sums):
    rows = norms[0].shape[0]
    depth, columns = pieces[0].shape
    pairs = len(pieces) // 2
    out_shape = [jax.ShapeDtypeStruct((4, rows, columns), F32)]
    if sums:
        out_shape.append(jax.ShapeDtypeStruct((4, 16, rows), F32))
    inputs = [where, *norms, *pieces] + ([] if acc is None else [acc])
    return pl.pallas_call(
        functools.partial(qkv_kernel, pairs, acc is not None, sums),
        out_shape=out_shape,
        in_specs=[SMEM] + [VMEM] * (len(inputs) - 1),
        out_specs=[VMEM] * len(out_shape),
        scratch_shapes=[pltpu.VMEM((2 * depth * pairs, columns), BF16)],
        compiler_params=params(40),
        cost_estimate=cost(2 * 4 * rows * 2 * depth * pairs * columns, 4 * rows * columns * 4),
    )(*inputs)


def heads_kernel(length_ref, qkv_ref, sums_ref, q_gain_ref, k_gain_ref, far1_ref, far3_ref, q_ref, k_ref, v_ref):
    rows = qkv_ref.shape[1]
    third = qkv_ref.shape[2] // 3
    width = 4 * third
    factor = 1.4426950408889634 / DH**0.5
    row = lax.broadcasted_iota(jnp.int32, (16, DH), 0)
    pick_q = (row == 0).astype(F32)
    pick_k = (row == 8).astype(F32)

    def inverse(block, pick):
        total = lax.dot_general(
            sums_ref[block],
            pick,
            (((0,), (0,)), ((), ())),
            precision=lax.Precision.HIGHEST,
            preferred_element_type=F32,
        )
        return lax.rsqrt(total * (1.0 / width) + 1e-06)

    for block in range(4):
        scale_q = inverse(block, pick_q) * factor
        scale_k = inverse(block, pick_k)
        for h in range(third // DH):
            at = slice(h * DH, (h + 1) * DH)
            q_ref[block, :, at] = (qkv_ref[block, :, at] * scale_q * q_gain_ref[:, at]).astype(BF16)
            at_k = slice(third + h * DH, third + (h + 1) * DH)
            k_ref[block, :, at] = (qkv_ref[block, :, at_k] * scale_k * k_gain_ref[:, at]).astype(BF16)
        v_ref[block] = qkv_ref[block, :, 2 * third :].astype(BF16)
    attend_block(length_ref, q_ref, k_ref, v_ref, 1, far1_ref)
    attend_block(length_ref, q_ref, k_ref, v_ref, 3, far3_ref)


def attend_block(length_ref, q_ref, k_ref, v_ref, block, out_ref):
    rows = q_ref.shape[1]
    first = block - block % 2
    place = lax.broadcasted_iota(jnp.int32, (1, rows), 1)
    masks = [place < length_ref[j] for j in range(2)]
    for h in range(q_ref.shape[2] // DH):
        at = slice(h * DH, (h + 1) * DH)
        query = q_ref[block, :, at]
        scores = []
        for j in range(2):
            part = lax.dot_general(
                query, k_ref[first + j, :, at], (((1,), (1,)), ((), ())), preferred_element_type=F32
            )
            scores.append(jnp.where(masks[j], part, -1e30))
        top = jnp.maximum(
            jnp.max(scores[0], axis=-1, keepdims=True), jnp.max(scores[1], axis=-1, keepdims=True)
        )
        total = 0.0
        weighted = 0.0
        for j in range(2):
            probs = jnp.exp2(scores[j] - top)
            total += jnp.sum(probs, axis=-1, keepdims=True)
            weighted += jnp.dot(probs.astype(BF16), v_ref[first + j, :, at], preferred_element_type=F32)
        out_ref[:, at] = (weighted / total).astype(BF16)


def near_kernel(length_ref, q_ref, k_ref, v_ref, near2_ref, near0_ref):
    attend_block(length_ref, q_ref, k_ref, v_ref, 2, near2_ref)
    attend_block(length_ref, q_ref, k_ref, v_ref, 0, near0_ref)


def attention(lengths, qkv, sums, q_gain, k_gain):
    rows = qkv.shape[1]
    third = qkv.shape[2] // 3
    block = jax.ShapeDtypeStruct((rows, third), BF16)
    blocks = jax.ShapeDtypeStruct((4, rows, third), BF16)
    flops = 2 * 2 * rows * 2 * 2 * rows * third
    far1, far3, q, k, v = pl.pallas_call(
        heads_kernel,
        out_shape=[block, block, blocks, blocks, blocks],
        in_specs=[SMEM] + [VMEM] * 4,
        out_specs=[VMEM] * 5,
        compiler_params=params(40),
        cost_estimate=cost(flops, qkv.size * 6, flops // 512),
    )(lengths, qkv, sums, q_gain, k_gain)
    near2, near0 = pl.pallas_call(
        near_kernel,
        out_shape=[block, block],
        in_specs=[SMEM] + [VMEM] * 3,
        out_specs=[VMEM] * 2,
        compiler_params=params(40),
        cost_estimate=cost(flops, qkv.size * 2, flops // 512),
    )(lengths, q, k, v)
    return far1, far3, near2, near0


def out_kernel(where_ref, state_ref, modes_ref, head_ref, *refs):
    attended = refs[:4]
    rest = refs[4:]
    pieces = rest[:-4]
    out_ref, group_ref, pair_ref, sum_ref = rest[-4:]
    side, core, own = where_ref[0], where_ref[1], where_ref[2]
    for j in range(4):
        group_ref[j] = attended[j][...]
    half = len(pieces) // 2
    columns = pieces[0].shape[1]
    pairs = half // 2
    depth = pieces[0].shape[0]
    for which in range(2):
        total = None
        for k in range(pairs):
            base = which * half + 2 * k
            place_pair(pair_ref.at[which * pairs + k], pieces[base], pieces[base + 1], side)
            part = jnp.dot(
                group_ref[where_ref[3 + k] ^ own],
                pair_ref[which * pairs + k],
                preferred_element_type=F32,
            )
            total = part if total is None else total + part
        spot = (core if which == 0 else 1 - core) * columns
        sum_ref[:, pl.ds(pl.multiple_of(spot, columns), columns)] = total
    block_out = (state_ref[...].astype(F32) + modes_ref[2:3, :] * sum_ref[...]).astype(BF16)
    head_in = layer_norm(block_out.astype(F32)) * (1.0 + modes_ref[4:5, :]) + modes_ref[3:4, :]
    out_ref[...] = jnp.dot(head_in.astype(BF16), head_ref[...], preferred_element_type=F32)


def project(where, state, modes, w_head, attended, pieces):
    rows, width = state.shape
    depth, columns = pieces[0].shape
    inputs = [where, state, modes, w_head, *attended, *pieces]
    return pl.pallas_call(
        out_kernel,
        out_shape=jax.ShapeDtypeStruct((rows, w_head.shape[1]), F32),
        in_specs=[SMEM] + [VMEM] * (len(inputs) - 1),
        out_specs=VMEM,
        scratch_shapes=[
            pltpu.VMEM((4, rows, width // 4), BF16),
            pltpu.VMEM((len(pieces) // 2, 2 * depth, columns), BF16),
            pltpu.VMEM((rows, width), F32),
        ],
        compiler_params=params(48),
        cost_estimate=cost(2 * rows * width * width, 2 * width * width),
    )(*inputs)


def updated_latent(velocity, latent, guidance, step_size, length, position):
    rows = velocity.shape[0]
    branch = lax.axis_index("cfg")
    scale = guidance[0]
    channels = velocity.shape[1] // 2
    own = lax.dynamic_slice_in_dim(velocity, branch * channels, channels, 1)
    outgoing = lax.dynamic_slice_in_dim(velocity, (1 - branch) * channels, channels, 1)
    other = lax.ppermute(outgoing.astype(BF16), "cfg", SWAP).astype(outgoing.dtype)
    cond = jnp.where(branch == 0, own, other)
    uncond = jnp.where(branch == 0, other, own)
    guided = uncond + scale * (cond - uncond)
    valid = position * rows + jnp.arange(rows, dtype=jnp.int32) < length
    current = latent[0]
    updated = jnp.where(valid[:, None], current - step_size[0] * guided, current)
    return updated[None]


def team_local(
    hidden, latent, modulation, w_qkv, w_out, q_gain, k_gain, w_head, lengths, guidance, step_size
):
    state = hidden[0, 0]
    modes = modulation[0]
    rows, width = state.shape
    depth = w_qkv.shape[0]
    third = width // 4
    core = lax.axis_index("cfg")
    position = lax.axis_index("seq")
    place = lax.axis_index("req")
    parts = lax.axis_size("req")
    side, pair = place % 2, place // 2
    group = 2 * position + core
    along = [(i, (i - 2) % parts) for i in range(parts)]
    across = [(i, i ^ 1) for i in range(parts)]
    steps = parts // 2
    owners = [(pair + k) % steps for k in range(steps)]

    def gathered(own):
        mine = [own]
        for _ in range(steps - 1):
            mine.append(lax.ppermute(mine[-1], "req", along))
        theirs = [lax.ppermute(piece, "req", across) for piece in mine]
        return [piece for both in zip(mine, theirs) for piece in both]

    normed = normalise(state, modes)
    normed_y = lax.ppermute(normed, "seq", SWAP)
    normed_c = lax.ppermute(normed, "cfg", SWAP)
    normed_yc = lax.ppermute(normed_y, "cfg", SWAP)
    norms = [normed, normed_y, normed_c, normed_yc]
    columns = jnp.concatenate(
        [lax.dynamic_slice_in_dim(w_qkv, j * width + group * third, third, 1) for j in range(3)], axis=1
    )
    pieces = gathered(columns)
    half = width // 2
    out_own = gathered(lax.dynamic_slice_in_dim(w_out, core * half, half, 1))
    out_other = [lax.ppermute(piece, "cfg", SWAP) for piece in out_own]

    first = jnp.stack([side] + owners[:-1]).astype(jnp.int32)
    last = jnp.stack([side, owners[-1]]).astype(jnp.int32)
    (acc,) = qkv_part(first, norms, pieces[:-2], None, False)
    qkv, sums = qkv_part(last, norms, pieces[-2:], acc, True)
    theirs = lax.ppermute(sums, "cfg", SWAP)
    sums = sums + jnp.concatenate([theirs[2:], theirs[:2]])
    theirs = lax.ppermute(sums, "seq", SWAP)
    sums = sums + jnp.concatenate([theirs[1:2], theirs[0:1], theirs[3:4], theirs[2:3]])
    length = lengths[0]
    limits = jnp.stack([length - position * rows, length - (1 - position) * rows]).astype(jnp.int32)
    gain_q = lax.dynamic_slice_in_dim(q_gain, group * third, third, 0)[None]
    gain_k = lax.dynamic_slice_in_dim(k_gain, group * third, third, 0)[None]
    far1, far3, near2, near0 = attention(limits, qkv, sums, gain_q, gain_k)
    diagonal = [(i, 3 - i) for i in range(4)]
    attended = [
        near0,
        lax.ppermute(near2, "cfg", SWAP),
        lax.ppermute(far1, "seq", SWAP),
        lax.ppermute(far3, ("cfg", "seq"), diagonal),
    ]
    where = jnp.stack([side, core, group] + owners).astype(jnp.int32)
    velocity = project(where, state, modes, w_head, attended, out_own + out_other)
    return updated_latent(velocity, latent, guidance, step_size, length, position)


def by_team(mesh, arguments):
    hidden, w_qkv = arguments[0], arguments[3]
    sizes = mesh.shape
    width = hidden.shape[3]
    depth = w_qkv.shape[0] // sizes["req"]
    return (
        sizes["cfg"] == 2
        and sizes["seq"] == 2
        and sizes["req"] % 2 == 0
        and width % (4 * DH) == 0
        and 2 * depth == width // 4
        and depth % 16 == 0
        and hidden.shape[2] // sizes["seq"] % 16 == 0
    )


def solution(mesh):
    def whole(*arguments):
        body = team_local if by_team(mesh, arguments) else ring_local
        return jax.shard_map(
            body,
            mesh=mesh,
            in_specs=(
                P("cfg", "req", "seq", None),
                P("req", "seq", "cfg"),
                P("req", None, None),
                P("req", None),
                P("req", None),
                P(),
                P(),
                P(),
                P("req"),
                P("req"),
                P("req"),
            ),
            out_specs=P("req", "seq", "cfg"),
            check_vma=False,
        )(*arguments)

    return whole
```

```python
import functools

import jax
import jax.numpy as jnp
from jax import lax
from jax.experimental import pallas as pl
from jax.experimental.pallas import tpu as pltpu
from jax.sharding import PartitionSpec as P

DH = 128
SWAP = [(0, 1), (1, 0)]
SMEM = pl.BlockSpec(memory_space=pltpu.SMEM)
ANY = pl.BlockSpec(memory_space=pl.ANY)
BF16 = jnp.bfloat16
F32 = jnp.float32


def params():
    return pltpu.CompilerParams(vmem_limit_bytes=60 * 2**20)


def cost(flops, moved, exps=0):
    return pl.CostEstimate(flops=int(flops), bytes_accessed=int(moved), transcendentals=int(exps))


def shape_of(*dims, dtype=BF16):
    return jax.ShapeDtypeStruct(dims, dtype)


def times(left, right):
    return jnp.dot(left, right, preferred_element_type=F32)


def times_turned(left, right):
    return lax.dot_general(left, right, (((1,), (1,)), ((), ())), preferred_element_type=F32)


def load_all(pairs, sem):
    copies = [pltpu.make_async_copy(source, target, sem.at[j]) for j, (source, target) in enumerate(pairs)]
    for copy in copies:
        copy.start()
    return copies


def passed_along(value, axis, steps):
    count = lax.axis_size(axis)
    pairs = [(source, (source + steps) % count) for source in range(count)]
    return lax.ppermute(value, axis, pairs)


def from_partner(value, axis, apart):
    mask = 2**apart
    pairs = [(source, source ^ mask) for source in range(lax.axis_size(axis))]
    return lax.ppermute(value, axis, pairs)


def layer_norm(values):
    centered = values - jnp.mean(values, axis=-1, keepdims=True)
    return centered / jnp.sqrt(jnp.mean(centered * centered, axis=-1, keepdims=True) + 1e-06)


def rms_gain(values, gain):
    return values / jnp.sqrt(jnp.mean(values * values, axis=-1, keepdims=True) + 1e-06) * gain


def add_rows(left, piece):
    return jnp.dot(left, piece, preferred_element_type=jnp.float32)


def attend(state, query, stacked, start, length):
    top, total, weighted = state
    keys = stacked[0]
    values = stacked[1]
    count = keys.shape[0]
    scores = jnp.einsum("qhd,khd->qhk", query, keys, preferred_element_type=jnp.float32) / jnp.sqrt(
        jnp.float32(query.shape[2])
    )
    valid = start + jnp.arange(count, dtype=jnp.int32) < length
    scores = jnp.where(valid[None, None, :], scores, jnp.float32(-1e30))
    new_top = jnp.maximum(top, jnp.max(scores, axis=-1))
    factor = jnp.exp(top - new_top)
    probs = jnp.where(valid[None, None, :], jnp.exp(scores - new_top[:, :, None]), jnp.float32(0.0))
    total = total * factor + jnp.sum(probs, axis=-1)
    weighted = weighted * factor[:, :, None] + jnp.einsum(
        "qhk,khd->qhd", probs.astype(jnp.bfloat16), values, preferred_element_type=jnp.float32
    )
    return (new_top, total, weighted)


def ring_local(
    hidden, latent, modulation, w_qkv, w_out, q_gain, k_gain, w_head, lengths, guidance, step_size
):
    state = hidden[0, 0]
    modes = modulation[0]
    length = lengths[0]
    rows = state.shape[0]
    width = state.shape[1]
    heads = q_gain.shape[0] // DH
    wide = state.astype(jnp.float32)
    normed = (layer_norm(wide) * (1.0 + modes[1]) + modes[0]).astype(jnp.bfloat16)
    qkv = add_rows(normed, lax.all_gather(w_qkv, "req", axis=0, tiled=True))
    query = rms_gain(qkv[:, :width], q_gain).astype(jnp.bfloat16).reshape(rows, heads, DH)
    keys = rms_gain(qkv[:, width : 2 * width], k_gain).astype(jnp.bfloat16).reshape(rows, heads, DH)
    values = qkv[:, 2 * width :].astype(jnp.bfloat16).reshape(rows, heads, DH)
    stacked = jnp.stack([keys, values])
    position = lax.axis_index("seq")
    members = lax.axis_size("seq")
    start_state = (
        jnp.full((rows, heads), -1e30, jnp.float32),
        jnp.zeros((rows, heads), jnp.float32),
        jnp.zeros((rows, heads, DH), jnp.float32),
    )
    first = attend(start_state, query, stacked, position * rows, length)

    def cycle_step(turn, carry):
        moving, inner = carry
        moving = passed_along(moving, "seq", 1)
        source = (position - turn) % members
        return (moving, attend(inner, query, moving, source * rows, length))

    moved, result = lax.fori_loop(1, members, cycle_step, (stacked, first))
    top, total, weighted = result
    attended = (weighted / total[:, :, None]).reshape(rows, width).astype(jnp.bfloat16)
    projected = add_rows(attended, lax.all_gather(w_out, "req", axis=0, tiled=True))
    block_out = (wide + modes[2] * projected).astype(jnp.bfloat16)
    head_in = (layer_norm(block_out.astype(jnp.float32)) * (1.0 + modes[4]) + modes[3]).astype(
        jnp.bfloat16
    )
    velocity = jnp.dot(head_in, w_head, preferred_element_type=jnp.float32)
    branch = lax.axis_index("cfg")
    scale = guidance[0]
    channels = velocity.shape[1] // 2
    own = lax.dynamic_slice_in_dim(velocity, branch * channels, channels, 1)
    outgoing = lax.dynamic_slice_in_dim(velocity, (1 - branch) * channels, channels, 1)
    other = from_partner(outgoing.astype(jnp.bfloat16), "cfg", 0).astype(outgoing.dtype)
    cond = jnp.where(branch == 0, own, other)
    uncond = jnp.where(branch == 0, other, own)
    guided = uncond + scale * (cond - uncond)
    valid = position * rows + jnp.arange(rows, dtype=jnp.int32) < length
    current = latent[0]
    updated = jnp.where(valid[:, None], current - step_size[0] * guided, current)
    return updated[None]


def norm_kernel(where_ref, state_ref, modes_ref, out_ref, state_in, modes_in, full_ref, out_buf, sem):
    side, pair, steps = where_ref[0], where_ref[1], where_ref[2]
    for copy in load_all([(state_ref, state_in), (modes_ref, modes_in)], sem):
        copy.wait()
    wide = state_in[...].astype(F32)
    full_ref[...] = layer_norm(wide) * (1.0 + modes_in[1]) + modes_in[0]
    count = 4
    depth = out_ref.shape[1] // count
    for k in range(count):
        owner = lax.rem(pair + k, steps)
        part = full_ref[:, pl.ds(pl.multiple_of(owner * depth, depth), depth)]
        part = jnp.where(side == 0, part, pltpu.roll(part, depth // 2, 1))
        out_buf[:, k * depth : (k + 1) * depth] = part.astype(BF16)
    for copy in load_all([(out_buf, out_ref)], sem):
        copy.wait()


def normalise(where, state, modes):
    return pl.pallas_call(
        norm_kernel,
        out_shape=shape_of(*state.shape),
        in_specs=[SMEM, ANY, ANY],
        out_specs=ANY,
        scratch_shapes=[
            pltpu.VMEM(state.shape, BF16),
            pltpu.VMEM(modes.shape, F32),
            pltpu.VMEM(state.shape, F32),
            pltpu.VMEM(state.shape, BF16),
            pltpu.SemaphoreType.DMA((2,)),
        ],
        compiler_params=params(),
        cost_estimate=cost(4e9, 1e6),
    )(where, state, modes)


def cut_kernel(where_ref, qkv_ref, out_ref, cut_ref, buf, sem):
    group = where_ref[0]
    third = cut_ref.shape[1] // 4
    width = qkv_ref.shape[1] // 3
    pairs = []
    for j in range(4):
        source_ref, base = (qkv_ref, j * width) if j < 3 else (out_ref, 0)
        source = source_ref.at[:, pl.ds(pl.multiple_of(base + group * third, third), third)]
        pairs.append((source, buf.at[:, j * third : (j + 1) * third]))
    for copy in load_all(pairs, sem):
        copy.wait()
    for copy in load_all([(buf, cut_ref)], sem):
        copy.wait()


def cut_columns(group, w_qkv, w_out):
    depth, width = w_out.shape
    return pl.pallas_call(
        cut_kernel,
        out_shape=shape_of(depth, width),
        in_specs=[SMEM, ANY, ANY],
        out_specs=ANY,
        scratch_shapes=[pltpu.VMEM((depth, width), BF16), pltpu.SemaphoreType.DMA((4,))],
        compiler_params=params(),
        cost_estimate=cost(2e9, 1e6),
    )(group, w_qkv, w_out)


def pack_kernel(count, *refs):
    pieces, packed_ref, held_ref, sem = refs[:count], refs[count], refs[count + 1], refs[count + 2]
    depth = held_ref.shape[0] // count
    columns = held_ref.shape[1]
    pairs = []
    for k, piece in enumerate(pieces):
        pairs.append((piece.at[:, piece.shape[1] - columns :], held_ref.at[k * depth : (k + 1) * depth]))
    for copy in load_all(pairs, sem):
        copy.wait()
    for copy in load_all([(held_ref, packed_ref)], sem):
        copy.wait()


def pack(pieces, columns):
    depth = pieces[0].shape[0]
    full = shape_of(depth * len(pieces), columns)
    return pl.pallas_call(
        functools.partial(pack_kernel, len(pieces)),
        out_shape=full,
        in_specs=[ANY] * len(pieces),
        out_specs=ANY,
        scratch_shapes=[pltpu.VMEM(full.shape, BF16), pltpu.SemaphoreType.DMA((len(pieces),))],
        compiler_params=params(),
        cost_estimate=cost(3e9, 1e6),
    )(*pieces)


def rows_of(piece_refs, held_ref, start=0):
    found, at = [], 0
    for piece in piece_refs:
        rows = piece.shape[0]
        source = piece.at[:, start : start + held_ref.shape[1]]
        found.append((source, held_ref.at[at : at + rows]))
        at += rows
    return found


def first_kernel(count, *refs):
    norms, pieces = refs[:4], refs[4 : 4 + count]
    qk_ref, v_ref = refs[4 + count : 6 + count]
    left_ref, held_ref, qk_out, v_out, sem, out_sem = refs[6 + count :]
    deep, columns = held_ref.shape
    split = 2 * columns // 3
    loads = load_all(
        rows_of(pieces, held_ref) + [(norms[b].at[:, :deep], left_ref.at[b]) for b in range(4)], sem
    )
    for copy in loads:
        copy.wait()
    stores = []
    for block in range(4):
        qk_out[block] = times(left_ref[block], held_ref[:, :split])
        v_out[block] = times(left_ref[block], held_ref[:, split:])
        for j, (source, target) in enumerate(((qk_out, qk_ref), (v_out, v_ref))):
            copy = pltpu.make_async_copy(source.at[block], target.at[block], out_sem.at[2 * block + j])
            copy.start()
            stores.append(copy)
    for copy in stores:
        copy.wait()


def first_part(norms, pieces):
    rows = norms[0].shape[0]
    columns = 3 * norms[0].shape[1] // 4
    deep = sum(piece.shape[0] for piece in pieces)
    qk = shape_of(4, rows, 2 * columns // 3, dtype=F32)
    v = shape_of(4, rows, columns // 3, dtype=F32)
    return pl.pallas_call(
        functools.partial(first_kernel, len(pieces)),
        out_shape=[qk, v],
        in_specs=[ANY] * (4 + len(pieces)),
        out_specs=[ANY] * 2,
        scratch_shapes=[
            pltpu.VMEM((4, rows, deep), BF16),
            pltpu.VMEM((deep, columns), BF16),
            pltpu.VMEM(qk.shape, F32),
            pltpu.VMEM(v.shape, F32),
            pltpu.SemaphoreType.DMA((4 + len(pieces),)),
            pltpu.SemaphoreType.DMA((8,)),
        ],
        compiler_params=params(),
        cost_estimate=cost(6e9, 1e6),
    )(*norms, *pieces)


def scores_kernel(count, *refs):
    norms, acc_ref, pieces = refs[:4], refs[4], refs[5 : 5 + count]
    out_ref, sums_ref, left_ref, held_ref, acc_in, sums_buf, sem, out_sem = refs[5 + count :]
    deep = held_ref.shape[0]
    third = out_ref.shape[2] // 2
    width = norms[0].shape[1]
    loads = load_all(
        rows_of(pieces, held_ref)
        + [(norms[b].at[:, width - deep :], left_ref.at[b]) for b in range(4)]
        + [(acc_ref.at[b], acc_in.at[b]) for b in range(4)],
        sem,
    )
    for copy in loads[: count + 4]:
        copy.wait()
    row = lax.broadcasted_iota(jnp.int32, (8, 4 * DH), 0)
    lane = lax.broadcasted_iota(jnp.int32, (8, 4 * DH), 1)
    pick = (row == lane // (2 * DH)).astype(BF16)
    stores = []
    for block in range(4):
        product = times(left_ref[block], held_ref[...])
        loads[count + 4 + block].wait()
        total = acc_in[block] + product
        acc_in[block] = total
        stores.append(pltpu.make_async_copy(acc_in.at[block], out_ref.at[block], out_sem.at[block]))
        stores[-1].start()
        squares = []
        for j in range(2):
            square = 0.0
            for h in range(third // DH):
                part = total[:, j * third + h * DH : j * third + (h + 1) * DH]
                square += part * part
            high = square.astype(BF16)
            squares += [high, (square - high.astype(F32)).astype(BF16)]
        sums_buf[block] = times_turned(pick, jnp.concatenate(squares, axis=1))
    stores.append(pltpu.make_async_copy(sums_buf, sums_ref, out_sem.at[4]))
    stores[-1].start()
    for copy in stores:
        copy.wait()


def last_scores(norms, acc, pieces):
    rows = norms[0].shape[0]
    columns = acc.shape[2]
    deep = sum(piece.shape[0] for piece in pieces)
    return pl.pallas_call(
        functools.partial(scores_kernel, len(pieces)),
        out_shape=[shape_of(4, rows, columns, dtype=F32), shape_of(4, 8, rows, dtype=F32)],
        in_specs=[ANY] * 5 + [ANY] * len(pieces),
        out_specs=[ANY, ANY],
        scratch_shapes=[
            pltpu.VMEM((4, rows, deep), BF16),
            pltpu.VMEM((deep, columns), BF16),
            pltpu.VMEM(acc.shape, F32),
            pltpu.VMEM((4, 8, rows), F32),
            pltpu.SemaphoreType.DMA((8 + len(pieces),)),
            pltpu.SemaphoreType.DMA((5,)),
        ],
        compiler_params=params(),
        cost_estimate=cost(6e9, 1e6),
    )(*norms, acc, *pieces)


def values_kernel(count, *refs):
    norms, acc_ref, pieces = refs[:4], refs[4], refs[5 : 5 + count]
    out_ref, left_ref, held_ref, acc_in, out_buf, sem = refs[5 + count :]
    deep, columns = held_ref.shape
    width = norms[0].shape[1]
    loads = load_all(
        rows_of(pieces, held_ref, 2 * columns)
        + [(norms[b].at[:, width - deep :], left_ref.at[b]) for b in range(4)]
        + [(acc_ref.at[b], acc_in.at[b]) for b in range(4)],
        sem,
    )
    for copy in loads:
        copy.wait()
    for block in range(4):
        out_buf[block] = (acc_in[block] + times(left_ref[block], held_ref[...])).astype(BF16)
    for copy in load_all([(out_buf, out_ref)], sem):
        copy.wait()


def last_values(norms, acc, pieces):
    rows = norms[0].shape[0]
    columns = acc.shape[2]
    deep = sum(piece.shape[0] for piece in pieces)
    return pl.pallas_call(
        functools.partial(values_kernel, len(pieces)),
        out_shape=shape_of(4, rows, columns),
        in_specs=[ANY] * 5 + [ANY] * len(pieces),
        out_specs=ANY,
        scratch_shapes=[
            pltpu.VMEM((4, rows, deep), BF16),
            pltpu.VMEM((deep, columns), BF16),
            pltpu.VMEM(acc.shape, F32),
            pltpu.VMEM(acc.shape, BF16),
            pltpu.SemaphoreType.DMA((8 + len(pieces),)),
        ],
        compiler_params=params(),
        cost_estimate=cost(4e9, 1e6),
    )(*norms, acc, *pieces)


def heads_kernel(where_ref, qk_ref, v_ref, s0_ref, s1_ref, s2_ref, s3_ref, gains_ref, *refs):
    outs = refs[:4]
    qk_in, v_in, sums_in, gains_in, out_buf, q_buf, k_buf, sem, out_sem = refs[4:]
    third = qk_ref.shape[2] // 2
    width = 4 * third
    factor = 1.4426950408889634 / DH**0.5
    sum_refs = (s0_ref, s1_ref, s2_ref, s3_ref)
    loads = load_all(
        [(sum_refs[j], sums_in.at[j]) for j in range(4)]
        + [(gains_ref, gains_in)]
        + [(qk_ref.at[b], qk_in.at[b]) for b in range(4)]
        + [(v_ref, v_in)],
        sem,
    )
    row = lax.broadcasted_iota(jnp.int32, (24, 2 * DH), 0)
    lane = lax.broadcasted_iota(jnp.int32, (24, 2 * DH), 1)
    pick = (row % 8 == lane // DH).astype(BF16)
    mine = pl.ds(pl.multiple_of(where_ref[3] * third, third), third)
    for copy in loads[:5]:
        copy.wait()
    gains = [gains_in[0, :, mine] * factor, gains_in[1, :, mine]]
    stores = []
    for block in range(4):
        sums = sums_in[0, block] + sums_in[1, block ^ 1] + sums_in[2, block ^ 2] + sums_in[3, block ^ 3]
        inverse = lax.rsqrt(sums * (1.0 / width) + 1e-06)
        high = inverse.astype(BF16).astype(F32)
        middle = (inverse - high).astype(BF16).astype(F32)
        stacked = jnp.concatenate([high, middle, inverse - high - middle], axis=0).astype(BF16)
        scales = lax.dot_general(stacked, pick, (((0,), (0,)), ((), ())), preferred_element_type=F32)
        loads[5 + block].wait()
        for j, buf in enumerate((q_buf, k_buf)):
            scale = scales[:, j * DH : (j + 1) * DH]
            for h in range(third // DH):
                at = slice(h * DH, (h + 1) * DH)
                raw = qk_in[block, :, j * third + h * DH : j * third + (h + 1) * DH]
                buf[block, :, at] = (raw * scale * gains[j][:, at]).astype(BF16)
    loads[9].wait()
    for block in (1, 3, 2, 0):
        attend_heads(where_ref, q_buf, k_buf, v_in, block, out_buf.at[block])
        stores.append(pltpu.make_async_copy(out_buf.at[block], outs[block], out_sem.at[block]))
        stores[-1].start()
    for copy in stores:
        copy.wait()


def attend_heads(where_ref, q_ref, k_ref, v_ref, block, out_ref):
    rows = q_ref.shape[1]
    first = block - block % 2
    place = lax.broadcasted_iota(jnp.int32, (1, rows), 1)
    masks = [place < where_ref[4 + j] for j in range(2)]
    for h in range(q_ref.shape[2] // DH):
        at = slice(h * DH, (h + 1) * DH)
        query = q_ref[block, :, at]
        scores = []
        for j in range(2):
            part = times_turned(query, k_ref[first + j, :, at])
            scores.append(jnp.where(masks[j], part, -1e30))
        top = jnp.maximum(
            jnp.max(scores[0], axis=-1, keepdims=True), jnp.max(scores[1], axis=-1, keepdims=True)
        )
        total = 0.0
        weighted = 0.0
        for j in range(2):
            probs = jnp.exp2(scores[j] - top)
            total += jnp.sum(probs, axis=-1, keepdims=True)
            weighted += times(probs.astype(BF16), v_ref[first + j, :, at])
        out_ref[:, at] = (weighted / total).astype(BF16)


def team_attention(where, qk, v, sums, gains):
    rows = qk.shape[1]
    third = qk.shape[2] // 2
    return pl.pallas_call(
        heads_kernel,
        out_shape=[shape_of(rows, third)] * 4,
        in_specs=[SMEM] + [ANY] * 7,
        out_specs=[ANY] * 4,
        scratch_shapes=[
            pltpu.VMEM(qk.shape, F32),
            pltpu.VMEM(v.shape, BF16),
            pltpu.VMEM((4, 4, 8, rows), F32),
            pltpu.VMEM((2, 1, 4 * third), F32),
            pltpu.VMEM((4, rows, third), BF16),
            pltpu.VMEM((4, rows, third), BF16),
            pltpu.VMEM((4, rows, third), BF16),
            pltpu.SemaphoreType.DMA((10,)),
            pltpu.SemaphoreType.DMA((4,)),
        ],
        compiler_params=params(),
        cost_estimate=cost(1.1e10, 1e6),
    )(where, qk, v, *sums, gains)


def out_kernel(where_ref, state_ref, modes_ref, head_ref, *refs):
    attended, pieces = refs[:4], refs[4:12]
    out_ref, att_in, group_ref, held_ref, state_in, modes_in, head_in_ref, out_buf, sem = refs[12:]
    half = pieces[0].shape[0]
    side, pair, steps, own = (where_ref[j] for j in range(4))
    third = attended[0].shape[1]

    def window(j):
        return pl.ds(pl.multiple_of(j * third, third), third)

    loads = load_all(
        [(attended[j], att_in.at[j]) for j in range(4)]
        + [(pieces[j], held_ref.at[:half, window(own ^ j)]) for j in range(4)]
        + [(pieces[4 + j], held_ref.at[half:, window(own ^ j)]) for j in range(4)]
        + [(state_ref, state_in), (modes_ref, modes_in), (head_ref, head_in_ref)],
        sem,
    )
    for j in range(4):
        loads[j].wait()
        part = att_in[j].astype(F32)
        part = jnp.where(side == 0, part, pltpu.roll(part, third // 2, 1)).astype(BF16)
        group_ref[:, window(lax.rem((own ^ j) + steps - pair, steps))] = part
    for copy in loads[4:]:
        copy.wait()
    total = times(group_ref[...], held_ref[...])
    block_out = (state_in[...].astype(F32) + modes_in[2] * total).astype(BF16)
    head_in = layer_norm(block_out.astype(F32)) * (1.0 + modes_in[4]) + modes_in[3]
    out_buf[...] = times_turned(head_in_ref[...], head_in.astype(BF16))
    for copy in load_all([(out_buf, out_ref)], sem):
        copy.wait()


def project(where, state, modes, w_head, attended, pieces):
    rows, width = state.shape
    third = width // 4
    return pl.pallas_call(
        out_kernel,
        out_shape=shape_of(w_head.shape[0], rows, dtype=F32),
        in_specs=[SMEM] + [ANY] * 15,
        out_specs=ANY,
        scratch_shapes=[
            pltpu.VMEM((4, rows, third), BF16),
            pltpu.VMEM((rows, width), BF16),
            pltpu.VMEM((width, width), BF16),
            pltpu.VMEM(state.shape, BF16),
            pltpu.VMEM(modes.shape, F32),
            pltpu.VMEM(w_head.shape, BF16),
            pltpu.VMEM((w_head.shape[0], rows), F32),
            pltpu.SemaphoreType.DMA((15,)),
        ],
        compiler_params=params(),
        cost_estimate=cost(8e9, 1e6),
    )(where, state, modes, w_head, *attended, *pieces)


def updated_latent(velocity, latent, guidance, step_size, length, position):
    rows = velocity.shape[1]
    branch = lax.axis_index("cfg")
    scale = guidance[0]
    channels = velocity.shape[0] // 2
    own = lax.dynamic_slice_in_dim(velocity, branch * channels, channels, 0)
    outgoing = lax.dynamic_slice_in_dim(velocity, (1 - branch) * channels, channels, 0)
    other = lax.ppermute(outgoing.astype(BF16), "cfg", SWAP).astype(outgoing.dtype)
    cond = jnp.where(branch == 0, own, other)
    uncond = jnp.where(branch == 0, other, own)
    guided = uncond + scale * (cond - uncond)
    valid = position * rows + jnp.arange(rows, dtype=jnp.int32) < length
    current = latent[0].T
    updated = jnp.where(valid[None, :], current - step_size[0] * guided, current)
    return updated.T[None]


def after(value, *others):
    return lax.optimization_barrier((value, *others))[0]


def team_local(
    hidden, latent, modulation, w_qkv, w_out, q_gain, k_gain, w_head, lengths, guidance, step_size
):
    state = hidden[0, 0]
    modes = jnp.transpose(modulation, (1, 0, 2))
    rows, width = state.shape
    third = width // 4
    core = lax.axis_index("cfg")
    position = lax.axis_index("seq")
    place = lax.axis_index("req")
    parts = lax.axis_size("req")
    side, pair = place % 2, place // 2
    steps = parts // 2
    group = 2 * position + core
    up = [(i, (i - 2) % parts) for i in range(parts)]
    down = [(i, (i + 2) % parts) for i in range(parts)]
    beside = [(i, i ^ 1) for i in range(parts)]

    def along(piece):
        return lax.ppermute(piece, "req", up)

    def back(piece):
        return lax.ppermute(piece, "req", down)

    def across(piece):
        return lax.ppermute(piece, "req", beside)

    def ints(*values):
        return jnp.stack([jnp.asarray(value, jnp.int32) for value in values])

    columns = cut_columns(ints(group), w_qkv, w_out)
    length = lengths[0]
    places = ints(side, pair, steps, group, length - position * rows, length - (1 - position) * rows)
    gains = jnp.stack([q_gain, k_gain])[:, None]

    normed = normalise(places, state, modes)

    def step(mine, theirs, gates):
        now = after(mine[-1], *gates)
        mine.append(along(now))
        theirs.append(across(now))

    mine, theirs = [columns], []
    step(mine, theirs, [])
    cut, split = columns.shape[0] // 2, 3 * third
    low = theirs[0][cut:, :split]
    out_last = theirs[0][:, split:]
    gates = [mine[1], theirs[0], low, out_last, normed, gains]
    normed_y = lax.ppermute(after(normed, *gates), "seq", SWAP)
    normed_c = lax.ppermute(after(normed, *gates), "cfg", SWAP)
    step(mine, theirs, gates)
    gates = [mine[2], theirs[1]]
    step(mine, theirs, gates)
    out_last = back(after(out_last, *gates))
    normed_yc = lax.ppermute(normed_y, "cfg", SWAP)
    norms = [normed, normed_y, normed_c, normed_yc]
    early = [mine[0], theirs[0], mine[1], theirs[1]]
    packed = [pack(early, third)]
    packed_y = [lax.ppermute(packed[0], "seq", SWAP)]
    acc_qk, acc_v = first_part(norms, early)
    gates = [mine[3], theirs[2], out_last, packed_y[0], acc_v]
    upper = across(after(mine[3][:cut, :split], *gates))
    lower = back(after(low, *gates))
    late = [mine[2], theirs[2], mine[3], upper, lower]
    packed.append(pack([mine[2], theirs[2], mine[3], out_last], third))
    packed_y.append(lax.ppermute(packed[1], "seq", SWAP))
    packed_c = [lax.ppermute(part, "cfg", SWAP) for part in packed]
    packed_yc = [lax.ppermute(part, "cfg", SWAP) for part in packed_y]

    qk_full, sums = last_scores(norms, acc_qk, late)
    v_full = last_values(norms, acc_v, late)
    diagonal = [(i, 3 - i) for i in range(4)]
    all_sums = [
        sums,
        lax.ppermute(sums, "seq", SWAP),
        lax.ppermute(sums, "cfg", SWAP),
        lax.ppermute(sums, ("cfg", "seq"), diagonal),
    ]
    v_full = after(v_full, packed_y[1], *packed_c, packed_yc[0])
    heads = team_attention(places, qk_full, v_full, all_sums, gains)
    attended = [
        heads[0],
        lax.ppermute(heads[2], "cfg", SWAP),
        lax.ppermute(heads[1], "seq", SWAP),
        lax.ppermute(heads[3], ("cfg", "seq"), diagonal),
    ]
    quarters = [part[j] for j in range(2) for part in (packed, packed_c, packed_y, packed_yc)]
    velocity = project(places, state, modes, w_head.T, attended, quarters)
    return updated_latent(velocity, latent, guidance, step_size, length, position)


def by_team(mesh, arguments):
    hidden, w_qkv = arguments[0], arguments[3]
    sizes = mesh.shape
    width = hidden.shape[3]
    depth = w_qkv.shape[0] // sizes["req"]
    return (
        sizes["cfg"] == 2
        and sizes["seq"] == 2
        and sizes["req"] == 8
        and width % (4 * DH) == 0
        and 8 * depth == width
        and depth % 32 == 0
        and hidden.shape[2] // sizes["seq"] % 16 == 0
    )


def solution(mesh):
    def whole(*arguments):
        body = team_local if by_team(mesh, arguments) else ring_local
        return jax.shard_map(
            body,
            mesh=mesh,
            in_specs=(
                P("cfg", "req", "seq", None),
                P("req", "seq", "cfg"),
                P("req", None, None),
                P("req", None),
                P("req", None),
                P(),
                P(),
                P(),
                P("req"),
                P("req"),
                P("req"),
            ),
            out_specs=P("req", "seq", "cfg"),
            check_vma=False,
        )(*arguments)

    return whole
```

```python
import functools

import jax
import jax.numpy as jnp
from jax import lax
from jax.experimental import pallas as pl
from jax.experimental.pallas import tpu as pltpu
from jax.sharding import PartitionSpec as P

DH = 128
SWAP = [(0, 1), (1, 0)]
SMEM = pl.BlockSpec(memory_space=pltpu.SMEM)
ANY = pl.BlockSpec(memory_space=pl.ANY)
BF16 = jnp.bfloat16
F32 = jnp.float32


def params():
    return pltpu.CompilerParams(vmem_limit_bytes=60 * 2**20)


def cost(flops, moved, exps=0):
    return pl.CostEstimate(flops=int(flops), bytes_accessed=int(moved), transcendentals=int(exps))


def shape_of(*dims, dtype=BF16):
    return jax.ShapeDtypeStruct(dims, dtype)


def times(left, right):
    return jnp.dot(left, right, preferred_element_type=F32)


def times_turned(left, right):
    return lax.dot_general(left, right, (((1,), (1,)), ((), ())), preferred_element_type=F32)


def passed_along(value, axis, steps):
    count = lax.axis_size(axis)
    pairs = [(source, (source + steps) % count) for source in range(count)]
    return lax.ppermute(value, axis, pairs)


def from_partner(value, axis, apart):
    mask = 2**apart
    pairs = [(source, source ^ mask) for source in range(lax.axis_size(axis))]
    return lax.ppermute(value, axis, pairs)


def layer_norm(values):
    centered = values - jnp.mean(values, axis=-1, keepdims=True)
    return centered / jnp.sqrt(jnp.mean(centered * centered, axis=-1, keepdims=True) + 1e-06)


def rms_gain(values, gain):
    return values / jnp.sqrt(jnp.mean(values * values, axis=-1, keepdims=True) + 1e-06) * gain


def add_rows(left, piece):
    return jnp.dot(left, piece, preferred_element_type=jnp.float32)


def attend(state, query, stacked, start, length):
    top, total, weighted = state
    keys = stacked[0]
    values = stacked[1]
    count = keys.shape[0]
    scores = jnp.einsum("qhd,khd->qhk", query, keys, preferred_element_type=jnp.float32) / jnp.sqrt(
        jnp.float32(query.shape[2])
    )
    valid = start + jnp.arange(count, dtype=jnp.int32) < length
    scores = jnp.where(valid[None, None, :], scores, jnp.float32(-1e30))
    new_top = jnp.maximum(top, jnp.max(scores, axis=-1))
    factor = jnp.exp(top - new_top)
    probs = jnp.where(valid[None, None, :], jnp.exp(scores - new_top[:, :, None]), jnp.float32(0.0))
    total = total * factor + jnp.sum(probs, axis=-1)
    weighted = weighted * factor[:, :, None] + jnp.einsum(
        "qhk,khd->qhd", probs.astype(jnp.bfloat16), values, preferred_element_type=jnp.float32
    )
    return (new_top, total, weighted)


def ring_local(
    hidden, latent, modulation, w_qkv, w_out, q_gain, k_gain, w_head, lengths, guidance, step_size
):
    state = hidden[0, 0]
    modes = modulation[0]
    length = lengths[0]
    rows = state.shape[0]
    width = state.shape[1]
    heads = q_gain.shape[0] // DH
    wide = state.astype(jnp.float32)
    normed = (layer_norm(wide) * (1.0 + modes[1]) + modes[0]).astype(jnp.bfloat16)
    qkv = add_rows(normed, lax.all_gather(w_qkv, "req", axis=0, tiled=True))
    query = rms_gain(qkv[:, :width], q_gain).astype(jnp.bfloat16).reshape(rows, heads, DH)
    keys = rms_gain(qkv[:, width : 2 * width], k_gain).astype(jnp.bfloat16).reshape(rows, heads, DH)
    values = qkv[:, 2 * width :].astype(jnp.bfloat16).reshape(rows, heads, DH)
    stacked = jnp.stack([keys, values])
    position = lax.axis_index("seq")
    members = lax.axis_size("seq")
    start_state = (
        jnp.full((rows, heads), -1e30, jnp.float32),
        jnp.zeros((rows, heads), jnp.float32),
        jnp.zeros((rows, heads, DH), jnp.float32),
    )
    first = attend(start_state, query, stacked, position * rows, length)

    def cycle_step(turn, carry):
        moving, inner = carry
        moving = passed_along(moving, "seq", 1)
        source = (position - turn) % members
        return (moving, attend(inner, query, moving, source * rows, length))

    moved, result = lax.fori_loop(1, members, cycle_step, (stacked, first))
    top, total, weighted = result
    attended = (weighted / total[:, :, None]).reshape(rows, width).astype(jnp.bfloat16)
    projected = add_rows(attended, lax.all_gather(w_out, "req", axis=0, tiled=True))
    block_out = (wide + modes[2] * projected).astype(jnp.bfloat16)
    head_in = (layer_norm(block_out.astype(jnp.float32)) * (1.0 + modes[4]) + modes[3]).astype(
        jnp.bfloat16
    )
    velocity = jnp.dot(head_in, w_head, preferred_element_type=jnp.float32)
    branch = lax.axis_index("cfg")
    scale = guidance[0]
    channels = velocity.shape[1] // 2
    own = lax.dynamic_slice_in_dim(velocity, branch * channels, channels, 1)
    outgoing = lax.dynamic_slice_in_dim(velocity, (1 - branch) * channels, channels, 1)
    other = from_partner(outgoing.astype(jnp.bfloat16), "cfg", 0).astype(outgoing.dtype)
    cond = jnp.where(branch == 0, own, other)
    uncond = jnp.where(branch == 0, other, own)
    guided = uncond + scale * (cond - uncond)
    valid = position * rows + jnp.arange(rows, dtype=jnp.int32) < length
    current = latent[0]
    updated = jnp.where(valid[:, None], current - step_size[0] * guided, current)
    return updated[None]


def load_all(pairs, sem):
    copies = [pltpu.make_async_copy(source, target, sem.at[j]) for j, (source, target) in enumerate(pairs)]
    for copy in copies:
        copy.start()
    return copies


def entry_kernel(where_ref, qkv_ref, w_out_ref, state_ref, modes_ref, cut_ref, norm_ref, *scratch):
    cut_buf, state_in, modes_in, full_ref, norm_buf, sem = scratch
    side, pair, steps, group = (where_ref[j] for j in range(4))
    third = cut_ref.shape[1] // 4
    width = 4 * third
    pairs = []
    for j in range(4):
        source_ref, base = (qkv_ref, j * width) if j < 3 else (w_out_ref, 0)
        source = source_ref.at[:, pl.ds(pl.multiple_of(base + group * third, third), third)]
        pairs.append((source, cut_buf.at[:, j * third : (j + 1) * third]))
    loads = load_all([(state_ref, state_in), (modes_ref, modes_in)] + pairs, sem)
    for copy in loads[:2]:
        copy.wait()
    full_ref[...] = layer_norm(state_in[...].astype(F32)) * (1.0 + modes_in[1]) + modes_in[0]
    for copy in loads[2:]:
        copy.wait()
    store = load_all([(cut_buf, cut_ref)], sem)
    count = 4
    for k in range(count):
        owner = lax.rem(pair + k, steps)
        part = full_ref[:, pl.ds(pl.multiple_of(owner * third, third), third)]
        part = jnp.where(side == 0, part, pltpu.roll(part, third // 2, 1))
        norm_buf[:, k * third : (k + 1) * third] = part.astype(BF16)
    store[0].wait()
    for copy in load_all([(norm_buf, norm_ref)], sem):
        copy.wait()


def entry(where, w_qkv, w_out, state, modes):
    return pl.pallas_call(
        entry_kernel,
        out_shape=[shape_of(*w_out.shape), shape_of(*state.shape)],
        in_specs=[SMEM, ANY, ANY, ANY, ANY],
        out_specs=[ANY, ANY],
        scratch_shapes=[
            pltpu.VMEM(w_out.shape, BF16),
            pltpu.VMEM(state.shape, BF16),
            pltpu.VMEM(modes.shape, F32),
            pltpu.VMEM(state.shape, F32),
            pltpu.VMEM(state.shape, BF16),
            pltpu.SemaphoreType.DMA((6,)),
        ],
        compiler_params=params(),
        cost_estimate=cost(4e9, 1e6),
    )(where, w_qkv, w_out, state, modes)


def pack_kernel(count, *refs):
    pieces, packed_ref, held_ref, sem = refs[:count], refs[count], refs[count + 1], refs[count + 2]
    depth = held_ref.shape[0] // count
    columns = held_ref.shape[1]
    pairs = []
    for k, piece in enumerate(pieces):
        pairs.append((piece.at[:, piece.shape[1] - columns :], held_ref.at[k * depth : (k + 1) * depth]))
    for copy in load_all(pairs, sem):
        copy.wait()
    for copy in load_all([(held_ref, packed_ref)], sem):
        copy.wait()


def pack(pieces, columns):
    depth = pieces[0].shape[0]
    full = shape_of(depth * len(pieces), columns)
    return pl.pallas_call(
        functools.partial(pack_kernel, len(pieces)),
        out_shape=full,
        in_specs=[ANY] * len(pieces),
        out_specs=ANY,
        scratch_shapes=[pltpu.VMEM(full.shape, BF16), pltpu.SemaphoreType.DMA((len(pieces),))],
        compiler_params=params(),
        cost_estimate=cost(3e9, 1e6),
    )(*pieces)


def rows_of(piece_refs, held_ref, start=0):
    found, at = [], 0
    for piece in piece_refs:
        rows = piece.shape[0]
        source = piece.at[:, start : start + held_ref.shape[1]]
        found.append((source, held_ref.at[at : at + rows]))
        at += rows
    return found


def first_kernel(count, *refs):
    norms, pieces = refs[:4], refs[4 : 4 + count]
    qk_ref, v_ref = refs[4 + count : 6 + count]
    left_ref, held_ref, qk_out, v_out, sem, out_sem = refs[6 + count :]
    deep, columns = held_ref.shape
    split = 2 * columns // 3
    loads = load_all(
        rows_of(pieces, held_ref) + [(norms[b].at[:, :deep], left_ref.at[b]) for b in range(4)], sem
    )
    for copy in loads:
        copy.wait()
    stores = []
    for block in range(4):
        qk_out[block] = times(left_ref[block], held_ref[:, :split]).astype(BF16)
        v_out[block] = times(left_ref[block], held_ref[:, split:]).astype(BF16)
        for j, (source, target) in enumerate(((qk_out, qk_ref), (v_out, v_ref))):
            copy = pltpu.make_async_copy(source.at[block], target.at[block], out_sem.at[2 * block + j])
            copy.start()
            stores.append(copy)
    for copy in stores:
        copy.wait()


def first_part(norms, pieces):
    rows = norms[0].shape[0]
    columns = 3 * norms[0].shape[1] // 4
    deep = sum(piece.shape[0] for piece in pieces)
    qk = shape_of(4, rows, 2 * columns // 3)
    v = shape_of(4, rows, columns // 3)
    return pl.pallas_call(
        functools.partial(first_kernel, len(pieces)),
        out_shape=[qk, v],
        in_specs=[ANY] * (4 + len(pieces)),
        out_specs=[ANY] * 2,
        scratch_shapes=[
            pltpu.VMEM((4, rows, deep), BF16),
            pltpu.VMEM((deep, columns), BF16),
            pltpu.VMEM(qk.shape, BF16),
            pltpu.VMEM(v.shape, BF16),
            pltpu.SemaphoreType.DMA((4 + len(pieces),)),
            pltpu.SemaphoreType.DMA((8,)),
        ],
        compiler_params=params(),
        cost_estimate=cost(6e9, 1e6),
    )(*norms, *pieces)


def scores_kernel(count, where_ref, *refs):
    norms, acc_ref, gains_ref, pieces = refs[:4], refs[4], refs[5], refs[6 : 6 + count]
    out_ref, sums_ref, left_ref, held_ref, acc_in, gains_in, out_buf, sums_buf, sem, out_sem = refs[6 + count :]
    deep = held_ref.shape[0]
    third = out_ref.shape[2] // 2
    width = norms[0].shape[1]
    loads = load_all(
        rows_of(pieces, held_ref)
        + [(gains_ref, gains_in)]
        + [(norms[b].at[:, width - deep :], left_ref.at[b]) for b in range(4)]
        + [(acc_ref.at[b], acc_in.at[b]) for b in range(4)],
        sem,
    )
    mine = pl.ds(pl.multiple_of(where_ref[3] * third, third), third)
    row = lax.broadcasted_iota(jnp.int32, (8, 4 * DH), 0)
    lane = lax.broadcasted_iota(jnp.int32, (8, 4 * DH), 1)
    pick = (row == lane // (2 * DH)).astype(BF16)
    for copy in loads[: count + 1]:
        copy.wait()
    gains = [gains_in[0, :, mine] * (1.4426950408889634 / DH**0.5), gains_in[1, :, mine]]
    stores = []
    for block in range(4):
        loads[count + 1 + block].wait()
        product = times(left_ref[block], held_ref[...])
        loads[count + 5 + block].wait()
        squares = []
        for j in range(2):
            square = 0.0
            for h in range(third // DH):
                at = slice(j * third + h * DH, j * third + (h + 1) * DH)
                part = acc_in[block, :, at].astype(F32) + product[:, at]
                square += part * part
                out_buf[block, :, at] = (part * gains[j][:, h * DH : (h + 1) * DH]).astype(BF16)
            high = square.astype(BF16)
            squares += [high, (square - high.astype(F32)).astype(BF16)]
        stores.append(pltpu.make_async_copy(out_buf.at[block], out_ref.at[block], out_sem.at[block]))
        stores[-1].start()
        sums_buf[block] = times_turned(pick, jnp.concatenate(squares, axis=1))
    stores.append(pltpu.make_async_copy(sums_buf, sums_ref, out_sem.at[4]))
    stores[-1].start()
    for copy in stores:
        copy.wait()


def last_scores(where, norms, acc, gains, pieces):
    rows = norms[0].shape[0]
    columns = acc.shape[2]
    deep = sum(piece.shape[0] for piece in pieces)
    return pl.pallas_call(
        functools.partial(scores_kernel, len(pieces)),
        out_shape=[shape_of(4, rows, columns), shape_of(4, 8, rows, dtype=F32)],
        in_specs=[SMEM] + [ANY] * (6 + len(pieces)),
        out_specs=[ANY, ANY],
        scratch_shapes=[
            pltpu.VMEM((4, rows, deep), BF16),
            pltpu.VMEM((deep, columns), BF16),
            pltpu.VMEM(acc.shape, BF16),
            pltpu.VMEM(gains.shape, F32),
            pltpu.VMEM(acc.shape, BF16),
            pltpu.VMEM((4, 8, rows), F32),
            pltpu.SemaphoreType.DMA((9 + len(pieces),)),
            pltpu.SemaphoreType.DMA((5,)),
        ],
        compiler_params=params(),
        cost_estimate=cost(6e9, 1e6),
    )(where, *norms, acc, gains, *pieces)


def values_kernel(count, *refs):
    norms, acc_ref, pieces = refs[:4], refs[4], refs[5 : 5 + count]
    out_ref, left_ref, held_ref, acc_in, out_buf, sem = refs[5 + count :]
    deep, columns = held_ref.shape
    width = norms[0].shape[1]
    loads = load_all(
        rows_of(pieces, held_ref, 2 * columns)
        + [(norms[b].at[:, width - deep :], left_ref.at[b]) for b in range(4)]
        + [(acc_ref.at[b], acc_in.at[b]) for b in range(4)],
        sem,
    )
    for copy in loads[:count]:
        copy.wait()
    stores = []
    for block in range(4):
        loads[count + block].wait()
        product = times(left_ref[block], held_ref[...])
        loads[count + 4 + block].wait()
        out_buf[block] = (acc_in[block].astype(F32) + product).astype(BF16)
        stores.append(pltpu.make_async_copy(out_buf.at[block], out_ref.at[block], sem.at[block]))
        stores[-1].start()
    for copy in stores:
        copy.wait()


def last_values(norms, acc, pieces):
    rows = norms[0].shape[0]
    columns = acc.shape[2]
    deep = sum(piece.shape[0] for piece in pieces)
    return pl.pallas_call(
        functools.partial(values_kernel, len(pieces)),
        out_shape=shape_of(4, rows, columns),
        in_specs=[ANY] * 5 + [ANY] * len(pieces),
        out_specs=ANY,
        scratch_shapes=[
            pltpu.VMEM((4, rows, deep), BF16),
            pltpu.VMEM((deep, columns), BF16),
            pltpu.VMEM(acc.shape, BF16),
            pltpu.VMEM(acc.shape, BF16),
            pltpu.SemaphoreType.DMA((8 + len(pieces),)),
        ],
        compiler_params=params(),
        cost_estimate=cost(4e9, 1e6),
    )(*norms, acc, *pieces)


def heads_kernel(where_ref, qk_ref, v_ref, s0_ref, s1_ref, s2_ref, s3_ref, *refs):
    outs = refs[:4]
    qk_in, v_in, sums_in, out_buf, sem, out_sem = refs[4:]
    rows = qk_ref.shape[1]
    third = qk_ref.shape[2] // 2
    count = third // DH
    width = 4 * third
    sum_refs = (s0_ref, s1_ref, s2_ref, s3_ref)
    loads = load_all(
        [(sum_refs[j], sums_in.at[j]) for j in range(4)]
        + [(qk_ref.at[b], qk_in.at[b]) for b in range(4)]
        + [
            (v_ref.at[b, :, h * DH : (h + 1) * DH], v_in.at[h, b // 2, b % 2 * rows : (b % 2 + 1) * rows, :DH])
            for b in range(4)
            for h in range(count)
        ],
        sem,
    )
    for h in range(count):
        for b in range(2):
            v_in[h, b, :, DH:] = jnp.ones((2 * rows, DH), BF16)
    row = lax.broadcasted_iota(jnp.int32, (24, DH), 0)
    pick = (row % 8 == 0).astype(BF16)
    place = lax.broadcasted_iota(jnp.int32, (1, rows), 1)
    masks = [place < where_ref[4 + j] for j in range(2)]
    for copy in loads[:4]:
        copy.wait()
    scale_q, scale_k = [], []
    for block in range(4):
        sums = sums_in[0, block] + sums_in[1, block ^ 1] + sums_in[2, block ^ 2] + sums_in[3, block ^ 3]
        inverse = lax.rsqrt(sums * (1.0 / width) + 1e-06)
        high = inverse.astype(BF16).astype(F32)
        middle = (inverse - high).astype(BF16).astype(F32)
        stacked = jnp.concatenate([high, middle, inverse - high - middle], axis=0).astype(BF16)
        turned = lax.dot_general(stacked, pick, (((0,), (0,)), ((), ())), preferred_element_type=F32)
        scale_q.append(turned[:, :1])
        scale_k.append(inverse[1:2, :])
    for copy in loads[4:8]:
        copy.wait()
    items = [(block, h) for block in (1, 3, 2, 0) for h in range(count)]

    def scores_of(block, h):
        first = block - block % 2
        query = qk_in[block, :, h * DH : (h + 1) * DH]
        found = []
        for j in range(2):
            keys = qk_in[first + j, :, third + h * DH : third + (h + 1) * DH]
            part = times_turned(query, keys) * scale_k[first + j]
            found.append(jnp.where(masks[j], part, -1e30))
        return found

    stores = []
    ahead = scores_of(*items[0])
    for at, (block, h) in enumerate(items):
        scores = ahead
        if at + 1 < len(items):
            ahead = scores_of(*items[at + 1])
        if at == 0:
            for copy in loads[8:]:
                copy.wait()
        top = jnp.maximum(
            jnp.max(scores[0], axis=-1, keepdims=True), jnp.max(scores[1], axis=-1, keepdims=True)
        )
        weighted = 0.0
        for j in range(2):
            probs = jnp.exp2((scores[j] - top) * scale_q[block]).astype(BF16)
            weighted += times(probs, v_in[h, block // 2, j * rows : (j + 1) * rows, :])
        out_buf[block, :, h * DH : (h + 1) * DH] = (weighted[:, :DH] / weighted[:, DH:]).astype(BF16)
        if h == count - 1:
            stores.append(pltpu.make_async_copy(out_buf.at[block], outs[block], out_sem.at[block]))
            stores[-1].start()
    for copy in stores:
        copy.wait()


def team_attention(where, qk, v, sums):
    rows = qk.shape[1]
    third = qk.shape[2] // 2
    return pl.pallas_call(
        heads_kernel,
        out_shape=[shape_of(rows, third)] * 4,
        in_specs=[SMEM] + [ANY] * 6,
        out_specs=[ANY] * 4,
        scratch_shapes=[
            pltpu.VMEM(qk.shape, BF16),
            pltpu.VMEM((third // DH, 2, 2 * rows, 2 * DH), BF16),
            pltpu.VMEM((4, 4, 8, rows), F32),
            pltpu.VMEM((4, rows, third), BF16),
            pltpu.SemaphoreType.DMA((8 + 4 * third // DH,)),
            pltpu.SemaphoreType.DMA((4,)),
        ],
        compiler_params=params(),
        cost_estimate=cost(1.1e10, 1e6),
    )(where, qk, v, *sums)


def out_kernel(where_ref, state_ref, modes_ref, head_ref, *refs):
    attended, pieces = refs[:4], refs[4:12]
    own_ref, sent_ref = refs[12:14]
    att_in, group_ref, held_ref, state_in, modes_in, head_in_ref, own_buf, sent_buf, sem = refs[14:]
    side, pair, steps, own = (where_ref[j] for j in range(4))
    third = attended[0].shape[1]
    half = pieces[0].shape[0]

    def window(j):
        return pl.ds(pl.multiple_of(j * third, third), third)

    loads = load_all(
        [(attended[j], att_in.at[j]) for j in range(4)]
        + [(pieces[j], held_ref.at[:half, window(own ^ j)]) for j in range(4)]
        + [(pieces[4 + j], held_ref.at[half:, window(own ^ j)]) for j in range(4)]
        + [(state_ref, state_in), (modes_ref, modes_in), (head_ref, head_in_ref)],
        sem,
    )
    for j in range(4):
        loads[j].wait()
        part = att_in[j].astype(F32)
        part = jnp.where(side == 0, part, pltpu.roll(part, third // 2, 1)).astype(BF16)
        group_ref[:, window(lax.rem((own ^ j) + steps - pair, steps))] = part
    for copy in loads[4:8]:
        copy.wait()
    total = times(group_ref[:, :half], held_ref[:half, :])
    for copy in loads[8:]:
        copy.wait()
    total += times(group_ref[:, half:], held_ref[half:, :])
    block_out = (state_in[...].astype(F32) + modes_in[2] * total).astype(BF16)
    head_in = layer_norm(block_out.astype(F32)) * (1.0 + modes_in[4]) + modes_in[3]
    velocity = times_turned(head_in_ref[...], head_in.astype(BF16))
    channels = own_buf.shape[0]
    core = lax.rem(own, 2)
    own_buf[...] = jnp.where(core == 0, velocity[:channels], velocity[channels:])
    sent_buf[...] = jnp.where(core == 0, velocity[channels:], velocity[:channels]).astype(BF16)
    for copy in load_all([(own_buf, own_ref), (sent_buf, sent_ref)], sem):
        copy.wait()


def project(where, state, modes, w_head, attended, pieces):
    rows, width = state.shape
    third = width // 4
    channels = w_head.shape[0] // 2
    return pl.pallas_call(
        out_kernel,
        out_shape=[shape_of(channels, rows, dtype=F32), shape_of(channels, rows)],
        in_specs=[SMEM] + [ANY] * 15,
        out_specs=[ANY, ANY],
        scratch_shapes=[
            pltpu.VMEM((4, rows, third), BF16),
            pltpu.VMEM((rows, width), BF16),
            pltpu.VMEM((width, width), BF16),
            pltpu.VMEM(state.shape, BF16),
            pltpu.VMEM(modes.shape, F32),
            pltpu.VMEM(w_head.shape, BF16),
            pltpu.VMEM((channels, rows), F32),
            pltpu.VMEM((channels, rows), BF16),
            pltpu.SemaphoreType.DMA((15,)),
        ],
        compiler_params=params(),
        cost_estimate=cost(8e9, 1e6),
    )(where, state, modes, w_head, *attended, *pieces)


def updated_latent(own, outgoing, latent, guidance, step_size, length, position):
    rows = own.shape[1]
    branch = lax.axis_index("cfg")
    scale = guidance[0]
    other = lax.ppermute(outgoing, "cfg", SWAP).astype(own.dtype)
    cond = jnp.where(branch == 0, own, other)
    uncond = jnp.where(branch == 0, other, own)
    guided = uncond + scale * (cond - uncond)
    valid = position * rows + jnp.arange(rows, dtype=jnp.int32) < length
    current = latent[0].T
    updated = jnp.where(valid[None, :], current - step_size[0] * guided, current)
    return updated.T[None]


def after(value, *others):
    return lax.optimization_barrier((value, *others))[0]


def team_local(
    hidden, latent, modulation, w_qkv, w_out, q_gain, k_gain, w_head, lengths, guidance, step_size
):
    state = hidden[0, 0]
    modes = jnp.transpose(modulation, (1, 0, 2))
    rows, width = state.shape
    third = width // 4
    core = lax.axis_index("cfg")
    position = lax.axis_index("seq")
    place = lax.axis_index("req")
    parts = lax.axis_size("req")
    side, pair = place % 2, place // 2
    steps = parts // 2
    group = 2 * position + core
    up = [(i, (i - 2) % parts) for i in range(parts)]
    down = [(i, (i + 2) % parts) for i in range(parts)]
    beside = [(i, i ^ 1) for i in range(parts)]

    def along(piece):
        return lax.ppermute(piece, "req", up)

    def back(piece):
        return lax.ppermute(piece, "req", down)

    def across(piece):
        return lax.ppermute(piece, "req", beside)

    def ints(*values):
        return jnp.stack([jnp.asarray(value, jnp.int32) for value in values])

    length = lengths[0]
    places = ints(side, pair, steps, group, length - position * rows, length - (1 - position) * rows)
    gains = jnp.stack([q_gain, k_gain])[:, None]

    columns, normed = entry(places, w_qkv, w_out, state, modes)
    normed_y = lax.ppermute(normed, "seq", SWAP)
    normed_c = lax.ppermute(normed, "cfg", SWAP)

    def step(mine, theirs, gates):
        now = after(mine[-1], *gates)
        mine.append(along(now))
        theirs.append(across(now))

    mine, theirs = [columns], []
    step(mine, theirs, [])
    cut, split = columns.shape[0] // 2, 3 * third
    low = theirs[0][cut:, :split]
    out_last = theirs[0][:, split:]
    gates = [mine[1], theirs[0], low, out_last, gains]
    step(mine, theirs, gates)
    gates = [mine[2], theirs[1]]
    step(mine, theirs, gates)
    out_last = back(after(out_last, *gates))
    normed_yc = lax.ppermute(normed_y, "cfg", SWAP)
    norms = [normed, normed_y, normed_c, normed_yc]
    early = [mine[0], theirs[0], mine[1], theirs[1]]
    packed = [pack(early, third)]
    packed_y = [lax.ppermute(packed[0], "seq", SWAP)]
    acc_qk, acc_v = first_part(norms, early)
    gates = [mine[3], theirs[2], out_last, packed_y[0], acc_v]
    upper = across(after(mine[3][:cut, :split], *gates))
    lower = back(after(low, *gates))
    late = [mine[2], theirs[2], mine[3], upper, lower]
    packed.append(pack([mine[2], theirs[2], mine[3], out_last], third))
    packed_y.append(lax.ppermute(packed[1], "seq", SWAP))
    packed_c = [lax.ppermute(part, "cfg", SWAP) for part in packed]
    packed_yc = [lax.ppermute(part, "cfg", SWAP) for part in packed_y]

    qk_full, sums = last_scores(places, norms, acc_qk, gains, late)
    v_full = last_values(norms, acc_v, late)
    diagonal = [(i, 3 - i) for i in range(4)]
    all_sums = [
        sums,
        lax.ppermute(sums, "seq", SWAP),
        lax.ppermute(sums, "cfg", SWAP),
        lax.ppermute(sums, ("cfg", "seq"), diagonal),
    ]
    v_full = after(v_full, packed_y[1], *packed_c, packed_yc[0])
    heads = team_attention(places, qk_full, v_full, all_sums)
    attended = [
        heads[0],
        lax.ppermute(heads[2], "cfg", SWAP),
        lax.ppermute(heads[1], "seq", SWAP),
        lax.ppermute(heads[3], ("cfg", "seq"), diagonal),
    ]
    quarters = [part[j] for j in range(2) for part in (packed, packed_c, packed_y, packed_yc)]
    own, outgoing = project(places, state, modes, w_head.T, attended, quarters)
    return updated_latent(own, outgoing, latent, guidance, step_size, length, position)


def by_team(mesh, arguments):
    hidden, w_qkv = arguments[0], arguments[3]
    sizes = mesh.shape
    width = hidden.shape[3]
    depth = w_qkv.shape[0] // sizes["req"]
    return (
        sizes["cfg"] == 2
        and sizes["seq"] == 2
        and sizes["req"] == 8
        and width % (4 * DH) == 0
        and 8 * depth == width
        and depth % 32 == 0
        and hidden.shape[2] // sizes["seq"] % 16 == 0
    )


def solution(mesh):
    def whole(*arguments):
        body = team_local if by_team(mesh, arguments) else ring_local
        return jax.shard_map(
            body,
            mesh=mesh,
            in_specs=(
                P("cfg", "req", "seq", None),
                P("req", "seq", "cfg"),
                P("req", None, None),
                P("req", None),
                P("req", None),
                P(),
                P(),
                P(),
                P("req"),
                P("req"),
                P("req"),
            ),
            out_specs=P("req", "seq", "cfg"),
            check_vma=False,
        )(*arguments)

    return whole
```

```python
import functools

import jax
import jax.numpy as jnp
from jax import lax
from jax.experimental import pallas as pl
from jax.experimental.pallas import tpu as pltpu
from jax.sharding import PartitionSpec as P

DH = 128
SWAP = [(0, 1), (1, 0)]
SMEM = pl.BlockSpec(memory_space=pltpu.SMEM)
ANY = pl.BlockSpec(memory_space=pl.ANY)
BF16 = jnp.bfloat16
F32 = jnp.float32


def params():
    return pltpu.CompilerParams(vmem_limit_bytes=60 * 2**20)


def cost(flops, moved, exps=0):
    return pl.CostEstimate(flops=int(flops), bytes_accessed=int(moved), transcendentals=int(exps))


def shape_of(*dims, dtype=BF16):
    return jax.ShapeDtypeStruct(dims, dtype)


def times(left, right):
    return jnp.dot(left, right, preferred_element_type=F32)


def times_turned(left, right):
    return lax.dot_general(left, right, (((1,), (1,)), ((), ())), preferred_element_type=F32)


def passed_along(value, axis, steps):
    count = lax.axis_size(axis)
    pairs = [(source, (source + steps) % count) for source in range(count)]
    return lax.ppermute(value, axis, pairs)


def from_partner(value, axis, apart):
    mask = 2**apart
    pairs = [(source, source ^ mask) for source in range(lax.axis_size(axis))]
    return lax.ppermute(value, axis, pairs)


def layer_norm(values):
    centered = values - jnp.mean(values, axis=-1, keepdims=True)
    return centered / jnp.sqrt(jnp.mean(centered * centered, axis=-1, keepdims=True) + 1e-06)


def rms_gain(values, gain):
    return values / jnp.sqrt(jnp.mean(values * values, axis=-1, keepdims=True) + 1e-06) * gain


def add_rows(left, piece):
    return jnp.dot(left, piece, preferred_element_type=jnp.float32)


def attend(state, query, stacked, start, length):
    top, total, weighted = state
    keys = stacked[0]
    values = stacked[1]
    count = keys.shape[0]
    scores = jnp.einsum("qhd,khd->qhk", query, keys, preferred_element_type=jnp.float32) / jnp.sqrt(
        jnp.float32(query.shape[2])
    )
    valid = start + jnp.arange(count, dtype=jnp.int32) < length
    scores = jnp.where(valid[None, None, :], scores, jnp.float32(-1e30))
    new_top = jnp.maximum(top, jnp.max(scores, axis=-1))
    factor = jnp.exp(top - new_top)
    probs = jnp.where(valid[None, None, :], jnp.exp(scores - new_top[:, :, None]), jnp.float32(0.0))
    total = total * factor + jnp.sum(probs, axis=-1)
    weighted = weighted * factor[:, :, None] + jnp.einsum(
        "qhk,khd->qhd", probs.astype(jnp.bfloat16), values, preferred_element_type=jnp.float32
    )
    return (new_top, total, weighted)


def ring_local(
    hidden, latent, modulation, w_qkv, w_out, q_gain, k_gain, w_head, lengths, guidance, step_size
):
    state = hidden[0, 0]
    modes = modulation[0]
    length = lengths[0]
    rows = state.shape[0]
    width = state.shape[1]
    heads = q_gain.shape[0] // DH
    wide = state.astype(jnp.float32)
    normed = (layer_norm(wide) * (1.0 + modes[1]) + modes[0]).astype(jnp.bfloat16)
    qkv = add_rows(normed, lax.all_gather(w_qkv, "req", axis=0, tiled=True))
    query = rms_gain(qkv[:, :width], q_gain).astype(jnp.bfloat16).reshape(rows, heads, DH)
    keys = rms_gain(qkv[:, width : 2 * width], k_gain).astype(jnp.bfloat16).reshape(rows, heads, DH)
    values = qkv[:, 2 * width :].astype(jnp.bfloat16).reshape(rows, heads, DH)
    stacked = jnp.stack([keys, values])
    position = lax.axis_index("seq")
    members = lax.axis_size("seq")
    start_state = (
        jnp.full((rows, heads), -1e30, jnp.float32),
        jnp.zeros((rows, heads), jnp.float32),
        jnp.zeros((rows, heads, DH), jnp.float32),
    )
    first = attend(start_state, query, stacked, position * rows, length)

    def cycle_step(turn, carry):
        moving, inner = carry
        moving = passed_along(moving, "seq", 1)
        source = (position - turn) % members
        return (moving, attend(inner, query, moving, source * rows, length))

    moved, result = lax.fori_loop(1, members, cycle_step, (stacked, first))
    top, total, weighted = result
    attended = (weighted / total[:, :, None]).reshape(rows, width).astype(jnp.bfloat16)
    projected = add_rows(attended, lax.all_gather(w_out, "req", axis=0, tiled=True))
    block_out = (wide + modes[2] * projected).astype(jnp.bfloat16)
    head_in = (layer_norm(block_out.astype(jnp.float32)) * (1.0 + modes[4]) + modes[3]).astype(
        jnp.bfloat16
    )
    velocity = jnp.dot(head_in, w_head, preferred_element_type=jnp.float32)
    branch = lax.axis_index("cfg")
    scale = guidance[0]
    channels = velocity.shape[1] // 2
    own = lax.dynamic_slice_in_dim(velocity, branch * channels, channels, 1)
    outgoing = lax.dynamic_slice_in_dim(velocity, (1 - branch) * channels, channels, 1)
    other = from_partner(outgoing.astype(jnp.bfloat16), "cfg", 0).astype(outgoing.dtype)
    cond = jnp.where(branch == 0, own, other)
    uncond = jnp.where(branch == 0, other, own)
    guided = uncond + scale * (cond - uncond)
    valid = position * rows + jnp.arange(rows, dtype=jnp.int32) < length
    current = latent[0]
    updated = jnp.where(valid[:, None], current - step_size[0] * guided, current)
    return updated[None]


def load_all(pairs, sem):
    copies = [pltpu.make_async_copy(source, target, sem.at[j]) for j, (source, target) in enumerate(pairs)]
    for copy in copies:
        copy.start()
    return copies


def places():
    place = lax.axis_index("req")
    group = 2 * lax.axis_index("seq") + lax.axis_index("cfg")
    return lax.rem(place, 2), place // 2, lax.axis_size("req") // 2, group


def window(j, size):
    return pl.ds(pl.multiple_of(j * size, size), size)


def scaled_norm(values, shift, scale):
    centered = values - jnp.mean(values, axis=-1, keepdims=True)
    inverse = lax.rsqrt(jnp.mean(centered * centered, axis=-1, keepdims=True) + 1e-06)
    return centered * inverse * (1.0 + scale) + shift


def entry_kernel(qkv_ref, w_out_ref, state_ref, modes_ref, cut_ref, norm_ref, *scratch):
    cut_buf, state_in, modes_in, full_ref, norm_buf, sem, out_sem = scratch
    side, pair, steps, group = places()
    third = cut_ref.shape[1] // 4
    loads = [(state_ref, state_in), (modes_ref, modes_in)]
    for j in range(3):
        loads.append((qkv_ref.at[:, window(4 * j + group, third)], cut_buf.at[:, j * third : (j + 1) * third]))
    loads.append((w_out_ref.at[:, window(group, third)], cut_buf.at[:, 3 * third :]))
    loads = load_all(loads, sem)
    for copy in loads[:2]:
        copy.wait()
    full_ref[...] = scaled_norm(state_in[...].astype(F32), modes_in[0], modes_in[1])
    for copy in loads[2:]:
        copy.wait()
    stores = [pltpu.make_async_copy(cut_buf, cut_ref, out_sem.at[0])]
    stores[0].start()
    count = 4
    for k in range(count):
        part = full_ref[:, window(lax.rem(pair + k, steps), third)]
        part = jnp.where(side == 0, part, pltpu.roll(part, third // 2, 1))
        norm_buf[:, k * third : (k + 1) * third] = part.astype(BF16)
    stores.append(pltpu.make_async_copy(norm_buf, norm_ref, out_sem.at[1]))
    stores[1].start()
    for copy in stores:
        copy.wait()


def entry(w_qkv, w_out, state, modes):
    return pl.pallas_call(
        entry_kernel,
        out_shape=[shape_of(*w_out.shape), shape_of(*state.shape)],
        in_specs=[ANY] * 4,
        out_specs=[ANY, ANY],
        scratch_shapes=[
            pltpu.VMEM(w_out.shape, BF16),
            pltpu.VMEM(state.shape, BF16),
            pltpu.VMEM(modes.shape, F32),
            pltpu.VMEM(state.shape, F32),
            pltpu.VMEM(state.shape, BF16),
            pltpu.SemaphoreType.DMA((6,)),
            pltpu.SemaphoreType.DMA((2,)),
        ],
        compiler_params=params(),
        cost_estimate=cost(4e9, 1e6),
    )(w_qkv, w_out, state, modes)


def pack_kernel(count, *refs):
    pieces, packed_ref, held_ref, sem = refs[:count], refs[count], refs[count + 1], refs[count + 2]
    depth = held_ref.shape[0] // count
    columns = held_ref.shape[1]
    pairs = []
    for k, piece in enumerate(pieces):
        pairs.append((piece.at[:, piece.shape[1] - columns :], held_ref.at[k * depth : (k + 1) * depth]))
    for copy in load_all(pairs, sem):
        copy.wait()
    for copy in load_all([(held_ref, packed_ref)], sem):
        copy.wait()


def pack(pieces, columns):
    depth = pieces[0].shape[0]
    full = shape_of(depth * len(pieces), columns)
    return pl.pallas_call(
        functools.partial(pack_kernel, len(pieces)),
        out_shape=full,
        in_specs=[ANY] * len(pieces),
        out_specs=ANY,
        scratch_shapes=[pltpu.VMEM(full.shape, BF16), pltpu.SemaphoreType.DMA((len(pieces),))],
        compiler_params=params(),
        cost_estimate=cost(3e9, 1e6),
    )(*pieces)


def rows_of(piece_refs, held_ref, start=0):
    found, at = [], 0
    for piece in piece_refs:
        rows = piece.shape[0]
        source = piece.at[:, start : start + held_ref.shape[1]]
        found.append((source, held_ref.at[at : at + rows]))
        at += rows
    return found


def first_kernel(count, *refs):
    norms, pieces = refs[:4], refs[4 : 4 + count]
    qk_ref, v_ref = refs[4 + count : 6 + count]
    left_ref, held_ref, qk_out, v_out, sem, out_sem = refs[6 + count :]
    deep, columns = held_ref.shape
    split = 2 * columns // 3
    loads = load_all(
        rows_of(pieces, held_ref) + [(norms[b].at[:, :deep], left_ref.at[b]) for b in range(4)], sem
    )
    for copy in loads:
        copy.wait()
    stores = []
    for block in range(4):
        qk_out[block] = times(left_ref[block], held_ref[:, :split]).astype(BF16)
        v_out[block] = times(left_ref[block], held_ref[:, split:]).astype(BF16)
        for j, (source, target) in enumerate(((qk_out, qk_ref), (v_out, v_ref))):
            copy = pltpu.make_async_copy(source.at[block], target.at[block], out_sem.at[2 * block + j])
            copy.start()
            stores.append(copy)
    for copy in stores:
        copy.wait()


def first_part(norms, pieces):
    rows = norms[0].shape[0]
    columns = 3 * norms[0].shape[1] // 4
    deep = sum(piece.shape[0] for piece in pieces)
    qk = shape_of(4, rows, 2 * columns // 3)
    v = shape_of(4, rows, columns // 3)
    return pl.pallas_call(
        functools.partial(first_kernel, len(pieces)),
        out_shape=[qk, v],
        in_specs=[ANY] * (4 + len(pieces)),
        out_specs=[ANY] * 2,
        scratch_shapes=[
            pltpu.VMEM((4, rows, deep), BF16),
            pltpu.VMEM((deep, columns), BF16),
            pltpu.VMEM(qk.shape, BF16),
            pltpu.VMEM(v.shape, BF16),
            pltpu.SemaphoreType.DMA((4 + len(pieces),)),
            pltpu.SemaphoreType.DMA((8,)),
        ],
        compiler_params=params(),
        cost_estimate=cost(6e9, 1e6),
    )(*norms, *pieces)


def scores_kernel(count, *refs):
    norms, acc_ref, gains_ref, pieces = refs[:4], refs[4], refs[5], refs[6 : 6 + count]
    out_ref, sums_ref, left_ref, held_ref, acc_in, gains_in, out_buf, sums_buf, sem, rest_sem, out_sem = refs[6 + count :]
    deep = held_ref.shape[0]
    third = out_ref.shape[2] // 2
    width = norms[0].shape[1]
    first = [(norms[0].at[:, width - deep :], left_ref.at[0]), (acc_ref.at[0], acc_in.at[0])]
    loads = load_all(rows_of(pieces, held_ref) + [(gains_ref, gains_in)] + first, sem)
    mine = window(places()[3], third)
    row = lax.broadcasted_iota(jnp.int32, (8, 4 * DH), 0)
    lane = lax.broadcasted_iota(jnp.int32, (8, 4 * DH), 1)
    pick = (row == lane // (2 * DH)).astype(BF16)
    for copy in loads:
        copy.wait()
    rest = []
    for b in range(1, 4):
        rest += [(norms[b].at[:, width - deep :], left_ref.at[b]), (acc_ref.at[b], acc_in.at[b])]
    loads = load_all(rest, rest_sem)
    gains = [gains_in[0, :, mine] * (1.4426950408889634 / DH**0.5), gains_in[1, :, mine]]
    stores = []
    for block in range(4):
        if block:
            loads[2 * block - 2].wait()
            loads[2 * block - 1].wait()
        product = times(left_ref[block], held_ref[...])
        squares = []
        for j in range(2):
            square = 0.0
            for h in range(third // DH):
                at = slice(j * third + h * DH, j * third + (h + 1) * DH)
                part = acc_in[block, :, at].astype(F32) + product[:, at]
                square += part * part
                out_buf[block, :, at] = (part * gains[j][:, h * DH : (h + 1) * DH]).astype(BF16)
            high = square.astype(BF16)
            squares += [high, (square - high.astype(F32)).astype(BF16)]
        stores.append(pltpu.make_async_copy(out_buf.at[block], out_ref.at[block], out_sem.at[block]))
        stores[-1].start()
        sums_buf[block] = times_turned(pick, jnp.concatenate(squares, axis=1))
    stores.append(pltpu.make_async_copy(sums_buf, sums_ref, out_sem.at[4]))
    stores[-1].start()
    for copy in stores:
        copy.wait()


def last_scores(norms, acc, gains, pieces):
    rows = norms[0].shape[0]
    columns = acc.shape[2]
    deep = sum(piece.shape[0] for piece in pieces)
    return pl.pallas_call(
        functools.partial(scores_kernel, len(pieces)),
        out_shape=[shape_of(4, rows, columns), shape_of(4, 8, rows, dtype=F32)],
        in_specs=[ANY] * (6 + len(pieces)),
        out_specs=[ANY, ANY],
        scratch_shapes=[
            pltpu.VMEM((4, rows, deep), BF16),
            pltpu.VMEM((deep, columns), BF16),
            pltpu.VMEM(acc.shape, BF16),
            pltpu.VMEM(gains.shape, F32),
            pltpu.VMEM(acc.shape, BF16),
            pltpu.VMEM((4, 8, rows), F32),
            pltpu.SemaphoreType.DMA((3 + len(pieces),)),
            pltpu.SemaphoreType.DMA((6,)),
            pltpu.SemaphoreType.DMA((5,)),
        ],
        compiler_params=params(),
        cost_estimate=cost(6e9, 1e6),
    )(*norms, acc, gains, *pieces)


def values_kernel(count, *refs):
    norms, acc_ref, pieces = refs[:4], refs[4], refs[5 : 5 + count]
    out_ref, left_ref, held_ref, acc_in, out_buf, sem = refs[5 + count :]
    deep, columns = held_ref.shape
    width = norms[0].shape[1]
    loads = load_all(
        rows_of(pieces, held_ref, 2 * columns)
        + [(norms[b].at[:, width - deep :], left_ref.at[b]) for b in range(4)]
        + [(acc_ref.at[b], acc_in.at[b]) for b in range(4)],
        sem,
    )
    for copy in loads[:count]:
        copy.wait()
    stores = []
    for block in range(4):
        loads[count + block].wait()
        product = times(left_ref[block], held_ref[...])
        loads[count + 4 + block].wait()
        out_buf[block] = (acc_in[block].astype(F32) + product).astype(BF16)
        stores.append(pltpu.make_async_copy(out_buf.at[block], out_ref.at[block], sem.at[block]))
        stores[-1].start()
    for copy in stores:
        copy.wait()


def last_values(norms, acc, pieces):
    rows = norms[0].shape[0]
    columns = acc.shape[2]
    deep = sum(piece.shape[0] for piece in pieces)
    return pl.pallas_call(
        functools.partial(values_kernel, len(pieces)),
        out_shape=shape_of(4, rows, columns),
        in_specs=[ANY] * 5 + [ANY] * len(pieces),
        out_specs=ANY,
        scratch_shapes=[
            pltpu.VMEM((4, rows, deep), BF16),
            pltpu.VMEM((deep, columns), BF16),
            pltpu.VMEM(acc.shape, BF16),
            pltpu.VMEM(acc.shape, BF16),
            pltpu.SemaphoreType.DMA((8 + len(pieces),)),
        ],
        compiler_params=params(),
        cost_estimate=cost(4e9, 1e6),
    )(*norms, acc, *pieces)


def heads_kernel(length_ref, qk_ref, v_ref, s0_ref, s1_ref, s2_ref, s3_ref, *refs):
    outs = refs[:4]
    qk_in, v_in, sums_in, out_buf, sem, out_sem = refs[4:]
    rows = qk_ref.shape[1]
    third = qk_ref.shape[2] // 2
    count = third // DH
    width = 4 * third
    sum_refs = (s0_ref, s1_ref, s2_ref, s3_ref)
    loads = load_all(
        [(sum_refs[j], sums_in.at[j]) for j in range(4)]
        + [(qk_ref.at[b], qk_in.at[b]) for b in range(4)]
        + [
            (v_ref.at[b, :, h * DH : (h + 1) * DH], v_in.at[h, b // 2, b % 2 * rows : (b % 2 + 1) * rows, :DH])
            for b in range(4)
            for h in range(count)
        ],
        sem,
    )
    for h in range(count):
        for b in range(2):
            v_in[h, b, :, DH:] = jnp.ones((2 * rows, DH), BF16)
    row = lax.broadcasted_iota(jnp.int32, (24, DH), 0)
    pick = (row % 8 == 0).astype(BF16)
    place = lax.broadcasted_iota(jnp.int32, (1, rows), 1)
    position = lax.axis_index("seq")
    masks = [place < length_ref[0] - (j + position - 2 * j * position) * rows for j in range(2)]
    for copy in loads[:4]:
        copy.wait()
    scale_q, scale_k = [], []
    for block in range(4):
        sums = sums_in[0, block] + sums_in[1, block ^ 1] + sums_in[2, block ^ 2] + sums_in[3, block ^ 3]
        inverse = lax.rsqrt(sums * (1.0 / width) + 1e-06)
        high = inverse.astype(BF16).astype(F32)
        middle = (inverse - high).astype(BF16).astype(F32)
        stacked = jnp.concatenate([high, middle, inverse - high - middle], axis=0).astype(BF16)
        turned = lax.dot_general(stacked, pick, (((0,), (0,)), ((), ())), preferred_element_type=F32)
        scale_q.append(turned[:, :1])
        scale_k.append(inverse[1:2, :])
    for copy in loads[4:8]:
        copy.wait()
    items = [(block, h) for block in (1, 3, 2, 0) for h in range(count)]

    def scores_of(block, h):
        first = block - block % 2
        query = qk_in[block, :, h * DH : (h + 1) * DH]
        found = []
        for j in range(2):
            keys = qk_in[first + j, :, third + h * DH : third + (h + 1) * DH]
            part = times_turned(query, keys) * scale_k[first + j]
            found.append(jnp.where(masks[j], part, -1e30))
        return found

    stores = []
    ahead = scores_of(*items[0])
    for at, (block, h) in enumerate(items):
        scores = ahead
        if at + 1 < len(items):
            ahead = scores_of(*items[at + 1])
        if at == 0:
            for copy in loads[8:]:
                copy.wait()
        top = jnp.maximum(
            jnp.max(scores[0], axis=-1, keepdims=True), jnp.max(scores[1], axis=-1, keepdims=True)
        )
        weighted = 0.0
        for j in range(2):
            probs = jnp.exp2((scores[j] - top) * scale_q[block]).astype(BF16)
            weighted += times(probs, v_in[h, block // 2, j * rows : (j + 1) * rows, :])
        out_buf[block, :, h * DH : (h + 1) * DH] = (weighted[:, :DH] / weighted[:, DH:]).astype(BF16)
        if h == count - 1:
            stores.append(pltpu.make_async_copy(out_buf.at[block], outs[block], out_sem.at[block]))
            stores[-1].start()
    for copy in stores:
        copy.wait()


def team_attention(length, qk, v, sums):
    rows = qk.shape[1]
    third = qk.shape[2] // 2
    return pl.pallas_call(
        heads_kernel,
        out_shape=[shape_of(rows, third)] * 4,
        in_specs=[SMEM] + [ANY] * 6,
        out_specs=[ANY] * 4,
        scratch_shapes=[
            pltpu.VMEM(qk.shape, BF16),
            pltpu.VMEM((third // DH, 2, 2 * rows, 2 * DH), BF16),
            pltpu.VMEM((4, 4, 8, rows), F32),
            pltpu.VMEM((4, rows, third), BF16),
            pltpu.SemaphoreType.DMA((8 + 4 * third // DH,)),
            pltpu.SemaphoreType.DMA((4,)),
        ],
        compiler_params=params(),
        cost_estimate=cost(1.1e10, 1e6),
    )(length, qk, v, *sums)


def out_kernel(state_ref, modes_ref, head_ref, *refs):
    attended, pieces = refs[:4], refs[4:12]
    own_ref, sent_ref = refs[12:14]
    att_in, group_ref, held_ref, state_in, modes_in, head_in_ref, own_buf, sent_buf, sem = refs[14:]
    side, pair, steps, own = places()
    third = attended[0].shape[1]
    half = pieces[0].shape[0]
    loads = load_all(
        [(attended[j], att_in.at[j]) for j in range(4)]
        + [(pieces[j], held_ref.at[:half, window(own ^ j, third)]) for j in range(4)]
        + [(pieces[4 + j], held_ref.at[half:, window(own ^ j, third)]) for j in range(4)]
        + [(state_ref, state_in), (modes_ref, modes_in), (head_ref, head_in_ref)],
        sem,
    )
    for j in range(4):
        loads[j].wait()
        part = att_in[j].astype(F32)
        part = jnp.where(side == 0, part, pltpu.roll(part, third // 2, 1)).astype(BF16)
        group_ref[:, window(lax.rem((own ^ j) + steps - pair, steps), third)] = part
    for copy in loads[4:8]:
        copy.wait()
    total = times(group_ref[:, :half], held_ref[:half, :])
    for copy in loads[8:]:
        copy.wait()
    total += times(group_ref[:, half:], held_ref[half:, :])
    block_out = (state_in[...].astype(F32) + modes_in[2] * total).astype(BF16)
    head_in = scaled_norm(block_out.astype(F32), modes_in[3], modes_in[4])
    velocity = times_turned(head_in_ref[...], head_in.astype(BF16))
    channels = own_buf.shape[0]
    core = lax.axis_index("cfg")
    own_buf[...] = jnp.where(core == 0, velocity[:channels], velocity[channels:])
    sent_buf[...] = jnp.where(core == 0, velocity[channels:], velocity[:channels]).astype(BF16)
    for copy in load_all([(own_buf, own_ref), (sent_buf, sent_ref)], sem):
        copy.wait()


def project(state, modes, w_head, attended, pieces):
    rows, width = state.shape
    third = width // 4
    channels = w_head.shape[0] // 2
    return pl.pallas_call(
        out_kernel,
        out_shape=[shape_of(channels, rows, dtype=F32), shape_of(channels, rows)],
        in_specs=[ANY] * 15,
        out_specs=[ANY, ANY],
        scratch_shapes=[
            pltpu.VMEM((4, rows, third), BF16),
            pltpu.VMEM((rows, width), BF16),
            pltpu.VMEM((width, width), BF16),
            pltpu.VMEM(state.shape, BF16),
            pltpu.VMEM(modes.shape, F32),
            pltpu.VMEM(w_head.shape, BF16),
            pltpu.VMEM((channels, rows), F32),
            pltpu.VMEM((channels, rows), BF16),
            pltpu.SemaphoreType.DMA((15,)),
        ],
        compiler_params=params(),
        cost_estimate=cost(8e9, 1e6),
    )(state, modes, w_head, *attended, *pieces)


def updated_latent(own, outgoing, latent, guidance, step_size, length, position):
    rows = own.shape[1]
    branch = lax.axis_index("cfg")
    scale = guidance[0]
    other = lax.ppermute(outgoing, "cfg", SWAP).astype(own.dtype)
    cond = jnp.where(branch == 0, own, other)
    uncond = jnp.where(branch == 0, other, own)
    guided = uncond + scale * (cond - uncond)
    valid = position * rows + jnp.arange(rows, dtype=jnp.int32) < length
    current = latent[0].T
    updated = jnp.where(valid[None, :], current - step_size[0] * guided, current)
    return updated.T[None]


def after(value, *others):
    return lax.optimization_barrier((value, *others))[0]


def team_local(
    hidden, latent, modulation, w_qkv, w_out, q_gain, k_gain, w_head, lengths, guidance, step_size
):
    state = hidden[0, 0]
    modes = jnp.transpose(modulation, (1, 0, 2))
    rows, width = state.shape
    third = width // 4
    parts = lax.axis_size("req")
    up = [(i, (i - 2) % parts) for i in range(parts)]
    down = [(i, (i + 2) % parts) for i in range(parts)]
    beside = [(i, i ^ 1) for i in range(parts)]

    def along(piece):
        return lax.ppermute(piece, "req", up)

    def back(piece):
        return lax.ppermute(piece, "req", down)

    def across(piece):
        return lax.ppermute(piece, "req", beside)

    gains = jnp.stack([q_gain, k_gain])[:, None]
    columns, normed = entry(w_qkv, w_out, state, modes)
    normed_y = lax.ppermute(normed, "seq", SWAP)
    normed_c = lax.ppermute(normed, "cfg", SWAP)

    def step(mine, theirs, gates):
        now = after(mine[-1], *gates)
        mine.append(along(now))
        theirs.append(across(now))

    mine, theirs = [columns], []
    step(mine, theirs, [])
    cut, split = columns.shape[0] // 2, 3 * third
    low = theirs[0][cut:, :split]
    out_last = theirs[0][:, split:]
    gates = [mine[1], theirs[0], low, out_last, gains]
    step(mine, theirs, gates)
    gates = [mine[2], theirs[1]]
    step(mine, theirs, gates)
    out_last = back(after(out_last, *gates))
    early = [mine[0], theirs[0], mine[1], theirs[1]]
    packed = [pack(early, third)]
    normed_yc = lax.ppermute(normed_y, "cfg", SWAP)
    norms = [normed, normed_y, normed_c, normed_yc]
    packed_y = [lax.ppermute(packed[0], "seq", SWAP)]
    acc_qk, acc_v = first_part(norms, early)
    gates = [mine[3], theirs[2], out_last, packed_y[0], acc_v]
    upper = across(after(mine[3][:cut, :split], *gates))
    lower = back(after(low, *gates))
    late = [mine[2], theirs[2], mine[3], upper, lower]
    packed.append(pack([mine[2], theirs[2], mine[3], out_last], third))
    packed_y.append(lax.ppermute(packed[1], "seq", SWAP))
    packed_c = [lax.ppermute(part, "cfg", SWAP) for part in packed]
    packed_yc = [lax.ppermute(part, "cfg", SWAP) for part in packed_y]

    qk_full, sums = last_scores(norms, acc_qk, gains, late)
    v_full = last_values(norms, acc_v, late)
    diagonal = [(i, 3 - i) for i in range(4)]
    all_sums = [
        sums,
        lax.ppermute(sums, "seq", SWAP),
        lax.ppermute(sums, "cfg", SWAP),
        lax.ppermute(sums, ("cfg", "seq"), diagonal),
    ]
    v_full = after(v_full, packed_y[1], *packed_c, packed_yc[0])
    heads = team_attention(lengths, qk_full, v_full, all_sums)
    attended = [
        heads[0],
        lax.ppermute(heads[2], "cfg", SWAP),
        lax.ppermute(heads[1], "seq", SWAP),
        lax.ppermute(heads[3], ("cfg", "seq"), diagonal),
    ]
    quarters = [part[j] for j in range(2) for part in (packed, packed_c, packed_y, packed_yc)]
    own, outgoing = project(state, modes, w_head.T, attended, quarters)
    return updated_latent(own, outgoing, latent, guidance, step_size, lengths[0], lax.axis_index("seq"))


def by_team(mesh, arguments):
    hidden, w_qkv = arguments[0], arguments[3]
    sizes = mesh.shape
    width = hidden.shape[3]
    depth = w_qkv.shape[0] // sizes["req"]
    return (
        sizes["cfg"] == 2
        and sizes["seq"] == 2
        and sizes["req"] == 8
        and width % (4 * DH) == 0
        and 8 * depth == width
        and depth % 32 == 0
        and hidden.shape[2] // sizes["seq"] % 16 == 0
    )


def solution(mesh):
    def whole(*arguments):
        body = team_local if by_team(mesh, arguments) else ring_local
        return jax.shard_map(
            body,
            mesh=mesh,
            in_specs=(
                P("cfg", "req", "seq", None),
                P("req", "seq", "cfg"),
                P("req", None, None),
                P("req", None),
                P("req", None),
                P(),
                P(),
                P(),
                P("req"),
                P("req"),
                P("req"),
            ),
            out_specs=P("req", "seq", "cfg"),
            check_vma=False,
        )(*arguments)

    return whole
```

```python
import functools

import jax
import jax.numpy as jnp
from jax import lax
from jax.experimental import pallas as pl
from jax.experimental.pallas import tpu as pltpu
from jax.sharding import PartitionSpec as P

DH = 128
SWAP = [(0, 1), (1, 0)]
SMEM = pl.BlockSpec(memory_space=pltpu.SMEM)
ANY = pl.BlockSpec(memory_space=pl.ANY)
BF16 = jnp.bfloat16
F32 = jnp.float32


def params():
    return pltpu.CompilerParams(vmem_limit_bytes=60 * 2**20)


def cost(flops, moved, exps=0):
    return pl.CostEstimate(flops=int(flops), bytes_accessed=int(moved), transcendentals=int(exps))


def shape_of(*dims, dtype=BF16):
    return jax.ShapeDtypeStruct(dims, dtype)


def times(left, right):
    return jnp.dot(left, right, preferred_element_type=F32)


def times_turned(left, right):
    return lax.dot_general(left, right, (((1,), (1,)), ((), ())), preferred_element_type=F32)


def passed_along(value, axis, steps):
    count = lax.axis_size(axis)
    pairs = [(source, (source + steps) % count) for source in range(count)]
    return lax.ppermute(value, axis, pairs)


def from_partner(value, axis, apart):
    mask = 2**apart
    pairs = [(source, source ^ mask) for source in range(lax.axis_size(axis))]
    return lax.ppermute(value, axis, pairs)


def layer_norm(values):
    centered = values - jnp.mean(values, axis=-1, keepdims=True)
    return centered / jnp.sqrt(jnp.mean(centered * centered, axis=-1, keepdims=True) + 1e-06)


def rms_gain(values, gain):
    return values / jnp.sqrt(jnp.mean(values * values, axis=-1, keepdims=True) + 1e-06) * gain


def add_rows(left, piece):
    return jnp.dot(left, piece, preferred_element_type=jnp.float32)


def attend(state, query, stacked, start, length):
    top, total, weighted = state
    keys = stacked[0]
    values = stacked[1]
    count = keys.shape[0]
    scores = jnp.einsum("qhd,khd->qhk", query, keys, preferred_element_type=jnp.float32) / jnp.sqrt(
        jnp.float32(query.shape[2])
    )
    valid = start + jnp.arange(count, dtype=jnp.int32) < length
    scores = jnp.where(valid[None, None, :], scores, jnp.float32(-1e30))
    new_top = jnp.maximum(top, jnp.max(scores, axis=-1))
    factor = jnp.exp(top - new_top)
    probs = jnp.where(valid[None, None, :], jnp.exp(scores - new_top[:, :, None]), jnp.float32(0.0))
    total = total * factor + jnp.sum(probs, axis=-1)
    weighted = weighted * factor[:, :, None] + jnp.einsum(
        "qhk,khd->qhd", probs.astype(jnp.bfloat16), values, preferred_element_type=jnp.float32
    )
    return (new_top, total, weighted)


def ring_local(
    hidden, latent, modulation, w_qkv, w_out, q_gain, k_gain, w_head, lengths, guidance, step_size
):
    state = hidden[0, 0]
    modes = modulation[0]
    length = lengths[0]
    rows = state.shape[0]
    width = state.shape[1]
    heads = q_gain.shape[0] // DH
    wide = state.astype(jnp.float32)
    normed = (layer_norm(wide) * (1.0 + modes[1]) + modes[0]).astype(jnp.bfloat16)
    qkv = add_rows(normed, lax.all_gather(w_qkv, "req", axis=0, tiled=True))
    query = rms_gain(qkv[:, :width], q_gain).astype(jnp.bfloat16).reshape(rows, heads, DH)
    keys = rms_gain(qkv[:, width : 2 * width], k_gain).astype(jnp.bfloat16).reshape(rows, heads, DH)
    values = qkv[:, 2 * width :].astype(jnp.bfloat16).reshape(rows, heads, DH)
    stacked = jnp.stack([keys, values])
    position = lax.axis_index("seq")
    members = lax.axis_size("seq")
    start_state = (
        jnp.full((rows, heads), -1e30, jnp.float32),
        jnp.zeros((rows, heads), jnp.float32),
        jnp.zeros((rows, heads, DH), jnp.float32),
    )
    first = attend(start_state, query, stacked, position * rows, length)

    def cycle_step(turn, carry):
        moving, inner = carry
        moving = passed_along(moving, "seq", 1)
        source = (position - turn) % members
        return (moving, attend(inner, query, moving, source * rows, length))

    moved, result = lax.fori_loop(1, members, cycle_step, (stacked, first))
    top, total, weighted = result
    attended = (weighted / total[:, :, None]).reshape(rows, width).astype(jnp.bfloat16)
    projected = add_rows(attended, lax.all_gather(w_out, "req", axis=0, tiled=True))
    block_out = (wide + modes[2] * projected).astype(jnp.bfloat16)
    head_in = (layer_norm(block_out.astype(jnp.float32)) * (1.0 + modes[4]) + modes[3]).astype(
        jnp.bfloat16
    )
    velocity = jnp.dot(head_in, w_head, preferred_element_type=jnp.float32)
    branch = lax.axis_index("cfg")
    scale = guidance[0]
    channels = velocity.shape[1] // 2
    own = lax.dynamic_slice_in_dim(velocity, branch * channels, channels, 1)
    outgoing = lax.dynamic_slice_in_dim(velocity, (1 - branch) * channels, channels, 1)
    other = from_partner(outgoing.astype(jnp.bfloat16), "cfg", 0).astype(outgoing.dtype)
    cond = jnp.where(branch == 0, own, other)
    uncond = jnp.where(branch == 0, other, own)
    guided = uncond + scale * (cond - uncond)
    valid = position * rows + jnp.arange(rows, dtype=jnp.int32) < length
    current = latent[0]
    updated = jnp.where(valid[:, None], current - step_size[0] * guided, current)
    return updated[None]


def load_all(pairs, sem):
    copies = [pltpu.make_async_copy(source, target, sem.at[j]) for j, (source, target) in enumerate(pairs)]
    for copy in copies:
        copy.start()
    return copies


def fold(pair):
    return pair ^ (pair // 2)


def places():
    place = lax.axis_index("req")
    group = 2 * lax.axis_index("seq") + lax.axis_index("cfg")
    return lax.rem(place, 2), fold(place // 2), lax.axis_size("req") // 2, group


def window(j, size):
    return pl.ds(pl.multiple_of(j * size, size), size)


def scaled_norm(values, shift, scale):
    centered = values - jnp.mean(values, axis=-1, keepdims=True)
    inverse = lax.rsqrt(jnp.mean(centered * centered, axis=-1, keepdims=True) + 1e-06)
    return centered * inverse * (1.0 + scale) + shift


def entry_kernel(qkv_ref, w_out_ref, state_ref, modes_ref, cut_ref, norm_ref, *scratch):
    cut_buf, state_in, modes_in, full_ref, norm_buf, sem, out_sem = scratch
    side, pair, steps, group = places()
    third = cut_ref.shape[1] // 4
    loads = [(state_ref, state_in), (modes_ref, modes_in)]
    for j in range(3):
        loads.append((qkv_ref.at[:, window(4 * j + group, third)], cut_buf.at[:, j * third : (j + 1) * third]))
    loads.append((w_out_ref.at[:, window(group, third)], cut_buf.at[:, 3 * third :]))
    loads = load_all(loads, sem)
    for copy in loads[:2]:
        copy.wait()
    full_ref[...] = scaled_norm(state_in[...].astype(F32), modes_in[0], modes_in[1])
    for copy in loads[2:]:
        copy.wait()
    stores = [pltpu.make_async_copy(cut_buf, cut_ref, out_sem.at[0])]
    stores[0].start()
    count = 4
    for k in range(count):
        part = full_ref[:, window(fold(lax.rem(pair + k, steps)), third)]
        part = jnp.where(side == 0, part, pltpu.roll(part, third // 2, 1))
        norm_buf[:, k * third : (k + 1) * third] = part.astype(BF16)
    stores.append(pltpu.make_async_copy(norm_buf, norm_ref, out_sem.at[1]))
    stores[1].start()
    for copy in stores:
        copy.wait()


def entry(w_qkv, w_out, state, modes):
    return pl.pallas_call(
        entry_kernel,
        out_shape=[shape_of(*w_out.shape), shape_of(*state.shape)],
        in_specs=[ANY] * 4,
        out_specs=[ANY, ANY],
        scratch_shapes=[
            pltpu.VMEM(w_out.shape, BF16),
            pltpu.VMEM(state.shape, BF16),
            pltpu.VMEM(modes.shape, F32),
            pltpu.VMEM(state.shape, F32),
            pltpu.VMEM(state.shape, BF16),
            pltpu.SemaphoreType.DMA((6,)),
            pltpu.SemaphoreType.DMA((2,)),
        ],
        compiler_params=params(),
        cost_estimate=cost(4e9, 1e6),
    )(w_qkv, w_out, state, modes)


def pack_kernel(count, *refs):
    pieces, packed_ref, held_ref, sem = refs[:count], refs[count], refs[count + 1], refs[count + 2]
    depth = held_ref.shape[0] // count
    columns = held_ref.shape[1]
    pairs = []
    for k, piece in enumerate(pieces):
        pairs.append((piece.at[:, piece.shape[1] - columns :], held_ref.at[k * depth : (k + 1) * depth]))
    for copy in load_all(pairs, sem):
        copy.wait()
    for copy in load_all([(held_ref, packed_ref)], sem):
        copy.wait()


def pack(pieces, columns):
    depth = pieces[0].shape[0]
    full = shape_of(depth * len(pieces), columns)
    return pl.pallas_call(
        functools.partial(pack_kernel, len(pieces)),
        out_shape=full,
        in_specs=[ANY] * len(pieces),
        out_specs=ANY,
        scratch_shapes=[pltpu.VMEM(full.shape, BF16), pltpu.SemaphoreType.DMA((len(pieces),))],
        compiler_params=params(),
        cost_estimate=cost(3e9, 1e6),
    )(*pieces)


def rows_of(piece_refs, held_ref, start=0):
    found, at = [], 0
    for piece in piece_refs:
        rows = piece.shape[0]
        source = piece.at[:, start : start + held_ref.shape[1]]
        found.append((source, held_ref.at[at : at + rows]))
        at += rows
    return found


def first_kernel(count, *refs):
    norms, pieces = refs[:4], refs[4 : 4 + count]
    qk_ref, v_ref = refs[4 + count : 6 + count]
    left_ref, held_ref, qk_out, v_out, sem, out_sem = refs[6 + count :]
    deep, columns = held_ref.shape
    split = 2 * columns // 3
    loads = load_all(
        rows_of(pieces, held_ref) + [(norms[b].at[:, :deep], left_ref.at[b]) for b in range(4)], sem
    )
    for copy in loads:
        copy.wait()
    stores = []
    for block in range(4):
        qk_out[block] = times(left_ref[block], held_ref[:, :split]).astype(BF16)
        v_out[block] = times(left_ref[block], held_ref[:, split:]).astype(BF16)
        for j, (source, target) in enumerate(((qk_out, qk_ref), (v_out, v_ref))):
            copy = pltpu.make_async_copy(source.at[block], target.at[block], out_sem.at[2 * block + j])
            copy.start()
            stores.append(copy)
    for copy in stores:
        copy.wait()


def first_part(norms, pieces):
    rows = norms[0].shape[0]
    columns = 3 * norms[0].shape[1] // 4
    deep = sum(piece.shape[0] for piece in pieces)
    qk = shape_of(4, rows, 2 * columns // 3)
    v = shape_of(4, rows, columns // 3)
    return pl.pallas_call(
        functools.partial(first_kernel, len(pieces)),
        out_shape=[qk, v],
        in_specs=[ANY] * (4 + len(pieces)),
        out_specs=[ANY] * 2,
        scratch_shapes=[
            pltpu.VMEM((4, rows, deep), BF16),
            pltpu.VMEM((deep, columns), BF16),
            pltpu.VMEM(qk.shape, BF16),
            pltpu.VMEM(v.shape, BF16),
            pltpu.SemaphoreType.DMA((4 + len(pieces),)),
            pltpu.SemaphoreType.DMA((8,)),
        ],
        compiler_params=params(),
        cost_estimate=cost(6e9, 1e6),
    )(*norms, *pieces)


def scores_kernel(count, *refs):
    norms, acc_ref, gains_ref, pieces = refs[:4], refs[4], refs[5], refs[6 : 6 + count]
    out_ref, sums_ref, left_ref, held_ref, acc_in, gains_in, out_buf, sums_buf, sem, rest_sem, out_sem = refs[6 + count :]
    deep = held_ref.shape[0]
    third = out_ref.shape[2] // 2
    width = norms[0].shape[1]
    first = [(norms[0].at[:, width - deep :], left_ref.at[0]), (acc_ref.at[0], acc_in.at[0])]
    loads = load_all(rows_of(pieces, held_ref) + [(gains_ref, gains_in)] + first, sem)
    mine = window(places()[3], third)
    row = lax.broadcasted_iota(jnp.int32, (8, 4 * DH), 0)
    lane = lax.broadcasted_iota(jnp.int32, (8, 4 * DH), 1)
    pick = (row == lane // (2 * DH)).astype(BF16)
    for copy in loads:
        copy.wait()
    rest = []
    for b in range(1, 4):
        rest += [(norms[b].at[:, width - deep :], left_ref.at[b]), (acc_ref.at[b], acc_in.at[b])]
    loads = load_all(rest, rest_sem)
    gains = [gains_in[0, :, mine] * (1.4426950408889634 / DH**0.5), gains_in[1, :, mine]]
    stores = []
    for block in range(4):
        if block:
            loads[2 * block - 2].wait()
            loads[2 * block - 1].wait()
        product = times(left_ref[block], held_ref[...])
        squares = []
        for j in range(2):
            square = 0.0
            for h in range(third // DH):
                at = slice(j * third + h * DH, j * third + (h + 1) * DH)
                part = acc_in[block, :, at].astype(F32) + product[:, at]
                square += part * part
                out_buf[block, :, at] = (part * gains[j][:, h * DH : (h + 1) * DH]).astype(BF16)
            high = square.astype(BF16)
            squares += [high, (square - high.astype(F32)).astype(BF16)]
        stores.append(pltpu.make_async_copy(out_buf.at[block], out_ref.at[block], out_sem.at[block]))
        stores[-1].start()
        sums_buf[block] = times_turned(pick, jnp.concatenate(squares, axis=1))
    stores.append(pltpu.make_async_copy(sums_buf, sums_ref, out_sem.at[4]))
    stores[-1].start()
    for copy in stores:
        copy.wait()


def last_scores(norms, acc, gains, pieces):
    rows = norms[0].shape[0]
    columns = acc.shape[2]
    deep = sum(piece.shape[0] for piece in pieces)
    return pl.pallas_call(
        functools.partial(scores_kernel, len(pieces)),
        out_shape=[shape_of(4, rows, columns), shape_of(4, 8, rows, dtype=F32)],
        in_specs=[ANY] * (6 + len(pieces)),
        out_specs=[ANY, ANY],
        scratch_shapes=[
            pltpu.VMEM((4, rows, deep), BF16),
            pltpu.VMEM((deep, columns), BF16),
            pltpu.VMEM(acc.shape, BF16),
            pltpu.VMEM(gains.shape, F32),
            pltpu.VMEM(acc.shape, BF16),
            pltpu.VMEM((4, 8, rows), F32),
            pltpu.SemaphoreType.DMA((3 + len(pieces),)),
            pltpu.SemaphoreType.DMA((6,)),
            pltpu.SemaphoreType.DMA((5,)),
        ],
        compiler_params=params(),
        cost_estimate=cost(6e9, 1e6),
    )(*norms, acc, gains, *pieces)


def values_kernel(count, *refs):
    norms, acc_ref, pieces = refs[:4], refs[4], refs[5 : 5 + count]
    out_ref, left_ref, held_ref, acc_in, out_buf, sem = refs[5 + count :]
    deep, columns = held_ref.shape
    width = norms[0].shape[1]
    loads = load_all(
        rows_of(pieces, held_ref, 2 * columns)
        + [(norms[b].at[:, width - deep :], left_ref.at[b]) for b in range(4)]
        + [(acc_ref.at[b], acc_in.at[b]) for b in range(4)],
        sem,
    )
    for copy in loads[:count]:
        copy.wait()
    stores = []
    for block in range(4):
        loads[count + block].wait()
        product = times(left_ref[block], held_ref[...])
        loads[count + 4 + block].wait()
        out_buf[block] = (acc_in[block].astype(F32) + product).astype(BF16)
        stores.append(pltpu.make_async_copy(out_buf.at[block], out_ref.at[block], sem.at[block]))
        stores[-1].start()
    for copy in stores:
        copy.wait()


def last_values(norms, acc, pieces):
    rows = norms[0].shape[0]
    columns = acc.shape[2]
    deep = sum(piece.shape[0] for piece in pieces)
    return pl.pallas_call(
        functools.partial(values_kernel, len(pieces)),
        out_shape=shape_of(4, rows, columns),
        in_specs=[ANY] * 5 + [ANY] * len(pieces),
        out_specs=ANY,
        scratch_shapes=[
            pltpu.VMEM((4, rows, deep), BF16),
            pltpu.VMEM((deep, columns), BF16),
            pltpu.VMEM(acc.shape, BF16),
            pltpu.VMEM(acc.shape, BF16),
            pltpu.SemaphoreType.DMA((8 + len(pieces),)),
        ],
        compiler_params=params(),
        cost_estimate=cost(4e9, 1e6),
    )(*norms, acc, *pieces)


def heads_kernel(blocks, length_ref, qk_ref, v_ref, s0_ref, s1_ref, s2_ref, s3_ref, *refs):
    outs = refs[:2]
    qk_in, v_in, sums_in, out_buf, sem, out_sem = refs[2:]
    rows = qk_ref.shape[1]
    third = qk_ref.shape[2] // 2
    count = third // DH
    width = 4 * third
    sum_refs = (s0_ref, s1_ref, s2_ref, s3_ref)
    loads = [(sum_refs[j], sums_in.at[j]) for j in range(4)]
    order = [b for block in blocks for b in (block - block % 2, block - block % 2 + 1)]
    for b in order:
        loads.append((qk_ref.at[b], qk_in.at[b]))
    for b in order:
        held = v_in.at[b // 2, b % 2 * rows : (b % 2 + 1) * rows]
        for h in range(count):
            loads.append((v_ref.at[b, :, h * DH : (h + 1) * DH], held.at[:, 2 * h * DH : (2 * h + 1) * DH]))
    loads = load_all(loads, sem)
    for b in range(2):
        for h in range(count):
            v_in[b, :, (2 * h + 1) * DH : (2 * h + 2) * DH] = jnp.ones((2 * rows, DH), BF16)
    row = lax.broadcasted_iota(jnp.int32, (24, DH), 0)
    pick = (row % 8 == 0).astype(BF16)
    place = lax.broadcasted_iota(jnp.int32, (1, rows), 1)
    position = lax.axis_index("seq")
    masks = [place < length_ref[0] - (j + position - 2 * j * position) * rows for j in range(2)]
    for copy in loads[:4]:
        copy.wait()
    scale_q, scale_k = {}, {}
    for block in range(4):
        sums = sums_in[0, block] + sums_in[1, block ^ 1] + sums_in[2, block ^ 2] + sums_in[3, block ^ 3]
        inverse = lax.rsqrt(sums * (1.0 / width) + 1e-06)
        scale_k[block] = inverse[1:2, :]
        if block in blocks:
            high = inverse.astype(BF16).astype(F32)
            middle = (inverse - high).astype(BF16).astype(F32)
            stacked = jnp.concatenate([high, middle, inverse - high - middle], axis=0).astype(BF16)
            turned = lax.dot_general(stacked, pick, (((0,), (0,)), ((), ())), preferred_element_type=F32)
            scale_q[block] = turned[:, :1]
    items = [(at, block, h) for at, block in enumerate(blocks) for h in range(count)]

    def scores_of(at, block, h):
        if h == 0:
            for copy in loads[4 + 2 * at : 6 + 2 * at]:
                copy.wait()
        first = block - block % 2
        query = qk_in[block, :, h * DH : (h + 1) * DH]
        found = []
        for j in range(2):
            keys = qk_in[first + j, :, third + h * DH : third + (h + 1) * DH]
            part = times_turned(query, keys) * scale_k[first + j]
            found.append(jnp.where(masks[j], part, -1e30))
        return found

    stores = []
    ahead = scores_of(*items[0])
    for turn, (at, block, h) in enumerate(items):
        scores = ahead
        if turn + 1 < len(items):
            ahead = scores_of(*items[turn + 1])
        if h == 0:
            for copy in loads[8 + 2 * count * at : 8 + 2 * count * (at + 1)]:
                copy.wait()
        top = jnp.maximum(
            jnp.max(scores[0], axis=-1, keepdims=True), jnp.max(scores[1], axis=-1, keepdims=True)
        )
        weighted = 0.0
        for j in range(2):
            probs = jnp.exp2((scores[j] - top) * scale_q[block]).astype(BF16)
            values = v_in[block // 2, j * rows : (j + 1) * rows, 2 * h * DH : (2 * h + 2) * DH]
            weighted += times(probs, values)
        out_buf[at, :, h * DH : (h + 1) * DH] = (weighted[:, :DH] / weighted[:, DH:]).astype(BF16)
        if h == count - 1:
            stores.append(pltpu.make_async_copy(out_buf.at[at], outs[at], out_sem.at[at]))
            stores[-1].start()
    for copy in stores:
        copy.wait()


def team_attention(blocks, effort, length, qk, v, sums):
    rows = qk.shape[1]
    third = qk.shape[2] // 2
    count = third // DH
    return pl.pallas_call(
        functools.partial(heads_kernel, blocks),
        out_shape=[shape_of(rows, third)] * 2,
        in_specs=[SMEM] + [ANY] * 6,
        out_specs=[ANY] * 2,
        scratch_shapes=[
            pltpu.VMEM(qk.shape, BF16),
            pltpu.VMEM((2, 2 * rows, 2 * third), BF16),
            pltpu.VMEM((4, 4, 8, rows), F32),
            pltpu.VMEM((2, rows, third), BF16),
            pltpu.SemaphoreType.DMA((8 + 4 * count,)),
            pltpu.SemaphoreType.DMA((2,)),
        ],
        compiler_params=params(),
        cost_estimate=cost(effort, 1e6),
    )(length, qk, v, *sums)


def out_kernel(state_ref, modes_ref, head_ref, *refs):
    attended, pieces = refs[:4], refs[4:12]
    own_ref, sent_ref = refs[12:14]
    att_in, group_ref, held_ref, state_in, modes_in, head_in_ref, own_buf, sent_buf, sem = refs[14:]
    side, pair, steps, own = places()
    third = attended[0].shape[1]
    half = pieces[0].shape[0]
    loads = load_all(
        [(attended[j], att_in.at[j]) for j in range(4)]
        + [(pieces[j], held_ref.at[:half, window(own ^ j, third)]) for j in range(4)]
        + [(pieces[4 + j], held_ref.at[half:, window(own ^ j, third)]) for j in range(4)]
        + [(state_ref, state_in), (modes_ref, modes_in), (head_ref, head_in_ref)],
        sem,
    )
    for j in range(4):
        loads[j].wait()
        part = att_in[j].astype(F32)
        part = jnp.where(side == 0, part, pltpu.roll(part, third // 2, 1)).astype(BF16)
        group_ref[:, window(lax.rem(fold(own ^ j) + steps - pair, steps), third)] = part
    for copy in loads[4:8]:
        copy.wait()
    total = times(group_ref[:, :half], held_ref[:half, :])
    for copy in loads[8:]:
        copy.wait()
    total += times(group_ref[:, half:], held_ref[half:, :])
    block_out = (state_in[...].astype(F32) + modes_in[2] * total).astype(BF16)
    head_in = scaled_norm(block_out.astype(F32), modes_in[3], modes_in[4])
    velocity = times_turned(head_in_ref[...], head_in.astype(BF16))
    channels = own_buf.shape[0]
    core = lax.axis_index("cfg")
    own_buf[...] = jnp.where(core == 0, velocity[:channels], velocity[channels:])
    sent_buf[...] = jnp.where(core == 0, velocity[channels:], velocity[:channels]).astype(BF16)
    for copy in load_all([(own_buf, own_ref), (sent_buf, sent_ref)], sem):
        copy.wait()


def project(state, modes, w_head, attended, pieces):
    rows, width = state.shape
    third = width // 4
    channels = w_head.shape[0] // 2
    return pl.pallas_call(
        out_kernel,
        out_shape=[shape_of(channels, rows, dtype=F32), shape_of(channels, rows)],
        in_specs=[ANY] * 15,
        out_specs=[ANY, ANY],
        scratch_shapes=[
            pltpu.VMEM((4, rows, third), BF16),
            pltpu.VMEM((rows, width), BF16),
            pltpu.VMEM((width, width), BF16),
            pltpu.VMEM(state.shape, BF16),
            pltpu.VMEM(modes.shape, F32),
            pltpu.VMEM(w_head.shape, BF16),
            pltpu.VMEM((channels, rows), F32),
            pltpu.VMEM((channels, rows), BF16),
            pltpu.SemaphoreType.DMA((15,)),
        ],
        compiler_params=params(),
        cost_estimate=cost(8e9, 1e6),
    )(state, modes, w_head, *attended, *pieces)


def updated_latent(own, outgoing, latent, guidance, step_size, length, position):
    rows = own.shape[1]
    branch = lax.axis_index("cfg")
    scale = guidance[0]
    other = lax.ppermute(outgoing, "cfg", SWAP).astype(own.dtype)
    cond = jnp.where(branch == 0, own, other)
    uncond = jnp.where(branch == 0, other, own)
    guided = uncond + scale * (cond - uncond)
    valid = position * rows + jnp.arange(rows, dtype=jnp.int32) < length
    current = latent[0].T
    updated = jnp.where(valid[None, :], current - step_size[0] * guided, current)
    return updated.T[None]


def after(value, *others):
    return lax.optimization_barrier((value, *others))[0]


def team_local(
    hidden, latent, modulation, w_qkv, w_out, q_gain, k_gain, w_head, lengths, guidance, step_size
):
    state = hidden[0, 0]
    modes = jnp.transpose(modulation, (1, 0, 2))
    rows, width = state.shape
    third = width // 4
    parts = lax.axis_size("req")
    up = [(2 * fold(i) + side, 2 * fold((i - 1) % 4) + side) for i in range(4) for side in range(2)]
    down = [(target, source) for source, target in up]
    beside = [(i, i ^ 1) for i in range(parts)]

    def along(piece):
        return lax.ppermute(piece, "req", up)

    def back(piece):
        return lax.ppermute(piece, "req", down)

    def across(piece):
        return lax.ppermute(piece, "req", beside)

    gains = jnp.stack([q_gain, k_gain])[:, None]
    columns, normed = entry(w_qkv, w_out, state, modes)
    normed_y = lax.ppermute(normed, "seq", SWAP)
    normed_c = lax.ppermute(normed, "cfg", SWAP)

    def step(mine, theirs, gates):
        now = after(mine[-1], *gates)
        mine.append(along(now))
        theirs.append(across(now))

    mine, theirs = [columns], []
    step(mine, theirs, [])
    cut, split = columns.shape[0] // 2, 3 * third
    low = theirs[0][cut:, :split]
    out_last = theirs[0][:, split:]
    gates = [mine[1], theirs[0], low, out_last, gains]
    step(mine, theirs, gates)
    gates = [mine[2], theirs[1]]
    step(mine, theirs, gates)
    out_last = back(after(out_last, *gates))
    early = [mine[0], theirs[0], mine[1], theirs[1]]
    packed = [pack(early, third)]
    normed_yc = lax.ppermute(normed_y, "cfg", SWAP)
    norms = [normed, normed_y, normed_c, normed_yc]
    packed_y = [lax.ppermute(packed[0], "seq", SWAP)]
    acc_qk, acc_v = first_part(norms, early)
    gates = [mine[3], theirs[2], out_last, packed_y[0], acc_v]
    upper = across(after(mine[3][:cut, :split], *gates))
    lower = back(after(low, *gates))
    late = [mine[2], theirs[2], mine[3], upper, lower]
    packed.append(pack([mine[2], theirs[2], mine[3], out_last], third))
    packed_y.append(lax.ppermute(packed[1], "seq", SWAP))
    packed_c = [lax.ppermute(part, "cfg", SWAP) for part in packed]
    packed_yc = [lax.ppermute(part, "cfg", SWAP) for part in packed_y]

    qk_full, sums = last_scores(norms, acc_qk, gains, late)
    v_full = last_values(norms, acc_v, late)
    diagonal = [(i, 3 - i) for i in range(4)]
    all_sums = [
        sums,
        lax.ppermute(sums, "seq", SWAP),
        lax.ppermute(sums, "cfg", SWAP),
        lax.ppermute(sums, ("cfg", "seq"), diagonal),
    ]
    v_full = after(v_full, packed_c[0], packed_yc[0])
    far = team_attention((1, 3), 6e9, lengths, qk_full, v_full, all_sums)
    far = lax.optimization_barrier((*far, packed_y[1], packed_c[1]))[:2]
    near = team_attention((2, 0), 1e6, lengths, after(qk_full, far[0]), v_full, all_sums)
    attended = [
        near[1],
        lax.ppermute(near[0], "cfg", SWAP),
        lax.ppermute(far[0], "seq", SWAP),
        lax.ppermute(far[1], ("cfg", "seq"), diagonal),
    ]
    quarters = [part[j] for j in range(2) for part in (packed, packed_c, packed_y, packed_yc)]
    own, outgoing = project(state, modes, w_head.T, attended, quarters)
    return updated_latent(own, outgoing, latent, guidance, step_size, lengths[0], lax.axis_index("seq"))


def by_team(mesh, arguments):
    hidden, w_qkv = arguments[0], arguments[3]
    sizes = mesh.shape
    width = hidden.shape[3]
    depth = w_qkv.shape[0] // sizes["req"]
    return (
        sizes["cfg"] == 2
        and sizes["seq"] == 2
        and sizes["req"] == 8
        and width % (4 * DH) == 0
        and 8 * depth == width
        and depth % 32 == 0
        and hidden.shape[2] // sizes["seq"] % 16 == 0
    )


def solution(mesh):
    def whole(*arguments):
        body = team_local if by_team(mesh, arguments) else ring_local
        return jax.shard_map(
            body,
            mesh=mesh,
            in_specs=(
                P("cfg", "req", "seq", None),
                P("req", "seq", "cfg"),
                P("req", None, None),
                P("req", None),
                P("req", None),
                P(),
                P(),
                P(),
                P("req"),
                P("req"),
                P("req"),
            ),
            out_specs=P("req", "seq", "cfg"),
            check_vma=False,
        )(*arguments)

    return whole
```

```python
import functools

import jax
import jax.numpy as jnp
from jax import lax
from jax.experimental import pallas as pl
from jax.experimental.pallas import tpu as pltpu
from jax.sharding import PartitionSpec as P

DH = 128
SWAP = [(0, 1), (1, 0)]
SMEM = pl.BlockSpec(memory_space=pltpu.SMEM)
ANY = pl.BlockSpec(memory_space=pl.ANY)
BF16 = jnp.bfloat16
F32 = jnp.float32


def params(megabytes):
    return pltpu.CompilerParams(vmem_limit_bytes=megabytes * 2**20)


def cost(flops, moved, exps=0):
    return pl.CostEstimate(flops=int(flops), bytes_accessed=int(moved), transcendentals=int(exps))


def shape_of(*dims, dtype=BF16):
    return jax.ShapeDtypeStruct(dims, dtype)


def times(left, right):
    return jnp.dot(left, right, preferred_element_type=F32)


def times_turned(left, right):
    return lax.dot_general(left, right, (((1,), (1,)), ((), ())), preferred_element_type=F32)


def passed_along(value, axis, steps):
    count = lax.axis_size(axis)
    pairs = [(source, (source + steps) % count) for source in range(count)]
    return lax.ppermute(value, axis, pairs)


def from_partner(value, axis, apart):
    mask = 2**apart
    pairs = [(source, source ^ mask) for source in range(lax.axis_size(axis))]
    return lax.ppermute(value, axis, pairs)


def layer_norm(values):
    centered = values - jnp.mean(values, axis=-1, keepdims=True)
    return centered / jnp.sqrt(jnp.mean(centered * centered, axis=-1, keepdims=True) + 1e-06)


def rms_gain(values, gain):
    return values / jnp.sqrt(jnp.mean(values * values, axis=-1, keepdims=True) + 1e-06) * gain


def add_rows(left, piece):
    return jnp.dot(left, piece, preferred_element_type=jnp.float32)


def attend(state, query, stacked, start, length):
    top, total, weighted = state
    keys = stacked[0]
    values = stacked[1]
    count = keys.shape[0]
    scores = jnp.einsum("qhd,khd->qhk", query, keys, preferred_element_type=jnp.float32) / jnp.sqrt(
        jnp.float32(query.shape[2])
    )
    valid = start + jnp.arange(count, dtype=jnp.int32) < length
    scores = jnp.where(valid[None, None, :], scores, jnp.float32(-1e30))
    new_top = jnp.maximum(top, jnp.max(scores, axis=-1))
    factor = jnp.exp(top - new_top)
    probs = jnp.where(valid[None, None, :], jnp.exp(scores - new_top[:, :, None]), jnp.float32(0.0))
    total = total * factor + jnp.sum(probs, axis=-1)
    weighted = weighted * factor[:, :, None] + jnp.einsum(
        "qhk,khd->qhd", probs.astype(jnp.bfloat16), values, preferred_element_type=jnp.float32
    )
    return (new_top, total, weighted)


def ring_local(
    hidden, latent, modulation, w_qkv, w_out, q_gain, k_gain, w_head, lengths, guidance, step_size
):
    state = hidden[0, 0]
    modes = modulation[0]
    length = lengths[0]
    rows = state.shape[0]
    width = state.shape[1]
    heads = q_gain.shape[0] // DH
    wide = state.astype(jnp.float32)
    normed = (layer_norm(wide) * (1.0 + modes[1]) + modes[0]).astype(jnp.bfloat16)
    qkv = add_rows(normed, lax.all_gather(w_qkv, "req", axis=0, tiled=True))
    query = rms_gain(qkv[:, :width], q_gain).astype(jnp.bfloat16).reshape(rows, heads, DH)
    keys = rms_gain(qkv[:, width : 2 * width], k_gain).astype(jnp.bfloat16).reshape(rows, heads, DH)
    values = qkv[:, 2 * width :].astype(jnp.bfloat16).reshape(rows, heads, DH)
    stacked = jnp.stack([keys, values])
    position = lax.axis_index("seq")
    members = lax.axis_size("seq")
    start_state = (
        jnp.full((rows, heads), -1e30, jnp.float32),
        jnp.zeros((rows, heads), jnp.float32),
        jnp.zeros((rows, heads, DH), jnp.float32),
    )
    first = attend(start_state, query, stacked, position * rows, length)

    def cycle_step(turn, carry):
        moving, inner = carry
        moving = passed_along(moving, "seq", 1)
        source = (position - turn) % members
        return (moving, attend(inner, query, moving, source * rows, length))

    moved, result = lax.fori_loop(1, members, cycle_step, (stacked, first))
    top, total, weighted = result
    attended = (weighted / total[:, :, None]).reshape(rows, width).astype(jnp.bfloat16)
    projected = add_rows(attended, lax.all_gather(w_out, "req", axis=0, tiled=True))
    block_out = (wide + modes[2] * projected).astype(jnp.bfloat16)
    head_in = (layer_norm(block_out.astype(jnp.float32)) * (1.0 + modes[4]) + modes[3]).astype(
        jnp.bfloat16
    )
    velocity = jnp.dot(head_in, w_head, preferred_element_type=jnp.float32)
    branch = lax.axis_index("cfg")
    scale = guidance[0]
    channels = velocity.shape[1] // 2
    own = lax.dynamic_slice_in_dim(velocity, branch * channels, channels, 1)
    outgoing = lax.dynamic_slice_in_dim(velocity, (1 - branch) * channels, channels, 1)
    other = from_partner(outgoing.astype(jnp.bfloat16), "cfg", 0).astype(outgoing.dtype)
    cond = jnp.where(branch == 0, own, other)
    uncond = jnp.where(branch == 0, other, own)
    guided = uncond + scale * (cond - uncond)
    valid = position * rows + jnp.arange(rows, dtype=jnp.int32) < length
    current = latent[0]
    updated = jnp.where(valid[:, None], current - step_size[0] * guided, current)
    return updated[None]


def load_all(pairs, sem):
    copies = [pltpu.make_async_copy(source, target, sem.at[j]) for j, (source, target) in enumerate(pairs)]
    for copy in copies:
        copy.start()
    return copies


def fold(pair):
    return pair ^ (pair // 2)


def places():
    place = lax.axis_index("req")
    group = 2 * lax.axis_index("seq") + lax.axis_index("cfg")
    return lax.rem(place, 2), fold(place // 2), lax.axis_size("req") // 2, group


def window(j, size):
    return pl.ds(pl.multiple_of(j * size, size), size)


def scaled_norm(values, shift, scale):
    centered = values - jnp.mean(values, axis=-1, keepdims=True)
    inverse = lax.rsqrt(jnp.mean(centered * centered, axis=-1, keepdims=True) + 1e-06)
    return centered * inverse * (1.0 + scale) + shift


def entry_kernel(qkv_ref, w_out_ref, state_ref, modes_ref, cut_ref, norm_ref, *scratch):
    cut_buf, state_in, modes_in, full_ref, norm_buf, sem, out_sem = scratch
    side, pair, steps, group = places()
    third = cut_ref.shape[1] // 4
    loads = [(state_ref, state_in), (modes_ref, modes_in)]
    for j in range(3):
        loads.append((qkv_ref.at[:, window(4 * j + group, third)], cut_buf.at[:, j * third : (j + 1) * third]))
    loads.append((w_out_ref.at[:, window(group, third)], cut_buf.at[:, 3 * third :]))
    loads = load_all(loads, sem)
    for copy in loads[:2]:
        copy.wait()
    full_ref[...] = scaled_norm(state_in[...].astype(F32), modes_in[0], modes_in[1])
    for copy in loads[2:]:
        copy.wait()
    stores = [pltpu.make_async_copy(cut_buf, cut_ref, out_sem.at[0])]
    stores[0].start()
    count = 4
    for k in range(count):
        part = full_ref[:, window(fold(lax.rem(pair + k, steps)), third)]
        part = jnp.where(side == 0, part, pltpu.roll(part, third // 2, 1))
        norm_buf[:, k * third : (k + 1) * third] = part.astype(BF16)
    stores.append(pltpu.make_async_copy(norm_buf, norm_ref, out_sem.at[1]))
    stores[1].start()
    for copy in stores:
        copy.wait()


def entry(w_qkv, w_out, state, modes):
    return pl.pallas_call(
        entry_kernel,
        out_shape=[shape_of(*w_out.shape), shape_of(*state.shape)],
        in_specs=[ANY] * 4,
        out_specs=[ANY, ANY],
        scratch_shapes=[
            pltpu.VMEM(w_out.shape, BF16),
            pltpu.VMEM(state.shape, BF16),
            pltpu.VMEM(modes.shape, F32),
            pltpu.VMEM(state.shape, F32),
            pltpu.VMEM(state.shape, BF16),
            pltpu.SemaphoreType.DMA((6,)),
            pltpu.SemaphoreType.DMA((2,)),
        ],
        compiler_params=params(60),
        cost_estimate=cost(4e9, 1e6),
    )(w_qkv, w_out, state, modes)


def pack_kernel(count, *refs):
    pieces, packed_ref, held_ref, sem = refs[:count], refs[count], refs[count + 1], refs[count + 2]
    depth = held_ref.shape[0] // count
    columns = held_ref.shape[1]
    pairs = []
    for k, piece in enumerate(pieces):
        pairs.append((piece.at[:, piece.shape[1] - columns :], held_ref.at[k * depth : (k + 1) * depth]))
    for copy in load_all(pairs, sem):
        copy.wait()
    for copy in load_all([(held_ref, packed_ref)], sem):
        copy.wait()


def pack(pieces, columns):
    depth = pieces[0].shape[0]
    full = shape_of(depth * len(pieces), columns)
    return pl.pallas_call(
        functools.partial(pack_kernel, len(pieces)),
        out_shape=full,
        in_specs=[ANY] * len(pieces),
        out_specs=ANY,
        scratch_shapes=[pltpu.VMEM(full.shape, BF16), pltpu.SemaphoreType.DMA((len(pieces),))],
        compiler_params=params(40),
        cost_estimate=cost(3e9, 1e6),
    )(*pieces)


def rows_of(piece_refs, held_ref, start=0):
    found, at = [], 0
    for piece in piece_refs:
        rows = piece.shape[0]
        source = piece.at[:, start : start + held_ref.shape[1]]
        found.append((source, held_ref.at[at : at + rows]))
        at += rows
    return found


def first_kernel(count, *refs):
    norms, pieces = refs[:4], refs[4 : 4 + count]
    qk_ref, v_ref = refs[4 + count : 6 + count]
    left_ref, held_ref, qk_out, v_out, sem, out_sem = refs[6 + count :]
    deep, columns = held_ref.shape
    split = 2 * columns // 3
    loads = load_all(
        rows_of(pieces, held_ref) + [(norms[b].at[:, :deep], left_ref.at[b]) for b in range(4)], sem
    )
    for copy in loads:
        copy.wait()
    stores = []
    for block in range(4):
        qk_out[block] = times(left_ref[block], held_ref[:, :split]).astype(BF16)
        v_out[block] = times(left_ref[block], held_ref[:, split:]).astype(BF16)
        for j, (source, target) in enumerate(((qk_out, qk_ref), (v_out, v_ref))):
            copy = pltpu.make_async_copy(source.at[block], target.at[block], out_sem.at[2 * block + j])
            copy.start()
            stores.append(copy)
    for copy in stores:
        copy.wait()


def first_part(norms, pieces):
    rows = norms[0].shape[0]
    columns = 3 * norms[0].shape[1] // 4
    deep = sum(piece.shape[0] for piece in pieces)
    qk = shape_of(4, rows, 2 * columns // 3)
    v = shape_of(4, rows, columns // 3)
    return pl.pallas_call(
        functools.partial(first_kernel, len(pieces)),
        out_shape=[qk, v],
        in_specs=[ANY] * (4 + len(pieces)),
        out_specs=[ANY] * 2,
        scratch_shapes=[
            pltpu.VMEM((4, rows, deep), BF16),
            pltpu.VMEM((deep, columns), BF16),
            pltpu.VMEM(qk.shape, BF16),
            pltpu.VMEM(v.shape, BF16),
            pltpu.SemaphoreType.DMA((4 + len(pieces),)),
            pltpu.SemaphoreType.DMA((8,)),
        ],
        compiler_params=params(40),
        cost_estimate=cost(6e9, 1e6),
    )(*norms, *pieces)


def scores_kernel(count, *refs):
    norms, acc_ref, gains_ref, pieces = refs[:4], refs[4], refs[5], refs[6 : 6 + count]
    out_ref, sums_ref, left_ref, held_ref, acc_in, gains_in, out_buf, sums_buf, sem, rest_sem, out_sem = refs[6 + count :]
    deep = held_ref.shape[0]
    third = out_ref.shape[2] // 2
    width = norms[0].shape[1]
    first = [(norms[0].at[:, width - deep :], left_ref.at[0]), (acc_ref.at[0], acc_in.at[0])]
    loads = load_all(rows_of(pieces, held_ref) + [(gains_ref, gains_in)] + first, sem)
    mine = window(places()[3], third)
    row = lax.broadcasted_iota(jnp.int32, (8, 4 * DH), 0)
    lane = lax.broadcasted_iota(jnp.int32, (8, 4 * DH), 1)
    pick = (row == lane // (2 * DH)).astype(BF16)
    for copy in loads:
        copy.wait()
    rest = []
    for b in range(1, 4):
        rest += [(norms[b].at[:, width - deep :], left_ref.at[b]), (acc_ref.at[b], acc_in.at[b])]
    loads = load_all(rest, rest_sem)
    gains = [gains_in[0, :, mine] * (1.4426950408889634 / DH**0.5), gains_in[1, :, mine]]
    stores = []
    for block in range(4):
        if block:
            loads[2 * block - 2].wait()
            loads[2 * block - 1].wait()
        product = times(left_ref[block], held_ref[...])
        squares = []
        for j in range(2):
            square = 0.0
            for h in range(third // DH):
                at = slice(j * third + h * DH, j * third + (h + 1) * DH)
                part = acc_in[block, :, at].astype(F32) + product[:, at]
                square += part * part
                out_buf[block, :, at] = (part * gains[j][:, h * DH : (h + 1) * DH]).astype(BF16)
            high = square.astype(BF16)
            squares += [high, (square - high.astype(F32)).astype(BF16)]
        stores.append(pltpu.make_async_copy(out_buf.at[block], out_ref.at[block], out_sem.at[block]))
        stores[-1].start()
        sums_buf[block] = times_turned(pick, jnp.concatenate(squares, axis=1))
    stores.append(pltpu.make_async_copy(sums_buf, sums_ref, out_sem.at[4]))
    stores[-1].start()
    for copy in stores:
        copy.wait()


def last_scores(norms, acc, gains, pieces):
    rows = norms[0].shape[0]
    columns = acc.shape[2]
    deep = sum(piece.shape[0] for piece in pieces)
    return pl.pallas_call(
        functools.partial(scores_kernel, len(pieces)),
        out_shape=[shape_of(4, rows, columns), shape_of(4, 8, rows, dtype=F32)],
        in_specs=[ANY] * (6 + len(pieces)),
        out_specs=[ANY, ANY],
        scratch_shapes=[
            pltpu.VMEM((4, rows, deep), BF16),
            pltpu.VMEM((deep, columns), BF16),
            pltpu.VMEM(acc.shape, BF16),
            pltpu.VMEM(gains.shape, F32),
            pltpu.VMEM(acc.shape, BF16),
            pltpu.VMEM((4, 8, rows), F32),
            pltpu.SemaphoreType.DMA((3 + len(pieces),)),
            pltpu.SemaphoreType.DMA((6,)),
            pltpu.SemaphoreType.DMA((5,)),
        ],
        compiler_params=params(48),
        cost_estimate=cost(6e9, 1e6),
    )(*norms, acc, gains, *pieces)


def values_kernel(count, *refs):
    norms, acc_ref, pieces = refs[:4], refs[4], refs[5 : 5 + count]
    out_ref, left_ref, held_ref, acc_in, out_buf, sem = refs[5 + count :]
    deep, columns = held_ref.shape
    width = norms[0].shape[1]
    loads = load_all(
        rows_of(pieces, held_ref, 2 * columns)
        + [(norms[b].at[:, width - deep :], left_ref.at[b]) for b in range(4)]
        + [(acc_ref.at[b], acc_in.at[b]) for b in range(4)],
        sem,
    )
    for copy in loads[:count]:
        copy.wait()
    stores = []
    for block in range(4):
        loads[count + block].wait()
        product = times(left_ref[block], held_ref[...])
        loads[count + 4 + block].wait()
        out_buf[block] = (acc_in[block].astype(F32) + product).astype(BF16)
        stores.append(pltpu.make_async_copy(out_buf.at[block], out_ref.at[block], sem.at[block]))
        stores[-1].start()
    for copy in stores:
        copy.wait()


def last_values(norms, acc, pieces):
    rows = norms[0].shape[0]
    columns = acc.shape[2]
    deep = sum(piece.shape[0] for piece in pieces)
    return pl.pallas_call(
        functools.partial(values_kernel, len(pieces)),
        out_shape=shape_of(4, rows, columns),
        in_specs=[ANY] * 5 + [ANY] * len(pieces),
        out_specs=ANY,
        scratch_shapes=[
            pltpu.VMEM((4, rows, deep), BF16),
            pltpu.VMEM((deep, columns), BF16),
            pltpu.VMEM(acc.shape, BF16),
            pltpu.VMEM(acc.shape, BF16),
            pltpu.SemaphoreType.DMA((8 + len(pieces),)),
        ],
        compiler_params=params(48),
        cost_estimate=cost(4e9, 1e6),
    )(*norms, acc, *pieces)


def heads_kernel(blocks, length_ref, qk_ref, v_ref, s0_ref, s1_ref, s2_ref, s3_ref, *refs):
    outs = refs[:2]
    qk_in, v_in, sums_in, out_buf, sem, out_sem = refs[2:]
    rows = qk_ref.shape[1]
    third = qk_ref.shape[2] // 2
    count = third // DH
    width = 4 * third
    sum_refs = (s0_ref, s1_ref, s2_ref, s3_ref)
    loads = [(sum_refs[j], sums_in.at[j]) for j in range(4)]
    order = [b for block in blocks for b in (block - block % 2, block - block % 2 + 1)]
    for b in order:
        loads.append((qk_ref.at[b], qk_in.at[b]))
    for b in order:
        held = v_in.at[b // 2, b % 2 * rows : (b % 2 + 1) * rows]
        for h in range(count):
            loads.append((v_ref.at[b, :, h * DH : (h + 1) * DH], held.at[:, 2 * h * DH : (2 * h + 1) * DH]))
    loads = load_all(loads, sem)
    for b in range(2):
        for h in range(count):
            v_in[b, :, (2 * h + 1) * DH : (2 * h + 2) * DH] = jnp.ones((2 * rows, DH), BF16)
    row = lax.broadcasted_iota(jnp.int32, (24, DH), 0)
    pick = (row % 8 == 0).astype(BF16)
    place = lax.broadcasted_iota(jnp.int32, (1, rows), 1)
    position = lax.axis_index("seq")
    masks = [place < length_ref[0] - (j + position - 2 * j * position) * rows for j in range(2)]
    for copy in loads[:4]:
        copy.wait()
    scale_q, scale_k = {}, {}
    for block in range(4):
        sums = sums_in[0, block] + sums_in[1, block ^ 1] + sums_in[2, block ^ 2] + sums_in[3, block ^ 3]
        inverse = lax.rsqrt(sums * (1.0 / width) + 1e-06)
        scale_k[block] = inverse[1:2, :]
        if block in blocks:
            high = inverse.astype(BF16).astype(F32)
            middle = (inverse - high).astype(BF16).astype(F32)
            stacked = jnp.concatenate([high, middle, inverse - high - middle], axis=0).astype(BF16)
            turned = lax.dot_general(stacked, pick, (((0,), (0,)), ((), ())), preferred_element_type=F32)
            scale_q[block] = turned[:, :1]
    items = [(at, block, h) for at, block in enumerate(blocks) for h in range(count)]

    def scores_of(at, block, h):
        if h == 0:
            for copy in loads[4 + 2 * at : 6 + 2 * at]:
                copy.wait()
        first = block - block % 2
        query = qk_in[block, :, h * DH : (h + 1) * DH]
        found = []
        for j in range(2):
            keys = qk_in[first + j, :, third + h * DH : third + (h + 1) * DH]
            part = times_turned(query, keys) * scale_k[first + j]
            found.append(jnp.where(masks[j], part, -1e30))
        return found

    stores = []
    ahead = scores_of(*items[0])
    for turn, (at, block, h) in enumerate(items):
        scores = ahead
        if turn + 1 < len(items):
            ahead = scores_of(*items[turn + 1])
        if h == 0:
            for copy in loads[8 + 2 * count * at : 8 + 2 * count * (at + 1)]:
                copy.wait()
        top = jnp.maximum(
            jnp.max(scores[0], axis=-1, keepdims=True), jnp.max(scores[1], axis=-1, keepdims=True)
        )
        weighted = 0.0
        for j in range(2):
            probs = jnp.exp2((scores[j] - top) * scale_q[block]).astype(BF16)
            values = v_in[block // 2, j * rows : (j + 1) * rows, 2 * h * DH : (2 * h + 2) * DH]
            weighted += times(probs, values)
        out_buf[at, :, h * DH : (h + 1) * DH] = (weighted[:, :DH] / weighted[:, DH:]).astype(BF16)
        if h == count - 1:
            stores.append(pltpu.make_async_copy(out_buf.at[at], outs[at], out_sem.at[at]))
            stores[-1].start()
    for copy in stores:
        copy.wait()


def team_attention(blocks, effort, length, qk, v, sums):
    rows = qk.shape[1]
    third = qk.shape[2] // 2
    count = third // DH
    return pl.pallas_call(
        functools.partial(heads_kernel, blocks),
        out_shape=[shape_of(rows, third)] * 2,
        in_specs=[SMEM] + [ANY] * 6,
        out_specs=[ANY] * 2,
        scratch_shapes=[
            pltpu.VMEM(qk.shape, BF16),
            pltpu.VMEM((2, 2 * rows, 2 * third), BF16),
            pltpu.VMEM((4, 4, 8, rows), F32),
            pltpu.VMEM((2, rows, third), BF16),
            pltpu.SemaphoreType.DMA((8 + 4 * count,)),
            pltpu.SemaphoreType.DMA((2,)),
        ],
        compiler_params=params(50),
        cost_estimate=cost(effort, 1e6),
    )(length, qk, v, *sums)


def out_kernel(state_ref, modes_ref, head_ref, *refs):
    attended, pieces = refs[:4], refs[4:12]
    own_ref, sent_ref = refs[12:14]
    att_in, group_ref, held_ref, state_in, modes_in, head_in_ref, own_buf, sent_buf, sem = refs[14:]
    side, pair, steps, own = places()
    third = attended[0].shape[1]
    half = pieces[0].shape[0]
    loads = load_all(
        [(attended[j], att_in.at[j]) for j in range(4)]
        + [(pieces[j], held_ref.at[:half, window(own ^ j, third)]) for j in range(4)]
        + [(pieces[4 + j], held_ref.at[half:, window(own ^ j, third)]) for j in range(4)]
        + [(state_ref, state_in), (modes_ref, modes_in), (head_ref, head_in_ref)],
        sem,
    )
    for j in range(4):
        loads[j].wait()
        part = att_in[j].astype(F32)
        part = jnp.where(side == 0, part, pltpu.roll(part, third // 2, 1)).astype(BF16)
        group_ref[:, window(lax.rem(fold(own ^ j) + steps - pair, steps), third)] = part
    for copy in loads[4:8]:
        copy.wait()
    total = times(group_ref[:, :half], held_ref[:half, :])
    for copy in loads[8:]:
        copy.wait()
    total += times(group_ref[:, half:], held_ref[half:, :])
    block_out = (state_in[...].astype(F32) + modes_in[2] * total).astype(BF16)
    head_in = scaled_norm(block_out.astype(F32), modes_in[3], modes_in[4])
    velocity = times_turned(head_in_ref[...], head_in.astype(BF16))
    channels = own_buf.shape[0]
    core = lax.axis_index("cfg")
    own_buf[...] = jnp.where(core == 0, velocity[:channels], velocity[channels:])
    sent_buf[...] = jnp.where(core == 0, velocity[channels:], velocity[:channels]).astype(BF16)
    for copy in load_all([(own_buf, own_ref), (sent_buf, sent_ref)], sem):
        copy.wait()


def project(state, modes, w_head, attended, pieces):
    rows, width = state.shape
    third = width // 4
    channels = w_head.shape[0] // 2
    return pl.pallas_call(
        out_kernel,
        out_shape=[shape_of(channels, rows, dtype=F32), shape_of(channels, rows)],
        in_specs=[ANY] * 15,
        out_specs=[ANY, ANY],
        scratch_shapes=[
            pltpu.VMEM((4, rows, third), BF16),
            pltpu.VMEM((rows, width), BF16),
            pltpu.VMEM((width, width), BF16),
            pltpu.VMEM(state.shape, BF16),
            pltpu.VMEM(modes.shape, F32),
            pltpu.VMEM(w_head.shape, BF16),
            pltpu.VMEM((channels, rows), F32),
            pltpu.VMEM((channels, rows), BF16),
            pltpu.SemaphoreType.DMA((15,)),
        ],
        compiler_params=params(50),
        cost_estimate=cost(8e9, 1e6),
    )(state, modes, w_head, *attended, *pieces)


def updated_latent(own, outgoing, latent, guidance, step_size, length, position):
    rows = own.shape[1]
    branch = lax.axis_index("cfg")
    scale = guidance[0]
    other = lax.ppermute(outgoing, "cfg", SWAP).astype(own.dtype)
    cond = jnp.where(branch == 0, own, other)
    uncond = jnp.where(branch == 0, other, own)
    guided = uncond + scale * (cond - uncond)
    valid = position * rows + jnp.arange(rows, dtype=jnp.int32) < length
    current = latent[0].T
    updated = jnp.where(valid[None, :], current - step_size[0] * guided, current)
    return updated.T[None]


def after(value, *others):
    return lax.optimization_barrier((value, *others))[0]


def team_local(
    hidden, latent, modulation, w_qkv, w_out, q_gain, k_gain, w_head, lengths, guidance, step_size
):
    state = hidden[0, 0]
    modes = jnp.transpose(modulation, (1, 0, 2))
    rows, width = state.shape
    third = width // 4
    parts = lax.axis_size("req")
    up = [(2 * fold(i) + side, 2 * fold((i - 1) % 4) + side) for i in range(4) for side in range(2)]
    down = [(target, source) for source, target in up]
    beside = [(i, i ^ 1) for i in range(parts)]

    def along(piece):
        return lax.ppermute(piece, "req", up)

    def back(piece):
        return lax.ppermute(piece, "req", down)

    def across(piece):
        return lax.ppermute(piece, "req", beside)

    gains = jnp.stack([q_gain, k_gain])[:, None]
    columns, normed = entry(w_qkv, w_out, state, modes)
    normed_y = lax.ppermute(normed, "seq", SWAP)
    normed_c = lax.ppermute(normed, "cfg", SWAP)

    def step(mine, theirs, gates):
        now = after(mine[-1], *gates)
        mine.append(along(now))
        theirs.append(across(now))

    mine, theirs = [columns], []
    step(mine, theirs, [])
    cut, split = columns.shape[0] // 2, 3 * third
    low = theirs[0][cut:, :split]
    out_last = theirs[0][:, split:]
    gates = [mine[1], theirs[0], low, out_last, gains]
    step(mine, theirs, gates)
    gates = [mine[2], theirs[1]]
    step(mine, theirs, gates)
    out_last = back(after(out_last, *gates))
    early = [mine[0], theirs[0], mine[1], theirs[1]]
    packed = [pack(early, third)]
    normed_yc = lax.ppermute(normed_y, "cfg", SWAP)
    norms = [normed, normed_y, normed_c, normed_yc]
    packed_y = [lax.ppermute(packed[0], "seq", SWAP)]
    acc_qk, acc_v = first_part(norms, early)
    gates = [mine[3], theirs[2], out_last, packed_y[0], acc_v]
    upper = across(after(mine[3][:cut, :split], *gates))
    lower = back(after(low, *gates))
    late = [mine[2], theirs[2], mine[3], upper, lower]
    packed.append(pack([mine[2], theirs[2], mine[3], out_last], third))
    packed_y.append(lax.ppermute(packed[1], "seq", SWAP))
    packed_c = [lax.ppermute(part, "cfg", SWAP) for part in packed]
    packed_yc = [lax.ppermute(part, "cfg", SWAP) for part in packed_y]

    qk_full, sums = last_scores(norms, acc_qk, gains, late)
    v_full = last_values(norms, acc_v, late)
    diagonal = [(i, 3 - i) for i in range(4)]
    all_sums = [
        sums,
        lax.ppermute(sums, "seq", SWAP),
        lax.ppermute(sums, "cfg", SWAP),
        lax.ppermute(sums, ("cfg", "seq"), diagonal),
    ]
    v_full = after(v_full, packed_c[0], packed_yc[0])
    far = team_attention((1, 3), 6e9, lengths, qk_full, v_full, all_sums)
    far = lax.optimization_barrier((*far, packed_y[1], packed_c[1]))[:2]
    near = team_attention((2, 0), 1e6, lengths, after(qk_full, far[0]), v_full, all_sums)
    attended = [
        near[1],
        lax.ppermute(near[0], "cfg", SWAP),
        lax.ppermute(far[0], "seq", SWAP),
        lax.ppermute(far[1], ("cfg", "seq"), diagonal),
    ]
    quarters = [part[j] for j in range(2) for part in (packed, packed_c, packed_y, packed_yc)]
    own, outgoing = project(state, modes, w_head.T, attended, quarters)
    return updated_latent(own, outgoing, latent, guidance, step_size, lengths[0], lax.axis_index("seq"))


def by_team(mesh, arguments):
    hidden, w_qkv = arguments[0], arguments[3]
    sizes = mesh.shape
    width = hidden.shape[3]
    depth = w_qkv.shape[0] // sizes["req"]
    return (
        sizes["cfg"] == 2
        and sizes["seq"] == 2
        and sizes["req"] == 8
        and width % (4 * DH) == 0
        and 8 * depth == width
        and depth % 32 == 0
        and hidden.shape[2] // sizes["seq"] % 16 == 0
    )


def solution(mesh):
    def whole(*arguments):
        body = team_local if by_team(mesh, arguments) else ring_local
        return jax.shard_map(
            body,
            mesh=mesh,
            in_specs=(
                P("cfg", "req", "seq", None),
                P("req", "seq", "cfg"),
                P("req", None, None),
                P("req", None),
                P("req", None),
                P(),
                P(),
                P(),
                P("req"),
                P("req"),
                P("req"),
            ),
            out_specs=P("req", "seq", "cfg"),
            check_vma=False,
        )(*arguments)

    return whole
```

```python
import functools

import jax
import jax.numpy as jnp
from jax import lax
from jax.experimental import pallas as pl
from jax.experimental.pallas import tpu as pltpu
from jax.sharding import PartitionSpec as P

DH = 128
SWAP = [(0, 1), (1, 0)]
VMEM = pl.BlockSpec(memory_space=pltpu.VMEM)
SMEM = pl.BlockSpec(memory_space=pltpu.SMEM)
ANY = pl.BlockSpec(memory_space=pl.ANY)
BF16 = jnp.bfloat16
F32 = jnp.float32


def params(megabytes):
    return pltpu.CompilerParams(vmem_limit_bytes=megabytes * 2**20)


def cost(flops, moved, exps=0):
    return pl.CostEstimate(flops=int(flops), bytes_accessed=int(moved), transcendentals=int(exps))


def shape_of(*dims, dtype=BF16):
    return jax.ShapeDtypeStruct(dims, dtype)


def times(left, right):
    return jnp.dot(left, right, preferred_element_type=F32)


def times_turned(left, right):
    return lax.dot_general(left, right, (((1,), (1,)), ((), ())), preferred_element_type=F32)


def passed_along(value, axis, steps):
    count = lax.axis_size(axis)
    pairs = [(source, (source + steps) % count) for source in range(count)]
    return lax.ppermute(value, axis, pairs)


def from_partner(value, axis, apart):
    mask = 2**apart
    pairs = [(source, source ^ mask) for source in range(lax.axis_size(axis))]
    return lax.ppermute(value, axis, pairs)


def layer_norm(values):
    centered = values - jnp.mean(values, axis=-1, keepdims=True)
    return centered / jnp.sqrt(jnp.mean(centered * centered, axis=-1, keepdims=True) + 1e-06)


def rms_gain(values, gain):
    return values / jnp.sqrt(jnp.mean(values * values, axis=-1, keepdims=True) + 1e-06) * gain


def add_rows(left, piece):
    return jnp.dot(left, piece, preferred_element_type=jnp.float32)


def attend(state, query, stacked, start, length):
    top, total, weighted = state
    keys = stacked[0]
    values = stacked[1]
    count = keys.shape[0]
    scores = jnp.einsum("qhd,khd->qhk", query, keys, preferred_element_type=jnp.float32) / jnp.sqrt(
        jnp.float32(query.shape[2])
    )
    valid = start + jnp.arange(count, dtype=jnp.int32) < length
    scores = jnp.where(valid[None, None, :], scores, jnp.float32(-1e30))
    new_top = jnp.maximum(top, jnp.max(scores, axis=-1))
    factor = jnp.exp(top - new_top)
    probs = jnp.where(valid[None, None, :], jnp.exp(scores - new_top[:, :, None]), jnp.float32(0.0))
    total = total * factor + jnp.sum(probs, axis=-1)
    weighted = weighted * factor[:, :, None] + jnp.einsum(
        "qhk,khd->qhd", probs.astype(jnp.bfloat16), values, preferred_element_type=jnp.float32
    )
    return (new_top, total, weighted)


def ring_local(
    hidden, latent, modulation, w_qkv, w_out, q_gain, k_gain, w_head, lengths, guidance, step_size
):
    state = hidden[0, 0]
    modes = modulation[0]
    length = lengths[0]
    rows = state.shape[0]
    width = state.shape[1]
    heads = q_gain.shape[0] // DH
    wide = state.astype(jnp.float32)
    normed = (layer_norm(wide) * (1.0 + modes[1]) + modes[0]).astype(jnp.bfloat16)
    qkv = add_rows(normed, lax.all_gather(w_qkv, "req", axis=0, tiled=True))
    query = rms_gain(qkv[:, :width], q_gain).astype(jnp.bfloat16).reshape(rows, heads, DH)
    keys = rms_gain(qkv[:, width : 2 * width], k_gain).astype(jnp.bfloat16).reshape(rows, heads, DH)
    values = qkv[:, 2 * width :].astype(jnp.bfloat16).reshape(rows, heads, DH)
    stacked = jnp.stack([keys, values])
    position = lax.axis_index("seq")
    members = lax.axis_size("seq")
    start_state = (
        jnp.full((rows, heads), -1e30, jnp.float32),
        jnp.zeros((rows, heads), jnp.float32),
        jnp.zeros((rows, heads, DH), jnp.float32),
    )
    first = attend(start_state, query, stacked, position * rows, length)

    def cycle_step(turn, carry):
        moving, inner = carry
        moving = passed_along(moving, "seq", 1)
        source = (position - turn) % members
        return (moving, attend(inner, query, moving, source * rows, length))

    moved, result = lax.fori_loop(1, members, cycle_step, (stacked, first))
    top, total, weighted = result
    attended = (weighted / total[:, :, None]).reshape(rows, width).astype(jnp.bfloat16)
    projected = add_rows(attended, lax.all_gather(w_out, "req", axis=0, tiled=True))
    block_out = (wide + modes[2] * projected).astype(jnp.bfloat16)
    head_in = (layer_norm(block_out.astype(jnp.float32)) * (1.0 + modes[4]) + modes[3]).astype(
        jnp.bfloat16
    )
    velocity = jnp.dot(head_in, w_head, preferred_element_type=jnp.float32)
    branch = lax.axis_index("cfg")
    scale = guidance[0]
    channels = velocity.shape[1] // 2
    own = lax.dynamic_slice_in_dim(velocity, branch * channels, channels, 1)
    outgoing = lax.dynamic_slice_in_dim(velocity, (1 - branch) * channels, channels, 1)
    other = from_partner(outgoing.astype(jnp.bfloat16), "cfg", 0).astype(outgoing.dtype)
    cond = jnp.where(branch == 0, own, other)
    uncond = jnp.where(branch == 0, other, own)
    guided = uncond + scale * (cond - uncond)
    valid = position * rows + jnp.arange(rows, dtype=jnp.int32) < length
    current = latent[0]
    updated = jnp.where(valid[:, None], current - step_size[0] * guided, current)
    return updated[None]


def load_all(pairs, sem):
    copies = [pltpu.make_async_copy(source, target, sem.at[j]) for j, (source, target) in enumerate(pairs)]
    for copy in copies:
        copy.start()
    return copies


def fold(pair):
    return pair ^ (pair // 2)


def places():
    place = lax.axis_index("req")
    group = 2 * lax.axis_index("seq") + lax.axis_index("cfg")
    return lax.rem(place, 2), fold(place // 2), lax.axis_size("req") // 2, group


def window(j, size):
    return pl.ds(pl.multiple_of(j * size, size), size)


def scaled_norm(values, shift, scale):
    centered = values - jnp.mean(values, axis=-1, keepdims=True)
    inverse = lax.rsqrt(jnp.mean(centered * centered, axis=-1, keepdims=True) + 1e-06)
    return centered * inverse * (1.0 + scale) + shift


def entry_kernel(qkv_ref, w_out_ref, state_ref, modes_ref, cut_ref, norm_ref, *scratch):
    cut_buf, state_in, modes_in, full_ref, norm_buf, sem, out_sem = scratch
    side, pair, steps, group = places()
    third = cut_ref.shape[1] // 4
    loads = [(state_ref, state_in), (modes_ref, modes_in)]
    for j in range(3):
        loads.append((qkv_ref.at[:, window(4 * j + group, third)], cut_buf.at[:, j * third : (j + 1) * third]))
    loads.append((w_out_ref.at[:, window(group, third)], cut_buf.at[:, 3 * third :]))
    loads = load_all(loads, sem)
    for copy in loads[:2]:
        copy.wait()
    full_ref[...] = scaled_norm(state_in[...].astype(F32), modes_in[0], modes_in[1])
    for copy in loads[2:]:
        copy.wait()
    stores = [pltpu.make_async_copy(cut_buf, cut_ref, out_sem.at[0])]
    stores[0].start()
    count = 4
    for k in range(count):
        part = full_ref[:, window(fold(lax.rem(pair + k, steps)), third)]
        part = jnp.where(side == 0, part, pltpu.roll(part, third // 2, 1))
        norm_buf[:, k * third : (k + 1) * third] = part.astype(BF16)
    stores.append(pltpu.make_async_copy(norm_buf, norm_ref, out_sem.at[1]))
    stores[1].start()
    for copy in stores:
        copy.wait()


def entry(w_qkv, w_out, state, modes):
    return pl.pallas_call(
        entry_kernel,
        out_shape=[shape_of(*w_out.shape), shape_of(*state.shape)],
        in_specs=[ANY] * 4,
        out_specs=[ANY, ANY],
        scratch_shapes=[
            pltpu.VMEM(w_out.shape, BF16),
            pltpu.VMEM(state.shape, BF16),
            pltpu.VMEM(modes.shape, F32),
            pltpu.VMEM(state.shape, F32),
            pltpu.VMEM(state.shape, BF16),
            pltpu.SemaphoreType.DMA((6,)),
            pltpu.SemaphoreType.DMA((2,)),
        ],
        compiler_params=params(60),
        cost_estimate=cost(4e9, 1e6),
    )(w_qkv, w_out, state, modes)


def pack_kernel(count, *refs):
    pieces, packed_ref, held_ref, sem = refs[:count], refs[count], refs[count + 1], refs[count + 2]
    depth = held_ref.shape[0] // count
    columns = held_ref.shape[1]
    pairs = []
    for k, piece in enumerate(pieces):
        pairs.append((piece.at[:, piece.shape[1] - columns :], held_ref.at[k * depth : (k + 1) * depth]))
    for copy in load_all(pairs, sem):
        copy.wait()
    for copy in load_all([(held_ref, packed_ref)], sem):
        copy.wait()


def pack(pieces, columns):
    depth = pieces[0].shape[0]
    full = shape_of(depth * len(pieces), columns)
    return pl.pallas_call(
        functools.partial(pack_kernel, len(pieces)),
        out_shape=full,
        in_specs=[ANY] * len(pieces),
        out_specs=ANY,
        scratch_shapes=[pltpu.VMEM(full.shape, BF16), pltpu.SemaphoreType.DMA((len(pieces),))],
        compiler_params=params(40),
        cost_estimate=cost(3e9, 1e6),
    )(*pieces)


def rows_of(piece_refs, held_ref, start=0):
    found, at = [], 0
    for piece in piece_refs:
        rows = piece.shape[0]
        source = piece.at[:, start : start + held_ref.shape[1]]
        found.append((source, held_ref.at[at : at + rows]))
        at += rows
    return found


def first_kernel(count, *refs):
    norms, pieces = refs[:4], refs[4 : 4 + count]
    qk_ref, v_ref = refs[4 + count : 6 + count]
    held_ref, sem = refs[6 + count :]
    deep, columns = held_ref.shape
    split = 2 * columns // 3
    loads = load_all(rows_of(pieces, held_ref), sem)
    for copy in loads:
        copy.wait()
    for block in range(4):
        qk_ref[block] = times(norms[block][:, :deep], held_ref[:, :split]).astype(BF16)
        v_ref[block] = times(norms[block][:, :deep], held_ref[:, split:]).astype(BF16)


def first_part(norms, pieces):
    rows = norms[0].shape[0]
    columns = 3 * norms[0].shape[1] // 4
    deep = sum(piece.shape[0] for piece in pieces)
    qk = shape_of(4, rows, 2 * columns // 3)
    v = shape_of(4, rows, columns // 3)
    return pl.pallas_call(
        functools.partial(first_kernel, len(pieces)),
        out_shape=[qk, v],
        in_specs=[VMEM] * 4 + [ANY] * len(pieces),
        out_specs=[VMEM] * 2,
        scratch_shapes=[
            pltpu.VMEM((deep, columns), BF16),
            pltpu.SemaphoreType.DMA((len(pieces),)),
        ],
        compiler_params=params(40),
        cost_estimate=cost(6e9, 1e6),
    )(*norms, *pieces)


def scores_kernel(count, *refs):
    norms, acc_ref, gains_ref, pieces = refs[:4], refs[4], refs[5], refs[6 : 6 + count]
    out_ref, sums_ref, held_ref, gains_in, sem = refs[6 + count :]
    deep = held_ref.shape[0]
    third = out_ref.shape[2] // 2
    width = norms[0].shape[1]
    loads = load_all(rows_of(pieces, held_ref) + [(gains_ref, gains_in)], sem)
    mine = window(places()[3], third)
    row = lax.broadcasted_iota(jnp.int32, (8, 4 * DH), 0)
    lane = lax.broadcasted_iota(jnp.int32, (8, 4 * DH), 1)
    pick = (row == lane // (2 * DH)).astype(BF16)
    for copy in loads:
        copy.wait()
    gains = [gains_in[0, :, mine] * (1.4426950408889634 / DH**0.5), gains_in[1, :, mine]]
    for block in range(4):
        product = times(norms[block][:, width - deep :], held_ref[...])
        squares = []
        for j in range(2):
            square = 0.0
            for h in range(third // DH):
                at = slice(j * third + h * DH, j * third + (h + 1) * DH)
                part = acc_ref[block, :, at].astype(F32) + product[:, at]
                square += part * part
                out_ref[block, :, at] = (part * gains[j][:, h * DH : (h + 1) * DH]).astype(BF16)
            high = square.astype(BF16)
            squares += [high, (square - high.astype(F32)).astype(BF16)]
        sums_ref[block] = times_turned(pick, jnp.concatenate(squares, axis=1))


def last_scores(norms, acc, gains, pieces):
    rows = norms[0].shape[0]
    columns = acc.shape[2]
    deep = sum(piece.shape[0] for piece in pieces)
    return pl.pallas_call(
        functools.partial(scores_kernel, len(pieces)),
        out_shape=[shape_of(4, rows, columns), shape_of(4, 8, rows, dtype=F32)],
        in_specs=[VMEM] * 5 + [ANY] * (1 + len(pieces)),
        out_specs=[VMEM, VMEM],
        scratch_shapes=[
            pltpu.VMEM((deep, columns), BF16),
            pltpu.VMEM(gains.shape, F32),
            pltpu.SemaphoreType.DMA((1 + len(pieces),)),
        ],
        compiler_params=params(40),
        cost_estimate=cost(6e9, 1e6),
    )(*norms, acc, gains, *pieces)


def values_kernel(count, *refs):
    norms, acc_ref, pieces = refs[:4], refs[4], refs[5 : 5 + count]
    out_ref, held_ref, sem = refs[5 + count :]
    deep, columns = held_ref.shape
    width = norms[0].shape[1]
    loads = load_all(rows_of(pieces, held_ref, 2 * columns), sem)
    for copy in loads:
        copy.wait()
    for block in range(4):
        product = times(norms[block][:, width - deep :], held_ref[...])
        out_ref[block] = (acc_ref[block].astype(F32) + product).astype(BF16)


def last_values(norms, acc, pieces):
    rows = norms[0].shape[0]
    columns = acc.shape[2]
    deep = sum(piece.shape[0] for piece in pieces)
    return pl.pallas_call(
        functools.partial(values_kernel, len(pieces)),
        out_shape=shape_of(4, rows, columns),
        in_specs=[VMEM] * 5 + [ANY] * len(pieces),
        out_specs=VMEM,
        scratch_shapes=[
            pltpu.VMEM((deep, columns), BF16),
            pltpu.SemaphoreType.DMA((len(pieces),)),
        ],
        compiler_params=params(40),
        cost_estimate=cost(4e9, 1e6),
    )(*norms, acc, *pieces)


def heads_kernel(blocks, length_ref, qk_ref, v_ref, s0_ref, s1_ref, s2_ref, s3_ref, *refs):
    outs = refs[:2]
    v_in, sums_in, out_buf, sem, out_sem = refs[2:]
    qk_in = qk_ref
    rows = qk_ref.shape[1]
    third = qk_ref.shape[2] // 2
    count = third // DH
    width = 4 * third
    sum_refs = (s0_ref, s1_ref, s2_ref, s3_ref)
    loads = [(sum_refs[j], sums_in.at[j]) for j in range(4)]
    order = [b for block in blocks for b in (block - block % 2, block - block % 2 + 1)]
    for b in order:
        held = v_in.at[b // 2, b % 2 * rows : (b % 2 + 1) * rows]
        for h in range(count):
            loads.append((v_ref.at[b, :, h * DH : (h + 1) * DH], held.at[:, 2 * h * DH : (2 * h + 1) * DH]))
    loads = load_all(loads, sem)
    for b in range(2):
        for h in range(count):
            v_in[b, :, (2 * h + 1) * DH : (2 * h + 2) * DH] = jnp.ones((2 * rows, DH), BF16)
    row = lax.broadcasted_iota(jnp.int32, (24, DH), 0)
    pick = (row % 8 == 0).astype(BF16)
    place = lax.broadcasted_iota(jnp.int32, (1, rows), 1)
    position = lax.axis_index("seq")
    masks = [place < length_ref[0] - (j + position - 2 * j * position) * rows for j in range(2)]
    for copy in loads[:4]:
        copy.wait()
    scale_q, scale_k = {}, {}
    for block in range(4):
        sums = sums_in[0, block] + sums_in[1, block ^ 1] + sums_in[2, block ^ 2] + sums_in[3, block ^ 3]
        inverse = lax.rsqrt(sums * (1.0 / width) + 1e-06)
        scale_k[block] = inverse[1:2, :]
        if block in blocks:
            high = inverse.astype(BF16).astype(F32)
            middle = (inverse - high).astype(BF16).astype(F32)
            stacked = jnp.concatenate([high, middle, inverse - high - middle], axis=0).astype(BF16)
            turned = lax.dot_general(stacked, pick, (((0,), (0,)), ((), ())), preferred_element_type=F32)
            scale_q[block] = turned[:, :1]
    items = [(at, block, h) for at, block in enumerate(blocks) for h in range(count)]

    def scores_of(at, block, h):
        first = block - block % 2
        query = qk_in[block, :, h * DH : (h + 1) * DH]
        found = []
        for j in range(2):
            keys = qk_in[first + j, :, third + h * DH : third + (h + 1) * DH]
            part = times_turned(query, keys) * scale_k[first + j]
            found.append(jnp.where(masks[j], part, -1e30))
        return found

    stores = []
    ahead = scores_of(*items[0])
    for turn, (at, block, h) in enumerate(items):
        scores = ahead
        if turn + 1 < len(items):
            ahead = scores_of(*items[turn + 1])
        if h == 0:
            for copy in loads[4 + 2 * count * at : 4 + 2 * count * (at + 1)]:
                copy.wait()
        top = jnp.maximum(
            jnp.max(scores[0], axis=-1, keepdims=True), jnp.max(scores[1], axis=-1, keepdims=True)
        )
        weighted = 0.0
        for j in range(2):
            probs = jnp.exp2((scores[j] - top) * scale_q[block]).astype(BF16)
            values = v_in[block // 2, j * rows : (j + 1) * rows, 2 * h * DH : (2 * h + 2) * DH]
            weighted += times(probs, values)
        out_buf[at, :, h * DH : (h + 1) * DH] = (weighted[:, :DH] / weighted[:, DH:]).astype(BF16)
        if h == count - 1:
            stores.append(pltpu.make_async_copy(out_buf.at[at], outs[at], out_sem.at[at]))
            stores[-1].start()
    for copy in stores:
        copy.wait()


def team_attention(blocks, effort, length, qk, v, sums):
    rows = qk.shape[1]
    third = qk.shape[2] // 2
    count = third // DH
    return pl.pallas_call(
        functools.partial(heads_kernel, blocks),
        out_shape=[shape_of(rows, third)] * 2,
        in_specs=[SMEM, VMEM] + [ANY] * 5,
        out_specs=[ANY] * 2,
        scratch_shapes=[
            pltpu.VMEM((2, 2 * rows, 2 * third), BF16),
            pltpu.VMEM((4, 4, 8, rows), F32),
            pltpu.VMEM((2, rows, third), BF16),
            pltpu.SemaphoreType.DMA((4 + 4 * count,)),
            pltpu.SemaphoreType.DMA((2,)),
        ],
        compiler_params=params(40),
        cost_estimate=cost(effort, 1e6),
    )(length, qk, v, *sums)


def out_kernel(state_ref, modes_ref, head_ref, *refs):
    attended, pieces = refs[:4], refs[4:12]
    own_ref, sent_ref = refs[12:14]
    att_in, group_ref, held_ref, state_in, modes_in, head_in_ref, own_buf, sent_buf, sem = refs[14:]
    side, pair, steps, own = places()
    third = attended[0].shape[1]
    half = pieces[0].shape[0]
    loads = load_all(
        [(attended[j], att_in.at[j]) for j in range(4)]
        + [(pieces[j], held_ref.at[:half, window(own ^ j, third)]) for j in range(4)]
        + [(pieces[4 + j], held_ref.at[half:, window(own ^ j, third)]) for j in range(4)]
        + [(state_ref, state_in), (modes_ref, modes_in), (head_ref, head_in_ref)],
        sem,
    )
    for j in range(4):
        loads[j].wait()
        part = att_in[j].astype(F32)
        part = jnp.where(side == 0, part, pltpu.roll(part, third // 2, 1)).astype(BF16)
        group_ref[:, window(lax.rem(fold(own ^ j) + steps - pair, steps), third)] = part
    for copy in loads[4:8]:
        copy.wait()
    total = times(group_ref[:, :half], held_ref[:half, :])
    for copy in loads[8:]:
        copy.wait()
    total += times(group_ref[:, half:], held_ref[half:, :])
    block_out = (state_in[...].astype(F32) + modes_in[2] * total).astype(BF16)
    head_in = scaled_norm(block_out.astype(F32), modes_in[3], modes_in[4])
    velocity = times_turned(head_in_ref[...], head_in.astype(BF16))
    channels = own_buf.shape[0]
    core = lax.axis_index("cfg")
    own_buf[...] = jnp.where(core == 0, velocity[:channels], velocity[channels:])
    sent_buf[...] = jnp.where(core == 0, velocity[channels:], velocity[:channels]).astype(BF16)
    for copy in load_all([(own_buf, own_ref), (sent_buf, sent_ref)], sem):
        copy.wait()


def project(state, modes, w_head, attended, pieces):
    rows, width = state.shape
    third = width // 4
    channels = w_head.shape[0] // 2
    return pl.pallas_call(
        out_kernel,
        out_shape=[shape_of(channels, rows, dtype=F32), shape_of(channels, rows)],
        in_specs=[ANY] * 15,
        out_specs=[ANY, ANY],
        scratch_shapes=[
            pltpu.VMEM((4, rows, third), BF16),
            pltpu.VMEM((rows, width), BF16),
            pltpu.VMEM((width, width), BF16),
            pltpu.VMEM(state.shape, BF16),
            pltpu.VMEM(modes.shape, F32),
            pltpu.VMEM(w_head.shape, BF16),
            pltpu.VMEM((channels, rows), F32),
            pltpu.VMEM((channels, rows), BF16),
            pltpu.SemaphoreType.DMA((15,)),
        ],
        compiler_params=params(50),
        cost_estimate=cost(8e9, 1e6),
    )(state, modes, w_head, *attended, *pieces)


def updated_latent(own, outgoing, latent, guidance, step_size, length, position):
    rows = own.shape[1]
    branch = lax.axis_index("cfg")
    scale = guidance[0]
    other = lax.ppermute(outgoing, "cfg", SWAP).astype(own.dtype)
    cond = jnp.where(branch == 0, own, other)
    uncond = jnp.where(branch == 0, other, own)
    guided = uncond + scale * (cond - uncond)
    valid = position * rows + jnp.arange(rows, dtype=jnp.int32) < length
    current = latent[0].T
    updated = jnp.where(valid[None, :], current - step_size[0] * guided, current)
    return updated.T[None]


def after(value, *others):
    return lax.optimization_barrier((value, *others))[0]


def team_local(
    hidden, latent, modulation, w_qkv, w_out, q_gain, k_gain, w_head, lengths, guidance, step_size
):
    state = hidden[0, 0]
    modes = jnp.transpose(modulation, (1, 0, 2))
    rows, width = state.shape
    third = width // 4
    parts = lax.axis_size("req")
    up = [(2 * fold(i) + side, 2 * fold((i - 1) % 4) + side) for i in range(4) for side in range(2)]
    down = [(target, source) for source, target in up]
    beside = [(i, i ^ 1) for i in range(parts)]

    def along(piece):
        return lax.ppermute(piece, "req", up)

    def back(piece):
        return lax.ppermute(piece, "req", down)

    def across(piece):
        return lax.ppermute(piece, "req", beside)

    gains = jnp.stack([q_gain, k_gain])[:, None]
    columns, normed = entry(w_qkv, w_out, state, modes)
    normed_y = lax.ppermute(normed, "seq", SWAP)
    normed_c = lax.ppermute(normed, "cfg", SWAP)

    def step(mine, theirs, gates):
        now = after(mine[-1], *gates)
        mine.append(along(now))
        theirs.append(across(now))

    mine, theirs = [columns], []
    step(mine, theirs, [])
    cut, split = columns.shape[0] // 2, 3 * third
    low = theirs[0][cut:, :split]
    out_last = theirs[0][:, split:]
    gates = [mine[1], theirs[0], low, out_last, gains]
    step(mine, theirs, gates)
    gates = [mine[2], theirs[1]]
    step(mine, theirs, gates)
    out_last = back(after(out_last, *gates))
    early = [mine[0], theirs[0], mine[1], theirs[1]]
    packed = [pack(early, third)]
    normed_yc = lax.ppermute(normed_y, "cfg", SWAP)
    norms = [normed, normed_y, normed_c, normed_yc]
    packed_y = [lax.ppermute(packed[0], "seq", SWAP)]
    acc_qk, acc_v = first_part(norms, early)
    gates = [mine[3], theirs[2], out_last, packed_y[0], acc_v]
    upper = across(after(mine[3][:cut, :split], *gates))
    lower = back(after(low, *gates))
    late = [mine[2], theirs[2], mine[3], upper, lower]
    packed.append(pack([mine[2], theirs[2], mine[3], out_last], third))
    packed_y.append(lax.ppermute(packed[1], "seq", SWAP))
    packed_c = [lax.ppermute(part, "cfg", SWAP) for part in packed]
    packed_yc = [lax.ppermute(part, "cfg", SWAP) for part in packed_y]

    qk_full, sums = last_scores(norms, acc_qk, gains, late)
    v_full = last_values(norms, acc_v, late)
    diagonal = [(i, 3 - i) for i in range(4)]
    all_sums = [
        sums,
        lax.ppermute(sums, "seq", SWAP),
        lax.ppermute(sums, "cfg", SWAP),
        lax.ppermute(sums, ("cfg", "seq"), diagonal),
    ]
    v_full = after(v_full, packed_c[0], packed_yc[0])
    far = team_attention((1, 3), 6e9, lengths, qk_full, v_full, all_sums)
    far = lax.optimization_barrier((*far, packed_y[1], packed_c[1]))[:2]
    near = team_attention((2, 0), 1e6, lengths, after(qk_full, far[0]), v_full, all_sums)
    attended = [
        near[1],
        lax.ppermute(near[0], "cfg", SWAP),
        lax.ppermute(far[0], "seq", SWAP),
        lax.ppermute(far[1], ("cfg", "seq"), diagonal),
    ]
    quarters = [part[j] for j in range(2) for part in (packed, packed_c, packed_y, packed_yc)]
    own, outgoing = project(state, modes, w_head.T, attended, quarters)
    return updated_latent(own, outgoing, latent, guidance, step_size, lengths[0], lax.axis_index("seq"))


def by_team(mesh, arguments):
    hidden, w_qkv = arguments[0], arguments[3]
    sizes = mesh.shape
    width = hidden.shape[3]
    depth = w_qkv.shape[0] // sizes["req"]
    return (
        sizes["cfg"] == 2
        and sizes["seq"] == 2
        and sizes["req"] == 8
        and width % (4 * DH) == 0
        and 8 * depth == width
        and depth % 32 == 0
        and hidden.shape[2] // sizes["seq"] % 16 == 0
    )


def solution(mesh):
    def whole(*arguments):
        body = team_local if by_team(mesh, arguments) else ring_local
        return jax.shard_map(
            body,
            mesh=mesh,
            in_specs=(
                P("cfg", "req", "seq", None),
                P("req", "seq", "cfg"),
                P("req", None, None),
                P("req", None),
                P("req", None),
                P(),
                P(),
                P(),
                P("req"),
                P("req"),
                P("req"),
            ),
            out_specs=P("req", "seq", "cfg"),
            check_vma=False,
        )(*arguments)

    return whole
```

```python
import functools

import jax
import jax.numpy as jnp
from jax import lax
from jax.experimental import pallas as pl
from jax.experimental.pallas import tpu as pltpu
from jax.sharding import PartitionSpec as P

DH = 128
SWAP = [(0, 1), (1, 0)]
VMEM = pl.BlockSpec(memory_space=pltpu.VMEM)
SMEM = pl.BlockSpec(memory_space=pltpu.SMEM)
ANY = pl.BlockSpec(memory_space=pl.ANY)
BF16 = jnp.bfloat16
F32 = jnp.float32


def params(megabytes):
    return pltpu.CompilerParams(vmem_limit_bytes=megabytes * 2**20)


def cost(flops, moved, exps=0):
    return pl.CostEstimate(flops=int(flops), bytes_accessed=int(moved), transcendentals=int(exps))


def shape_of(*dims, dtype=BF16):
    return jax.ShapeDtypeStruct(dims, dtype)


def times(left, right):
    return jnp.dot(left, right, preferred_element_type=F32)


def times_turned(left, right):
    return lax.dot_general(left, right, (((1,), (1,)), ((), ())), preferred_element_type=F32)


def passed_along(value, axis, steps):
    count = lax.axis_size(axis)
    pairs = [(source, (source + steps) % count) for source in range(count)]
    return lax.ppermute(value, axis, pairs)


def from_partner(value, axis, apart):
    mask = 2**apart
    pairs = [(source, source ^ mask) for source in range(lax.axis_size(axis))]
    return lax.ppermute(value, axis, pairs)


def layer_norm(values):
    centered = values - jnp.mean(values, axis=-1, keepdims=True)
    return centered / jnp.sqrt(jnp.mean(centered * centered, axis=-1, keepdims=True) + 1e-06)


def rms_gain(values, gain):
    return values / jnp.sqrt(jnp.mean(values * values, axis=-1, keepdims=True) + 1e-06) * gain


def add_rows(left, piece):
    return jnp.dot(left, piece, preferred_element_type=jnp.float32)


def attend(state, query, stacked, start, length):
    top, total, weighted = state
    keys = stacked[0]
    values = stacked[1]
    count = keys.shape[0]
    scores = jnp.einsum("qhd,khd->qhk", query, keys, preferred_element_type=jnp.float32) / jnp.sqrt(
        jnp.float32(query.shape[2])
    )
    valid = start + jnp.arange(count, dtype=jnp.int32) < length
    scores = jnp.where(valid[None, None, :], scores, jnp.float32(-1e30))
    new_top = jnp.maximum(top, jnp.max(scores, axis=-1))
    factor = jnp.exp(top - new_top)
    probs = jnp.where(valid[None, None, :], jnp.exp(scores - new_top[:, :, None]), jnp.float32(0.0))
    total = total * factor + jnp.sum(probs, axis=-1)
    weighted = weighted * factor[:, :, None] + jnp.einsum(
        "qhk,khd->qhd", probs.astype(jnp.bfloat16), values, preferred_element_type=jnp.float32
    )
    return (new_top, total, weighted)


def ring_local(
    hidden, latent, modulation, w_qkv, w_out, q_gain, k_gain, w_head, lengths, guidance, step_size
):
    state = hidden[0, 0]
    modes = modulation[0]
    length = lengths[0]
    rows = state.shape[0]
    width = state.shape[1]
    heads = q_gain.shape[0] // DH
    wide = state.astype(jnp.float32)
    normed = (layer_norm(wide) * (1.0 + modes[1]) + modes[0]).astype(jnp.bfloat16)
    qkv = add_rows(normed, lax.all_gather(w_qkv, "req", axis=0, tiled=True))
    query = rms_gain(qkv[:, :width], q_gain).astype(jnp.bfloat16).reshape(rows, heads, DH)
    keys = rms_gain(qkv[:, width : 2 * width], k_gain).astype(jnp.bfloat16).reshape(rows, heads, DH)
    values = qkv[:, 2 * width :].astype(jnp.bfloat16).reshape(rows, heads, DH)
    stacked = jnp.stack([keys, values])
    position = lax.axis_index("seq")
    members = lax.axis_size("seq")
    start_state = (
        jnp.full((rows, heads), -1e30, jnp.float32),
        jnp.zeros((rows, heads), jnp.float32),
        jnp.zeros((rows, heads, DH), jnp.float32),
    )
    first = attend(start_state, query, stacked, position * rows, length)

    def cycle_step(turn, carry):
        moving, inner = carry
        moving = passed_along(moving, "seq", 1)
        source = (position - turn) % members
        return (moving, attend(inner, query, moving, source * rows, length))

    moved, result = lax.fori_loop(1, members, cycle_step, (stacked, first))
    top, total, weighted = result
    attended = (weighted / total[:, :, None]).reshape(rows, width).astype(jnp.bfloat16)
    projected = add_rows(attended, lax.all_gather(w_out, "req", axis=0, tiled=True))
    block_out = (wide + modes[2] * projected).astype(jnp.bfloat16)
    head_in = (layer_norm(block_out.astype(jnp.float32)) * (1.0 + modes[4]) + modes[3]).astype(
        jnp.bfloat16
    )
    velocity = jnp.dot(head_in, w_head, preferred_element_type=jnp.float32)
    branch = lax.axis_index("cfg")
    scale = guidance[0]
    channels = velocity.shape[1] // 2
    own = lax.dynamic_slice_in_dim(velocity, branch * channels, channels, 1)
    outgoing = lax.dynamic_slice_in_dim(velocity, (1 - branch) * channels, channels, 1)
    other = from_partner(outgoing.astype(jnp.bfloat16), "cfg", 0).astype(outgoing.dtype)
    cond = jnp.where(branch == 0, own, other)
    uncond = jnp.where(branch == 0, other, own)
    guided = uncond + scale * (cond - uncond)
    valid = position * rows + jnp.arange(rows, dtype=jnp.int32) < length
    current = latent[0]
    updated = jnp.where(valid[:, None], current - step_size[0] * guided, current)
    return updated[None]


def load_all(pairs, sem):
    copies = [pltpu.make_async_copy(source, target, sem.at[j]) for j, (source, target) in enumerate(pairs)]
    for copy in copies:
        copy.start()
    return copies


def fold(pair):
    return pair ^ (pair // 2)


def places():
    place = lax.axis_index("req")
    group = 2 * lax.axis_index("seq") + lax.axis_index("cfg")
    return lax.rem(place, 2), fold(place // 2), lax.axis_size("req") // 2, group


def window(j, size):
    return pl.ds(pl.multiple_of(j * size, size), size)


def scaled_norm(values, shift, scale):
    centered = values - jnp.mean(values, axis=-1, keepdims=True)
    inverse = lax.rsqrt(jnp.mean(centered * centered, axis=-1, keepdims=True) + 1e-06)
    return centered * inverse * (1.0 + scale) + shift


def entry_kernel(qkv_ref, w_out_ref, state_ref, modes_ref, cut_ref, norm_ref, *scratch):
    cut_buf, state_in, modes_in, full_ref, norm_buf, sem, out_sem = scratch
    side, pair, steps, group = places()
    third = cut_ref.shape[1] // 4
    loads = [(state_ref, state_in), (modes_ref, modes_in)]
    for j in range(3):
        loads.append((qkv_ref.at[:, window(4 * j + group, third)], cut_buf.at[:, j * third : (j + 1) * third]))
    loads.append((w_out_ref.at[:, window(group, third)], cut_buf.at[:, 3 * third :]))
    loads = load_all(loads, sem)
    for copy in loads[:2]:
        copy.wait()
    full_ref[...] = scaled_norm(state_in[...].astype(F32), modes_in[0], modes_in[1])
    for copy in loads[2:]:
        copy.wait()
    stores = [pltpu.make_async_copy(cut_buf, cut_ref, out_sem.at[0])]
    stores[0].start()
    count = 4
    for k in range(count):
        part = full_ref[:, window(fold(lax.rem(pair + k, steps)), third)]
        part = jnp.where(side == 0, part, pltpu.roll(part, third // 2, 1))
        norm_buf[:, k * third : (k + 1) * third] = part.astype(BF16)
    stores.append(pltpu.make_async_copy(norm_buf, norm_ref, out_sem.at[1]))
    stores[1].start()
    for copy in stores:
        copy.wait()


def entry(w_qkv, w_out, state, modes):
    return pl.pallas_call(
        entry_kernel,
        out_shape=[shape_of(*w_out.shape), shape_of(*state.shape)],
        in_specs=[ANY] * 4,
        out_specs=[ANY, ANY],
        scratch_shapes=[
            pltpu.VMEM(w_out.shape, BF16),
            pltpu.VMEM(state.shape, BF16),
            pltpu.VMEM(modes.shape, F32),
            pltpu.VMEM(state.shape, F32),
            pltpu.VMEM(state.shape, BF16),
            pltpu.SemaphoreType.DMA((6,)),
            pltpu.SemaphoreType.DMA((2,)),
        ],
        compiler_params=params(60),
        cost_estimate=cost(4e9, 1e6),
    )(w_qkv, w_out, state, modes)


def pack_kernel(count, *refs):
    pieces, packed_ref, held_ref, sem = refs[:count], refs[count], refs[count + 1], refs[count + 2]
    depth = held_ref.shape[0] // count
    columns = held_ref.shape[1]
    pairs = []
    for k, piece in enumerate(pieces):
        pairs.append((piece.at[:, piece.shape[1] - columns :], held_ref.at[k * depth : (k + 1) * depth]))
    for copy in load_all(pairs, sem):
        copy.wait()
    for copy in load_all([(held_ref, packed_ref)], sem):
        copy.wait()


def pack(pieces, columns):
    depth = pieces[0].shape[0]
    full = shape_of(depth * len(pieces), columns)
    return pl.pallas_call(
        functools.partial(pack_kernel, len(pieces)),
        out_shape=full,
        in_specs=[ANY] * len(pieces),
        out_specs=ANY,
        scratch_shapes=[pltpu.VMEM(full.shape, BF16), pltpu.SemaphoreType.DMA((len(pieces),))],
        compiler_params=params(40),
        cost_estimate=cost(3e9, 1e6),
    )(*pieces)


def rows_of(piece_refs, held_ref, start=0):
    found, at = [], 0
    for piece in piece_refs:
        rows = piece.shape[0]
        source = piece.at[:, start : start + held_ref.shape[1]]
        found.append((source, held_ref.at[at : at + rows]))
        at += rows
    return found


def first_kernel(count, *refs):
    norms, pieces = refs[:4], refs[4 : 4 + count]
    qk_ref, v_ref = refs[4 + count : 6 + count]
    held_ref, sem = refs[6 + count :]
    deep, columns = held_ref.shape
    split = 2 * columns // 3
    loads = load_all(rows_of(pieces, held_ref), sem)
    for copy in loads:
        copy.wait()
    for block in range(4):
        qk_ref[block] = times(norms[block][:, :deep], held_ref[:, :split]).astype(BF16)
        v_ref[block] = times(norms[block][:, :deep], held_ref[:, split:]).astype(BF16)


def first_part(norms, pieces):
    rows = norms[0].shape[0]
    columns = 3 * norms[0].shape[1] // 4
    deep = sum(piece.shape[0] for piece in pieces)
    qk = shape_of(4, rows, 2 * columns // 3)
    v = shape_of(4, rows, columns // 3)
    return pl.pallas_call(
        functools.partial(first_kernel, len(pieces)),
        out_shape=[qk, v],
        in_specs=[VMEM] * 4 + [ANY] * len(pieces),
        out_specs=[VMEM] * 2,
        scratch_shapes=[
            pltpu.VMEM((deep, columns), BF16),
            pltpu.SemaphoreType.DMA((len(pieces),)),
        ],
        compiler_params=params(40),
        cost_estimate=cost(6e9, 1e6),
    )(*norms, *pieces)


def scores_kernel(count, *refs):
    norms, acc_ref, gains_ref, pieces = refs[:4], refs[4], refs[5], refs[6 : 6 + count]
    out_ref, sums_ref, held_ref, gains_in, sem = refs[6 + count :]
    deep = held_ref.shape[0]
    third = out_ref.shape[2] // 2
    width = norms[0].shape[1]
    loads = load_all(rows_of(pieces, held_ref) + [(gains_ref, gains_in)], sem)
    mine = window(places()[3], third)
    row = lax.broadcasted_iota(jnp.int32, (8, 4 * DH), 0)
    lane = lax.broadcasted_iota(jnp.int32, (8, 4 * DH), 1)
    pick = (row == lane // (2 * DH)).astype(BF16)
    for copy in loads:
        copy.wait()
    gains = [gains_in[0, :, mine] * (1.4426950408889634 / DH**0.5), gains_in[1, :, mine]]
    for block in range(4):
        product = times(norms[block][:, width - deep :], held_ref[...])
        squares = []
        for j in range(2):
            square = 0.0
            for h in range(third // DH):
                at = slice(j * third + h * DH, j * third + (h + 1) * DH)
                part = acc_ref[block, :, at].astype(F32) + product[:, at]
                square += part * part
                out_ref[block, :, at] = (part * gains[j][:, h * DH : (h + 1) * DH]).astype(BF16)
            high = square.astype(BF16)
            squares += [high, (square - high.astype(F32)).astype(BF16)]
        sums_ref[block] = times_turned(pick, jnp.concatenate(squares, axis=1))


def last_scores(norms, acc, gains, pieces):
    rows = norms[0].shape[0]
    columns = acc.shape[2]
    deep = sum(piece.shape[0] for piece in pieces)
    return pl.pallas_call(
        functools.partial(scores_kernel, len(pieces)),
        out_shape=[shape_of(4, rows, columns), shape_of(4, 8, rows, dtype=F32)],
        in_specs=[VMEM] * 5 + [ANY] * (1 + len(pieces)),
        out_specs=[VMEM, VMEM],
        scratch_shapes=[
            pltpu.VMEM((deep, columns), BF16),
            pltpu.VMEM(gains.shape, F32),
            pltpu.SemaphoreType.DMA((1 + len(pieces),)),
        ],
        compiler_params=params(40),
        cost_estimate=cost(6e9, 1e6),
    )(*norms, acc, gains, *pieces)


def values_kernel(count, *refs):
    norms, acc_ref, pieces = refs[:4], refs[4], refs[5 : 5 + count]
    out_ref, held_ref, sem = refs[5 + count :]
    deep, columns = held_ref.shape
    width = norms[0].shape[1]
    loads = load_all(rows_of(pieces, held_ref, 2 * columns), sem)
    for copy in loads:
        copy.wait()
    for block in range(4):
        product = times(norms[block][:, width - deep :], held_ref[...])
        out_ref[block] = (acc_ref[block].astype(F32) + product).astype(BF16)


def last_values(norms, acc, pieces):
    rows = norms[0].shape[0]
    columns = acc.shape[2]
    deep = sum(piece.shape[0] for piece in pieces)
    return pl.pallas_call(
        functools.partial(values_kernel, len(pieces)),
        out_shape=shape_of(4, rows, columns),
        in_specs=[VMEM] * 5 + [ANY] * len(pieces),
        out_specs=VMEM,
        scratch_shapes=[
            pltpu.VMEM((deep, columns), BF16),
            pltpu.SemaphoreType.DMA((len(pieces),)),
        ],
        compiler_params=params(40),
        cost_estimate=cost(4e9, 1e6),
    )(*norms, acc, *pieces)


def heads_kernel(blocks, length_ref, qk_ref, v_ref, s0_ref, s1_ref, s2_ref, s3_ref, *refs):
    outs = refs[:2]
    v_in, sums_in, out_buf, sem, out_sem = refs[2:]
    qk_in = qk_ref
    rows = qk_ref.shape[1]
    third = qk_ref.shape[2] // 2
    count = third // DH
    width = 4 * third
    sum_refs = (s0_ref, s1_ref, s2_ref, s3_ref)
    loads = [(sum_refs[j], sums_in.at[j]) for j in range(4)]
    order = [b for block in blocks for b in (block - block % 2, block - block % 2 + 1)]
    for b in order:
        held = v_in.at[b // 2, b % 2 * rows : (b % 2 + 1) * rows]
        for h in range(count):
            loads.append((v_ref.at[b, :, h * DH : (h + 1) * DH], held.at[:, 2 * h * DH : (2 * h + 1) * DH]))
    loads = load_all(loads, sem)
    for b in range(2):
        for h in range(count):
            v_in[b, :, (2 * h + 1) * DH : (2 * h + 2) * DH] = jnp.ones((2 * rows, DH), BF16)
    row = lax.broadcasted_iota(jnp.int32, (24, DH), 0)
    pick = (row % 8 == 0).astype(BF16)
    place = lax.broadcasted_iota(jnp.int32, (1, rows), 1)
    position = lax.axis_index("seq")
    masks = [place < length_ref[0] - (j + position - 2 * j * position) * rows for j in range(2)]
    for copy in loads[:4]:
        copy.wait()
    scale_q, scale_k = {}, {}
    for block in range(4):
        sums = sums_in[0, block] + sums_in[1, block ^ 1] + sums_in[2, block ^ 2] + sums_in[3, block ^ 3]
        inverse = lax.rsqrt(sums * (1.0 / width) + 1e-06)
        scale_k[block] = inverse[1:2, :]
        if block in blocks:
            high = inverse.astype(BF16).astype(F32)
            middle = (inverse - high).astype(BF16).astype(F32)
            stacked = jnp.concatenate([high, middle, inverse - high - middle], axis=0).astype(BF16)
            turned = lax.dot_general(stacked, pick, (((0,), (0,)), ((), ())), preferred_element_type=F32)
            scale_q[block] = turned[:, :1]
    items = [(at, block, h) for at, block in enumerate(blocks) for h in range(count)]

    def scores_of(at, block, h):
        first = block - block % 2
        query = qk_in[block, :, h * DH : (h + 1) * DH]
        found = []
        for j in range(2):
            keys = qk_in[first + j, :, third + h * DH : third + (h + 1) * DH]
            part = times_turned(query, keys) * scale_k[first + j]
            found.append(jnp.where(masks[j], part, -1e30))
        return found

    stores = []
    ahead = scores_of(*items[0])
    for turn, (at, block, h) in enumerate(items):
        scores = ahead
        if turn + 1 < len(items):
            ahead = scores_of(*items[turn + 1])
        if h == 0:
            for copy in loads[4 + 2 * count * at : 4 + 2 * count * (at + 1)]:
                copy.wait()
        top = jnp.maximum(
            jnp.max(scores[0], axis=-1, keepdims=True), jnp.max(scores[1], axis=-1, keepdims=True)
        )
        weighted = 0.0
        for j in range(2):
            probs = jnp.exp2((scores[j] - top) * scale_q[block]).astype(BF16)
            values = v_in[block // 2, j * rows : (j + 1) * rows, 2 * h * DH : (2 * h + 2) * DH]
            weighted += times(probs, values)
        out_buf[at, :, h * DH : (h + 1) * DH] = (weighted[:, :DH] / weighted[:, DH:]).astype(BF16)
        if h == count - 1:
            stores.append(pltpu.make_async_copy(out_buf.at[at], outs[at], out_sem.at[at]))
            stores[-1].start()
    for copy in stores:
        copy.wait()


def team_attention(blocks, effort, length, qk, v, sums):
    rows = qk.shape[1]
    third = qk.shape[2] // 2
    count = third // DH
    return pl.pallas_call(
        functools.partial(heads_kernel, blocks),
        out_shape=[shape_of(rows, third)] * 2,
        in_specs=[SMEM, VMEM] + [ANY] * 5,
        out_specs=[ANY] * 2,
        scratch_shapes=[
            pltpu.VMEM((2, 2 * rows, 2 * third), BF16),
            pltpu.VMEM((4, 4, 8, rows), F32),
            pltpu.VMEM((2, rows, third), BF16),
            pltpu.SemaphoreType.DMA((4 + 4 * count,)),
            pltpu.SemaphoreType.DMA((2,)),
        ],
        compiler_params=params(40),
        cost_estimate=cost(effort, 1e6),
    )(length, qk, v, *sums)


def out_kernel(state_ref, modes_ref, head_ref, *refs):
    attended, pieces = refs[:4], refs[4:12]
    own_ref, sent_ref = refs[12:14]
    att_in, group_ref, held_ref, state_in, modes_in, head_in_ref, own_buf, sent_buf, sem = refs[14:]
    side, pair, steps, own = places()
    third = attended[0].shape[1]
    half = pieces[0].shape[0]
    loads = load_all(
        [(attended[j], att_in.at[j]) for j in range(4)]
        + [(pieces[j], held_ref.at[:half, window(own ^ j, third)]) for j in range(4)]
        + [(pieces[4 + j], held_ref.at[half:, window(own ^ j, third)]) for j in range(4)]
        + [(state_ref, state_in), (modes_ref, modes_in), (head_ref, head_in_ref)],
        sem,
    )
    for j in range(4):
        loads[j].wait()
        part = att_in[j].astype(F32)
        part = jnp.where(side == 0, part, pltpu.roll(part, third // 2, 1)).astype(BF16)
        group_ref[:, window(lax.rem(fold(own ^ j) + steps - pair, steps), third)] = part
    for copy in loads[4:]:
        copy.wait()
    total = times(group_ref[...], held_ref[...])
    block_out = (state_in[...].astype(F32) + modes_in[2] * total).astype(BF16)
    head_in = scaled_norm(block_out.astype(F32), modes_in[3], modes_in[4])
    velocity = times_turned(head_in_ref[...], head_in.astype(BF16))
    channels = own_buf.shape[0]
    core = lax.axis_index("cfg")
    own_buf[...] = jnp.where(core == 0, velocity[:channels], velocity[channels:])
    sent_buf[...] = jnp.where(core == 0, velocity[channels:], velocity[:channels]).astype(BF16)
    for copy in load_all([(own_buf, own_ref), (sent_buf, sent_ref)], sem):
        copy.wait()


def project(state, modes, w_head, attended, pieces):
    rows, width = state.shape
    third = width // 4
    channels = w_head.shape[0] // 2
    return pl.pallas_call(
        out_kernel,
        out_shape=[shape_of(channels, rows, dtype=F32), shape_of(channels, rows)],
        in_specs=[ANY] * 15,
        out_specs=[ANY, ANY],
        scratch_shapes=[
            pltpu.VMEM((4, rows, third), BF16),
            pltpu.VMEM((rows, width), BF16),
            pltpu.VMEM((width, width), BF16),
            pltpu.VMEM(state.shape, BF16),
            pltpu.VMEM(modes.shape, F32),
            pltpu.VMEM(w_head.shape, BF16),
            pltpu.VMEM((channels, rows), F32),
            pltpu.VMEM((channels, rows), BF16),
            pltpu.SemaphoreType.DMA((15,)),
        ],
        compiler_params=params(50),
        cost_estimate=cost(8e9, 1e6),
    )(state, modes, w_head, *attended, *pieces)


def updated_latent(own, outgoing, latent, guidance, step_size, length, position):
    rows = own.shape[1]
    branch = lax.axis_index("cfg")
    scale = guidance[0]
    other = lax.ppermute(outgoing, "cfg", SWAP).astype(own.dtype)
    cond = jnp.where(branch == 0, own, other)
    uncond = jnp.where(branch == 0, other, own)
    guided = uncond + scale * (cond - uncond)
    valid = position * rows + jnp.arange(rows, dtype=jnp.int32) < length
    current = latent[0].T
    updated = jnp.where(valid[None, :], current - step_size[0] * guided, current)
    return updated.T[None]


def after(value, *others):
    return lax.optimization_barrier((value, *others))[0]


def team_local(
    hidden, latent, modulation, w_qkv, w_out, q_gain, k_gain, w_head, lengths, guidance, step_size
):
    state = hidden[0, 0]
    modes = jnp.transpose(modulation, (1, 0, 2))
    rows, width = state.shape
    third = width // 4
    parts = lax.axis_size("req")
    up = [(2 * fold(i) + side, 2 * fold((i - 1) % 4) + side) for i in range(4) for side in range(2)]
    down = [(target, source) for source, target in up]
    beside = [(i, i ^ 1) for i in range(parts)]

    def along(piece):
        return lax.ppermute(piece, "req", up)

    def back(piece):
        return lax.ppermute(piece, "req", down)

    def across(piece):
        return lax.ppermute(piece, "req", beside)

    gains = jnp.stack([q_gain, k_gain])[:, None]
    columns, normed = entry(w_qkv, w_out, state, modes)
    normed_y = lax.ppermute(normed, "seq", SWAP)
    normed_c = lax.ppermute(normed, "cfg", SWAP)

    def step(mine, theirs, gates):
        now = after(mine[-1], *gates)
        mine.append(along(now))
        theirs.append(across(now))

    mine, theirs = [columns], []
    step(mine, theirs, [])
    cut, split = columns.shape[0] // 2 + 16, 3 * third
    low = theirs[0][cut:, :split]
    out_last = theirs[0][:, split:]
    gates = [mine[1], theirs[0], low, out_last, gains]
    step(mine, theirs, gates)
    gates = [mine[2], theirs[1]]
    step(mine, theirs, gates)
    out_last = back(after(out_last, *gates))
    early = [mine[0], theirs[0], mine[1], theirs[1]]
    packed = [pack([*early, mine[2]], third)]
    normed_yc = lax.ppermute(normed_y, "cfg", SWAP)
    norms = [normed, normed_y, normed_c, normed_yc]
    packed_y = [lax.ppermute(packed[0], "seq", SWAP)]
    acc_qk, acc_v = first_part(norms, early)
    gates = [mine[3], theirs[2], out_last, acc_v]
    upper = across(after(mine[3][:cut, :split], *gates))
    lower = back(after(low, *gates))
    late = [mine[2], theirs[2], mine[3], upper, lower]
    packed.append(pack([after(theirs[2], packed_y[0]), mine[3], out_last], third))
    packed_y.append(lax.ppermute(packed[1], "seq", SWAP))
    packed_c = [lax.ppermute(part, "cfg", SWAP) for part in packed]
    packed_yc = [lax.ppermute(part, "cfg", SWAP) for part in packed_y]

    qk_full, sums = last_scores(norms, acc_qk, gains, late)
    v_full = last_values(norms, acc_v, late)
    diagonal = [(i, 3 - i) for i in range(4)]
    all_sums = [
        sums,
        lax.ppermute(sums, "seq", SWAP),
        lax.ppermute(sums, "cfg", SWAP),
        lax.ppermute(sums, ("cfg", "seq"), diagonal),
    ]
    v_full = after(v_full, packed_c[0], packed_yc[0])
    far = team_attention((1, 3), 6e9, lengths, qk_full, v_full, all_sums)
    far = lax.optimization_barrier((*far, packed_y[1], packed_c[1]))[:2]
    near = team_attention((2, 0), 1e6, lengths, after(qk_full, far[0]), v_full, all_sums)
    attended = [
        near[1],
        lax.ppermute(near[0], "cfg", SWAP),
        lax.ppermute(far[0], "seq", SWAP),
        lax.ppermute(far[1], ("cfg", "seq"), diagonal),
    ]
    quarters = [part[j] for j in range(2) for part in (packed, packed_c, packed_y, packed_yc)]
    own, outgoing = project(state, modes, w_head.T, attended, quarters)
    return updated_latent(own, outgoing, latent, guidance, step_size, lengths[0], lax.axis_index("seq"))


def by_team(mesh, arguments):
    hidden, w_qkv = arguments[0], arguments[3]
    sizes = mesh.shape
    width = hidden.shape[3]
    depth = w_qkv.shape[0] // sizes["req"]
    return (
        sizes["cfg"] == 2
        and sizes["seq"] == 2
        and sizes["req"] == 8
        and width % (4 * DH) == 0
        and 8 * depth == width
        and depth % 32 == 0
        and hidden.shape[2] // sizes["seq"] % 16 == 0
    )


def solution(mesh):
    def whole(*arguments):
        body = team_local if by_team(mesh, arguments) else ring_local
        return jax.shard_map(
            body,
            mesh=mesh,
            in_specs=(
                P("cfg", "req", "seq", None),
                P("req", "seq", "cfg"),
                P("req", None, None),
                P("req", None),
                P("req", None),
                P(),
                P(),
                P(),
                P("req"),
                P("req"),
                P("req"),
            ),
            out_specs=P("req", "seq", "cfg"),
            check_vma=False,
        )(*arguments)

    return whole
```
